512 devices in a mesh: rep: 64 (over z, y), slab: 8 (over x, core).
Axes of the slice: x: 4, y: 8, z: 8, core: 2. Of those that a mesh axis runs over, the one named last changes fastest.
Arguments:
- features: bfloat16 [64, 24, 32, 8, 128], P('rep', None, 'slab'), may hold values from -6 to 6
- cotangent: bfloat16 [64, 16, 32, 8, 128], P('rep', None, 'slab'), may hold values from -6 to 6
- conv_weight: bfloat16 [24, 24, 3, 3, 3], replicated, may hold values from -0.25 to 0.25
- conv_bias: float32 [24], replicated, may hold values from -3 to 3
- head_weight: bfloat16 [24, 16], replicated, may hold values from -1.25 to 1.25
- grad_rest: float32 [64, 8, 246168], P('rep', 'slab'), may hold values from -6400 to 6400
- master: float32 [262144], P('rep'), may hold values from -1.2 to 1.2
- moment: float32 [262144], P('rep'), may hold values from -6 to 6
- second: float32 [262144], P('rep'), may hold values from 0.5 to 4
Outputs:
- input_grad: bfloat16 [64, 24, 32, 8, 128], P('rep', None, 'slab')
- new_moment: float32 [262144], P('rep')
- new_second: float32 [262144], P('rep')
- new_master: float32 [262144], P('rep')
- weights: bfloat16 [262144], replicated
The draws below stay inside these ranges and needn't reach their ends.
All inputs are finite; a program needn't handle non-finite values.
Results may differ from the reference program's by a relative error of at most 0.0049.
Values may be sent and summed in bfloat16 or wider, within the bound.
A program may use at most 64 MiB of HBM per device.

```python
import math
import jax
import jax.numpy as jnp
from jax import lax

CH = 24
EMB = 16
YD = 8
XD = 128
P_REST = 246168
LOSS_SCALE = 2048
ZN = 32
PARAMS = 262144
N_REP = 64
N_SLAB = 8


def strengthened(drawn, rng, source, target, blocks, factor):
    def block_of(position):
        return (jnp.arange(drawn.shape[position]) // (drawn.shape[position] // blocks)).reshape((-1,) + (1,) * (drawn.ndim - 1 - position))

    first = jax.random.permutation(rng, blocks)[block_of(target)]
    far = (block_of(target) + blocks // 2) % blocks
    return jnp.where((block_of(source) == first) | (block_of(source) == far), factor * drawn, drawn)


def levels(stream_key, extent, cuts, smallest, top_value):
    loudness, own = 1.0, jax.random.fold_in(stream_key, 6)
    for axis_at, parts in cuts:
        heights = jnp.exp(jax.random.uniform(jax.random.fold_in(own, axis_at), (parts,), jnp.float32, smallest / len(cuts), top_value / len(cuts)))
        loudness = loudness * jnp.repeat(heights, extent[axis_at] // parts).reshape([-1 if axis == axis_at else 1 for axis in range(len(extent))])
    return loudness


def gaussian(key, extent, width, most, pieces=(), kind=jnp.bfloat16):
    gain = levels(key, extent, pieces, -0.22, 0.18) if pieces else 1.0
    values = jax.random.normal(key, extent, jnp.float32) * width * gain
    return jnp.minimum(jnp.maximum(values, -most), most).astype(kind)


def noise_with(rng, dims, scale, bound, shards, heavy, kind=jnp.bfloat16):
    drawn = scale * jax.random.normal(rng, dims, jnp.float32)
    if shards:
        drawn = drawn * levels(rng, dims, shards, -0.22, 0.18)
    return jnp.clip(strengthened(drawn, jax.random.fold_in(rng, 3), *heavy), -bound, bound).astype(kind)


def setup_inputs(seed: int = 0) -> dict:
    seeds = jax.random.split(jax.random.key(seed), 10)
    features = gaussian(seeds[0], (N_REP, CH, ZN, YD, XD), 1.0, 6.0, ((0, 64), (2, 8)))
    cotangent = gaussian(seeds[1], (N_REP, EMB, ZN, YD, XD), 1.0, 6.0, ((0, 64), (2, 8)))
    conv_weight = gaussian(seeds[2], (CH, CH, 3, 3, 3), (27 * CH) ** -0.5, 0.25)
    conv_bias = gaussian(seeds[3], (CH,), 0.5, 3.0, (), jnp.float32)
    head_weight = gaussian(seeds[4], (CH, EMB), CH ** -0.5, 1.25)
    grad_rest = noise_with(seeds[5], (N_REP, N_SLAB, P_REST), 1024.0, 6400.0, ((0, 64), (1, 8)), (0, 2, 8, 2.0), jnp.float32)
    master = gaussian(seeds[6], (PARAMS,), 0.2, 1.2, ((0, 64),), jnp.float32)
    moment = gaussian(seeds[7], (PARAMS,), 1.0, 6.0, ((0, 64),), jnp.float32)
    second = jnp.clip(jnp.exp(math.log(4.0) - 2.0794415 * jax.random.uniform(seeds[8], (PARAMS,), jnp.float32) ** levels(seeds[8], (PARAMS,), ((0, 64),), -0.2, 0.2)), 0.5, 4.0)
    return dict(features=features, cotangent=cotangent, conv_weight=conv_weight, conv_bias=conv_bias, head_weight=head_weight, grad_rest=grad_rest, master=master, moment=moment, second=second)


beta_one = 0.9
beta_two = 0.99
learn_rate = 0.01
adam_eps = 1e-08
step_count = 10.0

def correlate(lhs, rhs, numbers):
    return lax.conv_general_dilated(lhs, rhs, (1, 1, 1), [(1, 1), (1, 1), (1, 1)], dimension_numbers=numbers, precision=lax.Precision.HIGHEST)

def crop_grads_with(pair, weight_in, bias_in, head_in):
    feats, cotan = pair
    feats_f = feats.astype(jnp.float32)[None]
    weight_f = weight_in.astype(jnp.float32)
    pre = correlate(feats_f, weight_f, ('NCDHW', 'OIDHW', 'NCDHW'))[0] + bias_in[:, None, None, None]
    sigma = jax.nn.sigmoid(pre)
    act = (pre * sigma).astype(jnp.bfloat16)
    cot_f = cotan.astype(jnp.float32)
    dact = jnp.einsum('ie,ezyx->izyx', head_in.astype(jnp.float32), cot_f, precision=lax.Precision.HIGHEST)
    dpre = (dact * sigma * (1.0 + pre * (1.0 - sigma))).astype(jnp.bfloat16)
    dpre_f = dpre.astype(jnp.float32)[None]
    wgrad = correlate(feats_f, dpre_f, ('CNDHW', 'IODHW', 'NCDHW')).transpose(1, 0, 2, 3, 4)
    flipped = weight_f[:, :, ::-1, ::-1, ::-1]
    dinput = correlate(dpre_f, flipped, ('NCDHW', 'IODHW', 'NCDHW'))[0].astype(jnp.bfloat16)
    bgrad = lax.optimization_barrier(jnp.sum(dpre_f, axis=(0, 2, 3, 4)))
    hgrad = jnp.dot(act.astype(jnp.float32).reshape(CH, -1), cot_f.reshape(EMB, -1).T, precision=lax.Precision.HIGHEST)
    hbias = lax.optimization_barrier(jnp.sum(cot_f, axis=(1, 2, 3)))
    flat = jnp.concatenate([wgrad.reshape(-1), bgrad, hgrad.reshape(-1), hbias])
    return (flat, dinput)

def reference(features, cotangent, conv_weight, conv_bias, head_weight, grad_rest, master, moment, second):

    def one_crop(pair):
        return crop_grads_with(pair, conv_weight, conv_bias, head_weight)
    flats, input_grad = lax.map(one_crop, (features, cotangent))
    window = lax.optimization_barrier(jnp.sum(flats, axis=0))
    rest = lax.optimization_barrier(jnp.sum(grad_rest, axis=(0, 1)))
    grad = jnp.concatenate([window, rest]) / LOSS_SCALE
    new_moment = beta_one * moment + (1.0 - beta_one) * grad
    new_second = beta_two * second + (1.0 - beta_two) * grad * grad
    update = new_moment / (1.0 - beta_one ** step_count) / (jnp.sqrt(new_second / (1.0 - beta_two ** step_count)) + adam_eps)
    new_master = master - learn_rate * update
    return (input_grad, new_moment, new_second, new_master, new_master.astype(jnp.bfloat16))
```

```python
import functools

import jax
import jax.numpy as jnp
import numpy as np
from jax import lax
from jax.experimental import pallas as pl
from jax.experimental.pallas import tpu as pltpu
from jax.sharding import PartitionSpec as P

LOSS_SCALE = 2048

beta_one = 0.9
beta_two = 0.99
learn_rate = 0.01
adam_eps = 1e-08
step_count = 10.0

f32 = jnp.float32
bf16 = jnp.bfloat16
MESH = pl.DeviceIdType.MESH
LANES = 128
CONV_ROWS = 124
CONV_LANES = 104
WIN = 128


def adam_update(grad, moment, second, master):
    new_moment = beta_one * moment + (1.0 - beta_one) * grad
    new_second = beta_two * second + (1.0 - beta_two) * grad * grad
    update = (
        new_moment
        / (1.0 - beta_one**step_count)
        / (jnp.sqrt(new_second / (1.0 - beta_two**step_count)) + adam_eps)
    )
    return (new_moment, new_second, master - learn_rate * update)


def selection_tables(ch, emb):
    rows = 8 * ch
    repeat_rows = np.zeros((rows, ch), np.float32)
    repeat_rows[np.arange(rows), np.arange(rows) // 8] = 1
    repeat_lanes = np.zeros((ch, 256), np.float32)
    repeat_lanes[np.arange(rows) // 8, np.arange(rows)] = 1
    repeat_emb = np.zeros((emb, 128), np.float32)
    repeat_emb[np.arange(128) // 8, np.arange(128)] = 1
    add_rows = np.zeros((32, rows + 16), np.float32)
    for i in range(ch + 1):
        add_rows[i, 8 * i : 8 * i + 8] = 1
    order = np.zeros((5 * 256, 768), np.float32)
    for a in range(3):
        for c in range(3):
            pair, slot = divmod(a * 3 + c, 2)
            for i in range(ch):
                tile, local = divmod(i, 16)
                for b in range(3):
                    lane = (8 * local + 6 + b + 3 * slot) % 128
                    order[pair * 256 + tile * 128 + lane, i * 27 + a * 9 + b * 3 + c] = 1
    order[2 * 256 + 128 + 8 * 8 + 7, ch * 27] = 1
    emb_order = np.zeros((128, 128), np.float32)
    for e in range(emb):
        emb_order[8 * e + 7, 88 + e] = 1
    place = np.zeros((WIN, 256), np.float32)
    for o in range(ch):
        for k in range(7):
            place[5 * o + k, k * ch + o] = 1
        place[121, 7 * ch + o] = 1
    for i in range(ch + 1):
        place[121 + i // 8, 192 + i] = 1
        place[122 + i // 8, 224 + i] = 1
    tables = (repeat_rows, repeat_lanes, repeat_emb, add_rows, order, emb_order, place)
    return tuple(jnp.asarray(t, bf16) for t in tables)


def dot(lhs, rhs):
    return jnp.dot(lhs, rhs, preferred_element_type=f32)


def dot_nt(lhs, rhs):
    return lax.dot_general(lhs, rhs, (((1,), (1,)), ((), ())), preferred_element_type=f32)


def dot_tn(lhs, rhs):
    return lax.dot_general(lhs, rhs, (((0,), (0,)), ((), ())), preferred_element_type=f32)


def iota(shape, dim):
    return lax.broadcasted_iota(jnp.int32, shape, dim)


def kernel(
    sizes,
    feat_ref, cot_ref, w_ref, bias_ref, headt_ref, rest_ref, master_ref, moment_ref, second_ref,
    rep_rows_ref, rep_lanes_ref, rep_emb_ref, add_ref, order_hbm, emb_order_ref, place_ref,
    igrad_ref, nmom_ref, nsec_ref, nmas_ref, weights_ref,
    rest_v, flat_b, feat_v, cot_v, wband, hband, conv_v, act_v, dpre_v, grad_v, packed_v, stack_v, order_v,
    fh_send, fh_recv, dh_send, dh_recv,
    p1_recv, p1w_send, p1w_recv, sum_v, p2_send, p2_recv, shard_v, p3_send, p3_recv, grad_shard,
    local_sem, fh_ssem, fh_rsem, dh_ssem, dh_rsem,
    p1_ssem, p1_rsem, p1w_ssem, p1w_rsem, p2_ssem, p2_rsem, p3_ssem, p3_rsem,
    b1_ssem, b1_rsem, g_ssem, g_rsem, b2_ssem, b2_rsem, b3_ssem, b3_rsem,
):
    zs, ys, ss, shard_rows, planes, ch, emb = sizes
    rows = 8 * ch
    cells = planes * LANES
    block_rows = ys * shard_rows
    rep = lax.axis_index("rep")
    s = lax.axis_index("slab")
    z = rep // ys
    y = rep % ys

    def at(zz, yy, sl):
        return (zz * ys + yy, sl)

    def remote(src, dst, ssem, rsem, device):
        return pltpu.make_async_remote_copy(
            src_ref=src, dst_ref=dst, send_sem=ssem, recv_sem=rsem, device_id=device, device_id_type=MESH
        )

    rest_copy = pltpu.make_async_copy(rest_ref.at[0], rest_v, local_sem.at[0])
    rest_copy.start()
    order_copy = pltpu.make_async_copy(order_hbm, order_v, local_sem.at[1])
    order_copy.start()

    barrier = pltpu.get_barrier_semaphore()
    for d in range(1, ss):
        pl.semaphore_signal(barrier, inc=1, device_id=at(z, y, (s + d) % ss), device_id_type=MESH)
    for d in range(1, ys):
        pl.semaphore_signal(barrier, inc=1, device_id=at(z, (y + d) % ys, s), device_id_type=MESH)
    for d in range(1, zs):
        pl.semaphore_signal(barrier, inc=1, device_id=at((z + d) % zs, y, s), device_id_type=MESH)

    for p in range(planes):
        plane = feat_ref[:, p].astype(f32).reshape(rows, LANES).astype(bf16)
        feat_v[0:rows, LANES * (p + 1) : LANES * (p + 2)] = plane
        if p == 0:
            fh_send[0] = plane
        if p == planes - 1:
            fh_send[1] = plane
        cot_v[:, LANES * p : LANES * (p + 1)] = cot_ref[:, p].astype(f32).reshape(8 * emb, LANES).astype(bf16)
    feat_v[rows : rows + 16, :] = jnp.ones((16, cells + 2 * LANES), bf16)
    feat_v[rows + 16 : 256, :] = jnp.zeros((256 - rows - 16, cells + 2 * LANES), bf16)

    pl.semaphore_wait(barrier, (ss - 1) + (ys - 1) + (zs - 1))

    def halo(send, recv, ssem, rsem, up):
        source, slot = (1, 0) if up else (0, 1)
        other = (s + 1) % ss if up else (s + ss - 1) % ss
        return remote(send.at[source], recv.at[slot], ssem.at[source], rsem.at[slot], at(z, y, other))

    def start_halo(send, recv, ssem, rsem):
        @pl.when(s < ss - 1)
        def _():
            halo(send, recv, ssem, rsem, True).start()

        @pl.when(s > 0)
        def _():
            halo(send, recv, ssem, rsem, False).start()

        @pl.when(s == 0)
        def _():
            recv[0] = jnp.zeros((rows, LANES), bf16)

        @pl.when(s == ss - 1)
        def _():
            recv[1] = jnp.zeros((rows, LANES), bf16)

    def wait_halo(send, recv, ssem, rsem):
        @pl.when(s < ss - 1)
        def _():
            halo(send, recv, ssem, rsem, True).wait_send()
            halo(send, recv, ssem, rsem, False).wait_recv()

        @pl.when(s > 0)
        def _():
            halo(send, recv, ssem, rsem, False).wait_send()
            halo(send, recv, ssem, rsem, True).wait_recv()

    start_halo(fh_send, fh_recv, fh_ssem, fh_rsem)

    rest_copy.wait()
    first, last = CONV_ROWS // 16, flat_b.shape[0] // 16 - 1
    flat_b[0 : 16 * first, :] = jnp.zeros((16 * first, LANES), bf16)
    lane16 = iota((16, LANES), 1)

    def moved(here, later):
        return pltpu.roll(jnp.where(lane16 >= LANES - CONV_LANES, here, later), CONV_LANES, 1).astype(bf16)

    def rest_rows(at_row, count):
        start = at_row * LANES
        if not isinstance(start, int):
            start = pl.multiple_of(start, LANES)
        return rest_v[0:1, pl.ds(start, count * LANES)].reshape(count, LANES)

    def align(j, carry):
        at_row = j * 16 - CONV_ROWS - 1
        flat_b[pl.ds(pl.multiple_of(j * 16, 16), 16), :] = moved(rest_rows(at_row, 16), rest_rows(at_row + 1, 16))
        return carry

    lead = CONV_ROWS - 16 * first
    start_rows = rest_rows(0, 8)
    flat_b[16 * first : 16 * first + 16, :] = moved(
        jnp.concatenate([jnp.zeros((lead + 1, LANES), f32), start_rows[0 : 15 - lead]], axis=0),
        jnp.concatenate([jnp.zeros((lead, LANES), f32), start_rows[0 : 16 - lead]], axis=0),
    )
    lax.fori_loop(first + 1, last, align, 0)
    end_row = 16 * last - CONV_ROWS - 1
    end = rest_v[0:1, (end_row + 16) * LANES :]
    end = jnp.concatenate([end, jnp.zeros((1, LANES - end.shape[1]), f32)], axis=1)
    end_rows = rest_rows(end_row, 16)
    flat_b[16 * last : 16 * last + 16, :] = moved(end_rows, jnp.concatenate([end_rows[1:16], end], axis=0))

    def p1(d):
        other = (s + d) % ss
        return remote(
            flat_b.at[pl.ds(pl.multiple_of(other * block_rows, 16), block_rows)],
            p1_recv.at[d - 1], p1_ssem.at[d - 1], p1_rsem.at[d - 1], at(z, y, other),
        )

    for d in range(1, ss):
        p1(d).start()

    row = iota((rows, 256), 0)
    lane = iota((rows, 256), 1)
    shift = (lane % 8) - (7 - row % 8)
    spread = dot(w_ref[...].astype(f32).reshape(27 * ch, ch).astype(bf16), rep_lanes_ref[...])
    for a in range(3):
        for c in range(3):
            band = jnp.zeros((rows, 256), f32)
            for b in range(3):
                at_row = (a * 9 + b * 3 + c) * ch
                full = dot(rep_rows_ref[...], spread[at_row : at_row + ch].astype(bf16))
                band = jnp.where(shift == b - 1, full, band)
            wband[a, rows * c : rows * (c + 1), :] = band.astype(bf16)
    head = dot(dot_nt(rep_rows_ref[...], headt_ref[...]).astype(bf16), rep_emb_ref[...])
    hband[...] = jnp.where(shift[:, :LANES] == 0, head, 0.0).astype(bf16)
    bias_row = jnp.concatenate([bias_ref[...], jnp.zeros((1, LANES - ch), f32)], axis=1)
    row_l = iota((rows, LANES), 0)
    lane_l = iota((rows, LANES), 1)
    bias = jnp.sum(jnp.where(lane_l == row_l // 8, jnp.broadcast_to(bias_row, (rows, LANES)), 0.0), axis=1, keepdims=True)

    conv_v[...] = dot(wband[1], feat_v[:, LANES : LANES + cells])
    wait_halo(fh_send, fh_recv, fh_ssem, fh_rsem)
    feat_v[0:rows, 0:LANES] = fh_recv[0]
    feat_v[0:rows, LANES + cells : 2 * LANES + cells] = fh_recv[1]
    conv_v[...] += dot(wband[0], feat_v[:, 0:cells]) + dot(wband[2], feat_v[:, 2 * LANES : 2 * LANES + cells])

    def right(v):
        return jnp.where(lane_l == 0, 0.0, pltpu.roll(v, 1, 1))

    def left(v):
        return jnp.where(lane_l == LANES - 1, 0.0, pltpu.roll(v, LANES - 1, 1))

    def spread_dpre(dpre, p):
        at_lane = slice(LANES * p, LANES * (p + 1))
        dpre_v[0:rows, at_lane] = left(dpre).astype(bf16)
        dpre_v[rows : 2 * rows, at_lane] = dpre.astype(bf16)
        dpre_v[2 * rows : 3 * rows, at_lane] = right(dpre).astype(bf16)

    for p in (0, planes - 1) + tuple(range(1, planes - 1)):
        at_lane = slice(LANES * p, LANES * (p + 1))
        pre = (
            conv_v[rows : 2 * rows, at_lane]
            + right(conv_v[0:rows, at_lane])
            + left(conv_v[2 * rows : 3 * rows, at_lane])
            + bias
        )
        sigma = jax.nn.sigmoid(pre)
        act_v[0:rows, at_lane] = (pre * sigma).astype(bf16)
        dact = dot(hband[...], cot_v[:, at_lane])
        dpre = (dact * sigma * (1.0 + pre * (1.0 - sigma))).astype(bf16)
        if p == 0:
            dh_send[0] = dpre
        if p == planes - 1:
            dh_send[1] = dpre
        spread_dpre(dpre.astype(f32), p + 1)
        if p == planes - 1:
            start_halo(dh_send, dh_recv, dh_ssem, dh_rsem)
    act_v[rows : rows + 16, :] = jnp.ones((16, cells), bf16)

    def p1w(slot):
        return remote(p1w_send, p1w_recv.at[slot], p1w_ssem, p1w_rsem.at[slot], at(z, y, 0))

    def p2(d):
        other = (y + d) % ys
        return remote(
            p2_send.at[pl.ds(pl.multiple_of(other * shard_rows, 16), shard_rows)],
            p2_recv.at[d - 1], p2_ssem.at[d - 1], p2_rsem.at[d - 1], at(z, other, s),
        )

    def p3(slot):
        return remote(p3_send, p3_recv.at[slot], p3_ssem, p3_rsem.at[slot], at(s, y, s))

    def b1(d):
        mine = weights_ref.at[pl.ds(pl.multiple_of(s * block_rows + y * shard_rows, 16), shard_rows)]
        return remote(mine, mine, b1_ssem.at[d - 1], b1_rsem, at((z + d) % zs, y, s))

    def share(d):
        return remote(grad_shard, grad_shard, g_ssem.at[d - 1], g_rsem, at(z, y, (s + d) % ss))

    def b2(d, back):
        owner = (y + ys - d) % ys if back else y
        part = weights_ref.at[pl.ds(pl.multiple_of(s * block_rows + owner * shard_rows, 16), shard_rows)]
        return remote(part, part, b2_ssem.at[d - 1], b2_rsem.at[d - 1], at(z, (y + d) % ys, s))

    def b3(d, back):
        owner = (s + ss - d) % ss if back else s
        part = weights_ref.at[pl.ds(pl.multiple_of(owner * block_rows, 16), block_rows)]
        return remote(part, part, b3_ssem.at[d - 1], b3_rsem.at[d - 1], at(z, y, (s + d) % ss))

    def sum_slabs(with_window):
        for d in range(1, ss):
            p1(d).wait_recv()
        total = flat_b[pl.ds(pl.multiple_of(s * block_rows, 16), block_rows), :].astype(f32)
        for d in range(1, ss):
            total = total + p1_recv[d - 1].astype(f32)
        sum_v[...] = total
        if with_window:
            for d in range(1, ss):
                p1w(d - 1).wait_recv()
            window = p1w_send[...].astype(f32)
            for d in range(1, ss):
                window = window + p1w_recv[d - 1].astype(f32)
            sum_v[0:WIN, :] += window
        p2_send[...] = sum_v[...].astype(bf16)
        for d in range(1, ys):
            p2(d).start()

    def sum_ys():
        for d in range(1, ys):
            p2(d).wait_recv()
        total = sum_v[pl.ds(pl.multiple_of(y * shard_rows, 16), shard_rows), :]
        for d in range(1, ys):
            total = total + p2_recv[d - 1].astype(f32)
        shard_v[...] = total

        @pl.when(z != s)
        def _():
            p3_send[...] = total.astype(bf16)
            p3((s + zs - z - 1) % zs).start()

    def update():
        new_moment, new_second, new_master = adam_update(
            grad_shard[...], moment_ref[...], second_ref[...], master_ref[...]
        )
        nmom_ref[...] = new_moment
        nsec_ref[...] = new_second
        nmas_ref[...] = new_master
        return new_master

    def reduce_shard():
        for d in range(1, zs):
            p3(d - 1).wait_recv()
        total = shard_v[...]
        for d in range(1, zs):
            total = total + p3_recv[d - 1].astype(f32)
        grad_shard[...] = total / LOSS_SCALE
        new_master = update()
        weights_ref[pl.ds(pl.multiple_of(s * block_rows + y * shard_rows, 16), shard_rows), :] = new_master.astype(bf16)
        for d in range(1, zs):
            b1(d).start()
        for d in range(1, ss):
            share(d).start()

    def gather_ys():
        @pl.when(z != s)
        def _():
            b1(1).wait_recv()

        for d in range(1, ys):
            b2(d, False).start()

    def gather_slabs():
        for d in range(1, ys):
            b2(d, True).wait_recv()
        for d in range(1, ss):
            b3(d, False).start()

    early = s != 0
    late = s == 0

    pl.when(early)(lambda: sum_slabs(False))

    mask = ((lane < rows) & (shift >= -1) & (shift <= 1)) | ((lane >= rows) & (lane < rows + 8) & (shift == 0))
    mask = [mask[:, :LANES], mask[:, LANES:]]
    for a in range(3):
        grad_v[a] = dot_nt(dpre_v[:, LANES : LANES + cells], feat_v[:, LANES * a : LANES * a + cells])
    pl.when(early)(sum_ys)
    order_copy.wait()

    def rolled(v, by):
        return jnp.concatenate(
            [pltpu.roll(v[8 * o : 8 * o + 8], by, 1, stride=1, stride_axis=0) for o in range(v.shape[0] // 8)], axis=0
        )

    for pair in range(5):
        for t in range(2):
            total = None
            for slot in range(2):
                if pair * 2 + slot < 9:
                    a, c = divmod(pair * 2 + slot, 3)
                    part = grad_v[a, rows * c : rows * (c + 1), LANES * t : LANES * (t + 1)]
                    part = rolled(jnp.where(mask[t], part, 0.0), 3 * slot)
                    total = part if total is None else total + part
            at_lane = pair * 256 + t * LANES
            packed_v[:, at_lane : at_lane + LANES] = total.astype(bf16)
    sums = dot(add_ref[0:ch, 0:rows], packed_v[...])
    ordered = dot(sums.astype(bf16), order_v[...])
    lane8 = iota((8, LANES), 1)
    row8 = iota((8, LANES), 0)
    zero8 = jnp.zeros((8, LANES), f32)
    for t in range(ch // 8):
        whole, base = divmod(64 * t, LANES)
        by = base + 8 * row8
        tiles = []
        for k in range(6):
            piece = ordered[8 * t : 8 * t + 8, LANES * k : LANES * (k + 1)]
            if k == 5:
                piece = jnp.where(lane8 < 8, piece, 0.0)
            tiles.append(pltpu.roll(piece, base, 1, stride=8, stride_axis=0))
        for m in range(7):
            k = m - whole
            high = tiles[k] if 0 <= k < 6 else zero8
            low = tiles[k - 1] if 0 <= k - 1 < 6 else zero8
            stack_v[m * ch + 8 * t : m * ch + 8 * t + 8, :] = jnp.where(lane8 >= by, high, low)
        bgrad = jnp.broadcast_to(ordered[8 * t : 8 * t + 8, 27 * ch : 27 * ch + 1], (8, LANES))
        stack_v[7 * ch + 8 * t : 7 * ch + 8 * t + 8, :] = jnp.where(lane8 == 64 + 8 * t + row8, bgrad, 0.0)

    hgrad = dot_nt(act_v[...], cot_v[...])
    row_h = iota((rows + 16, LANES), 0)
    lane_h = iota((rows + 16, LANES), 1)
    hgrad = rolled(jnp.where(lane_h % 8 == 7 - row_h % 8, hgrad, 0.0), 0).astype(bf16)
    hgrad = dot(dot(add_ref[...], hgrad).astype(bf16), emb_order_ref[...])
    for t in range(4):
        piece = pltpu.roll(hgrad[8 * t : 8 * t + 8], 0, 1, stride=16, stride_axis=0)
        stack_v[192 + 8 * t : 200 + 8 * t, :] = jnp.where(lane8 >= 88, piece, 0.0)
        stack_v[224 + 8 * t : 232 + 8 * t, :] = jnp.where(lane8 < 88, piece, 0.0)
    p1w_send[...] = dot(place_ref[...], stack_v[...].astype(bf16)).astype(bf16)

    @pl.when(early)
    def _():
        p1w(ss - 1 - s).start()

    reducer = z == s
    pl.when(early & reducer)(reduce_shard)

    wait_halo(dh_send, dh_recv, dh_ssem, dh_rsem)
    spread_dpre(dh_recv[0].astype(f32), 0)
    spread_dpre(dh_recv[1].astype(f32), planes + 1)

    pl.when(late)(lambda: sum_slabs(True))
    pl.when(early)(gather_ys)

    total = None
    for a in range(3):
        part = dot_tn(wband[a, :, 0:rows], dpre_v[:, LANES * (2 - a) : LANES * (2 - a) + cells])
        total = part if total is None else total + part
    for p in range(planes):
        igrad_ref[:, p] = total[:, LANES * p : LANES * (p + 1)].reshape(ch, 8, LANES).astype(bf16)

    pl.when(late)(sum_ys)
    pl.when(early)(gather_slabs)
    pl.when(late & reducer)(reduce_shard)
    pl.when(late)(gather_ys)
    pl.when(late)(gather_slabs)

    @pl.when(jnp.logical_not(reducer))
    def _():
        share(1).wait_recv()
        update()

    for d in range(1, ss):
        b3(d, True).wait_recv()

    for d in range(1, ss):
        p1(d).wait_send()
        b3(d, False).wait_send()
    for d in range(1, ys):
        p2(d).wait_send()
        b2(d, False).wait_send()

    @pl.when(early)
    def _():
        p1w(0).wait_send()

    @pl.when(jnp.logical_not(reducer))
    def _():
        p3(0).wait_send()

    @pl.when(reducer)
    def _():
        for d in range(1, zs):
            b1(d).wait_send()
        for d in range(1, ss):
            share(d).wait_send()


def on_device(
    features, cotangent, conv_weight, conv_bias, head_weight, grad_rest, master, moment, second
):
    ss = lax.axis_size("slab")
    zs = ss
    ys = lax.axis_size("rep") // zs
    ch, planes = features.shape[1], features.shape[2]
    emb = cotangent.shape[1]
    rows = 8 * ch
    cells = planes * LANES
    shard_rows = master.shape[0] // LANES
    block_rows = ys * shard_rows
    all_rows = ss * block_rows
    rest = grad_rest.shape[2]
    sizes = (zs, ys, ss, shard_rows, planes, ch, emb)
    tables = selection_tables(ch, emb)
    vmem = pl.BlockSpec(memory_space=pltpu.VMEM)
    anywhere = pl.BlockSpec(memory_space=pl.ANY)
    dma = pltpu.SemaphoreType.DMA
    shard = jax.ShapeDtypeStruct((shard_rows, LANES), f32)
    outs = pl.pallas_call(
        functools.partial(kernel, sizes),
        out_shape=(
            jax.ShapeDtypeStruct(features.shape[1:], bf16),
            shard,
            shard,
            shard,
            jax.ShapeDtypeStruct((all_rows, LANES), bf16),
        ),
        in_specs=[vmem] * 5 + [anywhere] + [vmem] * 3 + [vmem] * 4 + [anywhere] + [vmem] * 2,
        out_specs=(vmem,) * 5,
        scratch_shapes=[
            pltpu.VMEM((1, rest), f32),
            pltpu.VMEM((all_rows, LANES), bf16),
            pltpu.VMEM((256, cells + 2 * LANES), bf16),
            pltpu.VMEM((8 * emb, cells), bf16),
            pltpu.VMEM((3, 3 * rows, 256), bf16),
            pltpu.VMEM((rows, LANES), bf16),
            pltpu.VMEM((3 * rows, cells), f32),
            pltpu.VMEM((rows + 16, cells), bf16),
            pltpu.VMEM((3 * rows, cells + 2 * LANES), bf16),
            pltpu.VMEM((3, 3 * rows, 256), f32),
            pltpu.VMEM((rows, 5 * 256), bf16),
            pltpu.VMEM((256, LANES), f32),
            pltpu.VMEM((5 * 256, 768), bf16),
            pltpu.VMEM((2, rows, LANES), bf16),
            pltpu.VMEM((2, rows, LANES), bf16),
            pltpu.VMEM((2, rows, LANES), bf16),
            pltpu.VMEM((2, rows, LANES), bf16),
            pltpu.VMEM((ss - 1, block_rows, LANES), bf16),
            pltpu.VMEM((WIN, LANES), bf16),
            pltpu.VMEM((ss - 1, WIN, LANES), bf16),
            pltpu.VMEM((block_rows, LANES), f32),
            pltpu.VMEM((block_rows, LANES), bf16),
            pltpu.VMEM((ys - 1, shard_rows, LANES), bf16),
            pltpu.VMEM((shard_rows, LANES), f32),
            pltpu.VMEM((shard_rows, LANES), bf16),
            pltpu.VMEM((zs - 1, shard_rows, LANES), bf16),
            pltpu.VMEM((shard_rows, LANES), f32),
            dma((2,)),
            dma((2,)), dma((2,)), dma((2,)), dma((2,)),
            dma((ss - 1,)), dma((ss - 1,)),
            dma, dma((ss - 1,)),
            dma((ys - 1,)), dma((ys - 1,)),
            dma, dma((zs - 1,)),
            dma((zs - 1,)), dma,
            dma((ss - 1,)), dma,
            dma((ys - 1,)), dma((ys - 1,)),
            dma((ss - 1,)), dma((ss - 1,)),
        ],
        compiler_params=pltpu.CompilerParams(
            collective_id=0, has_side_effects=True, vmem_limit_bytes=48 << 20
        ),
    )(
        features[0],
        cotangent[0],
        conv_weight.transpose(2, 3, 4, 0, 1).reshape(27, ch, ch),
        conv_bias.reshape(1, ch),
        head_weight.T,
        grad_rest,
        master.reshape(shard_rows, LANES),
        moment.reshape(shard_rows, LANES),
        second.reshape(shard_rows, LANES),
        *tables,
    )
    igrad, new_moment, new_second, new_master, weights = outs
    return (
        igrad[None],
        new_moment.reshape(-1),
        new_second.reshape(-1),
        new_master.reshape(-1),
        weights.reshape(-1),
    )


def solution(mesh):
    return jax.shard_map(
        on_device,
        mesh=mesh,
        in_specs=(
            P("rep", None, "slab", None, None),
            P("rep", None, "slab", None, None),
            P(),
            P(),
            P(),
            P("rep", "slab", None),
            P("rep"),
            P("rep"),
            P("rep"),
        ),
        out_specs=(P("rep", None, "slab", None, None), P("rep"), P("rep"), P("rep"), P()),
        check_vma=False,
    )
```

```python
import functools

import jax
import jax.numpy as jnp
import numpy as np
from jax import lax
from jax.experimental import pallas as pl
from jax.experimental.pallas import tpu as pltpu
from jax.sharding import PartitionSpec as P

LOSS_SCALE = 2048

beta_one = 0.9
beta_two = 0.99
learn_rate = 0.01
adam_eps = 1e-08
step_count = 10.0

f32 = jnp.float32
bf16 = jnp.bfloat16
MESH = pl.DeviceIdType.MESH
LANES = 128
CONV_ROWS = 124
CONV_LANES = 104
WIN = 128


def adam_update(grad, moment, second, master):
    new_moment = beta_one * moment + (1.0 - beta_one) * grad
    new_second = beta_two * second + (1.0 - beta_two) * grad * grad
    update = (
        new_moment
        / (1.0 - beta_one**step_count)
        / (jnp.sqrt(new_second / (1.0 - beta_two**step_count)) + adam_eps)
    )
    return (new_moment, new_second, master - learn_rate * update)


def selection_tables(ch, emb):
    rows = 8 * ch
    repeat_rows = np.zeros((rows, ch), np.float32)
    repeat_rows[np.arange(rows), np.arange(rows) // 8] = 1
    repeat_lanes = np.zeros((ch, 256), np.float32)
    repeat_lanes[np.arange(rows) // 8, np.arange(rows)] = 1
    repeat_emb = np.zeros((emb, 128), np.float32)
    repeat_emb[np.arange(128) // 8, np.arange(128)] = 1
    add_rows = np.zeros((32, rows + 16), np.float32)
    for i in range(ch + 1):
        add_rows[i, 8 * i : 8 * i + 8] = 1
    order = np.zeros((5 * 256, 768), np.float32)
    for a in range(3):
        for c in range(3):
            pair, slot = divmod(a * 3 + c, 2)
            for i in range(ch):
                tile, local = divmod(i, 16)
                for b in range(3):
                    lane = (8 * local + 6 + b + 3 * slot) % 128
                    order[pair * 256 + tile * 128 + lane, i * 27 + a * 9 + b * 3 + c] = 1
    order[2 * 256 + 128 + 8 * 8 + 7, ch * 27] = 1
    emb_order = np.zeros((128, 128), np.float32)
    for e in range(emb):
        emb_order[8 * e + 7, 88 + e] = 1
    place = np.zeros((WIN, 256), np.float32)
    for o in range(ch):
        for k in range(7):
            place[5 * o + k, k * ch + o] = 1
        place[121, 7 * ch + o] = 1
    for i in range(ch + 1):
        place[121 + i // 8, 192 + i] = 1
        place[122 + i // 8, 224 + i] = 1
    tables = (repeat_rows, repeat_lanes, repeat_emb, add_rows, order, emb_order, place)
    return tuple(jnp.asarray(t, bf16) for t in tables)


def dot(lhs, rhs):
    return jnp.dot(lhs, rhs, preferred_element_type=f32)


def dot_nt(lhs, rhs):
    return lax.dot_general(lhs, rhs, (((1,), (1,)), ((), ())), preferred_element_type=f32)


def dot_tn(lhs, rhs):
    return lax.dot_general(lhs, rhs, (((0,), (0,)), ((), ())), preferred_element_type=f32)


def iota(shape, dim):
    return lax.broadcasted_iota(jnp.int32, shape, dim)


def kernel(
    sizes,
    feat_in, cot_in, w_in, bias_in, headt_in, rest_in, master_in, moment_in, second_in,
    rep_rows_in, rep_lanes_in, rep_emb_in, add_in, order_in, emb_order_in, place_in,
    igrad_out, nmom_out, nsec_out, nmas_out, weights_out,
    feat_ref, cot_ref, w_ref, bias_ref, headt_ref, rest_v, own_state,
    rep_rows_ref, rep_lanes_ref, rep_emb_ref, add_ref, order_ref, emb_order_ref, place_ref,
    igrad_v, shards_v, weights_v,
    flat_b, feat_v, cot_v, wband, hband, conv_v, act_v, dpre_v, grad_v, packed_v, stack_v,
    fh_send, fh_recv, dh_send, dh_recv,
    p1_recv, sum_v, p2_send, p2_recv, p3_all, col_state, grad_shard, own_grad,
    win_send, win_recv, wy_all, wz_all, win_state, win_grad, win_weights,
    local_sem, out_sem, fh_ssem, fh_rsem, dh_ssem, dh_rsem,
    p1_ssem, p1_rsem, p2_ssem, p2_rsem, p3_ssem, p3_rsem,
    col_ssem, col_rsem, share_ssem, share_rsem, b2_ssem, b2_rsem, b3_ssem, b3_rsem,
    w1_ssem, w1_rsem, wy_ssem, wy_rsem, wz_ssem, wz_rsem, wb_ssem, wb_rsem,
    ws_y_ssem, ws_z_ssem, ws_rsem, wshare_ssem, wshare_rsem,
):
    zs, ys, ss, shard_rows, planes, ch, emb = sizes
    rows = 8 * ch
    cells = planes * LANES
    block_rows = ys * shard_rows
    rep = lax.axis_index("rep")
    s = lax.axis_index("slab")
    z = rep // ys
    y = rep % ys

    def at(zz, yy, sl):
        return (zz * ys + yy, sl)

    def remote(src, dst, ssem, rsem, device):
        return pltpu.make_async_remote_copy(
            src_ref=src, dst_ref=dst, send_sem=ssem, recv_sem=rsem, device_id=device, device_id_type=MESH
        )

    ins = (
        (feat_in, feat_ref), (w_in, w_ref), (rep_lanes_in, rep_lanes_ref), (rep_rows_in, rep_rows_ref),
        (rest_in.at[0], rest_v), (headt_in, headt_ref), (rep_emb_in, rep_emb_ref), (bias_in, bias_ref),
        (cot_in, cot_ref), (order_in, order_ref), (add_in, add_ref), (emb_order_in, emb_order_ref),
        (place_in, place_ref),
        *[(ref, own_state.at[pl.ds(i * shard_rows, shard_rows)]) for i, ref in enumerate((moment_in, second_in, master_in))],
    )
    copies = [pltpu.make_async_copy(src, dst, local_sem.at[i]) for i, (src, dst) in enumerate(ins)]
    for copy in copies:
        copy.start()

    barrier = pltpu.get_barrier_semaphore()
    for d in range(1, ss):
        pl.semaphore_signal(barrier, inc=1, device_id=at(z, y, (s + d) % ss), device_id_type=MESH)
    for d in range(1, ys):
        pl.semaphore_signal(barrier, inc=1, device_id=at(z, (y + d) % ys, s), device_id_type=MESH)
    for d in range(1, zs):
        pl.semaphore_signal(barrier, inc=1, device_id=at((z + d) % zs, y, s), device_id_type=MESH)

    copies[0].wait()
    for p in range(planes):
        plane = feat_ref[:, p].astype(f32).reshape(rows, LANES).astype(bf16)
        feat_v[0:rows, LANES * (p + 1) : LANES * (p + 2)] = plane
        if p == 0:
            fh_send[0] = plane
        if p == planes - 1:
            fh_send[1] = plane
    feat_v[rows : rows + 16, :] = jnp.ones((16, cells + 2 * LANES), bf16)
    feat_v[rows + 16 : 256, :] = jnp.zeros((256 - rows - 16, cells + 2 * LANES), bf16)

    pl.semaphore_wait(barrier, (ss - 1) + (ys - 1) + (zs - 1))

    def halo(send, recv, ssem, rsem, up):
        source, slot = (1, 0) if up else (0, 1)
        other = (s + 1) % ss if up else (s + ss - 1) % ss
        return remote(send.at[source], recv.at[slot], ssem.at[source], rsem.at[slot], at(z, y, other))

    def start_halo(send, recv, ssem, rsem):
        @pl.when(s < ss - 1)
        def _():
            halo(send, recv, ssem, rsem, True).start()

        @pl.when(s > 0)
        def _():
            halo(send, recv, ssem, rsem, False).start()

        @pl.when(s == 0)
        def _():
            recv[0] = jnp.zeros((rows, LANES), bf16)

        @pl.when(s == ss - 1)
        def _():
            recv[1] = jnp.zeros((rows, LANES), bf16)

    def wait_halo(send, recv, ssem, rsem):
        @pl.when(s < ss - 1)
        def _():
            halo(send, recv, ssem, rsem, True).wait_send()
            halo(send, recv, ssem, rsem, False).wait_recv()

        @pl.when(s > 0)
        def _():
            halo(send, recv, ssem, rsem, False).wait_send()
            halo(send, recv, ssem, rsem, True).wait_recv()

    start_halo(fh_send, fh_recv, fh_ssem, fh_rsem)

    for i in (13, 14, 15):
        copies[i].wait()
    reducer = z == s
    win_part = WIN // ss
    win_y = (s * win_part) // shard_rows
    win_row = (s * win_part) % shard_rows
    win_source = (z == 0) & (y == win_y)

    def col(d):
        return remote(own_state, col_state, col_ssem.at[d - 1], col_rsem, at((z + d) % zs, y, s))

    def ws_y(d):
        return remote(win_state, win_state, ws_y_ssem.at[d - 1], ws_rsem, at(z, (y + d) % ys, s))

    def ws_z(d):
        return remote(win_state, win_state, ws_z_ssem.at[d - 1], ws_rsem, at((z + d) % zs, y, s))

    @pl.when(reducer)
    def _():
        for d in range(1, zs):
            col(d).start()
        col_state[...] = own_state[...]

    @pl.when(win_source)
    def _():
        for i in range(3):
            win_state[i * win_part : (i + 1) * win_part, :] = own_state[
                pl.ds(pl.multiple_of(i * shard_rows + win_row, 16), win_part), :
            ]
        for d in range(1, ys):
            ws_y(d).start()
        for d in range(1, zs):
            ws_z(d).start()

    copies[4].wait()
    first, last = CONV_ROWS // 16, flat_b.shape[0] // 16 - 1
    flat_b[0 : 16 * first, :] = jnp.zeros((16 * first, LANES), bf16)
    lane16 = iota((16, LANES), 1)

    def moved(here, later):
        return pltpu.roll(jnp.where(lane16 >= LANES - CONV_LANES, here, later), CONV_LANES, 1).astype(bf16)

    def rest_rows(at_row, count):
        start = at_row * LANES
        if not isinstance(start, int):
            start = pl.multiple_of(start, LANES)
        return rest_v[0:1, pl.ds(start, count * LANES)].reshape(count, LANES)

    def align(j, carry):
        at_row = j * 16 - CONV_ROWS - 1
        flat_b[pl.ds(pl.multiple_of(j * 16, 16), 16), :] = moved(rest_rows(at_row, 16), rest_rows(at_row + 1, 16))
        return carry

    lead = CONV_ROWS - 16 * first
    start_rows = rest_rows(0, 8)
    flat_b[16 * first : 16 * first + 16, :] = moved(
        jnp.concatenate([jnp.zeros((lead + 1, LANES), f32), start_rows[0 : 15 - lead]], axis=0),
        jnp.concatenate([jnp.zeros((lead, LANES), f32), start_rows[0 : 16 - lead]], axis=0),
    )
    lax.fori_loop(first + 1, last, align, 0)
    end_row = 16 * last - CONV_ROWS - 1
    end = rest_v[0:1, (end_row + 16) * LANES :]
    end = jnp.concatenate([end, jnp.zeros((1, LANES - end.shape[1]), f32)], axis=1)
    end_rows = rest_rows(end_row, 16)
    flat_b[16 * last : 16 * last + 16, :] = moved(end_rows, jnp.concatenate([end_rows[1:16], end], axis=0))

    def p1(d):
        other = (s + d) % ss
        return remote(
            flat_b.at[pl.ds(pl.multiple_of(other * block_rows, 16), block_rows)],
            p1_recv.at[d - 1], p1_ssem.at[d - 1], p1_rsem.at[d - 1], at(z, y, other),
        )

    for d in range(1, ss):
        p1(d).start()

    row = iota((rows, 256), 0)
    lane = iota((rows, 256), 1)
    shift = (lane % 8) - (7 - row % 8)
    for i in (1, 2, 3, 5, 6, 7, 8):
        copies[i].wait()
    for p in range(planes):
        cot_v[:, LANES * p : LANES * (p + 1)] = cot_ref[:, p].astype(f32).reshape(8 * emb, LANES).astype(bf16)
    spread = dot(w_ref[...].astype(f32).reshape(27 * ch, ch).astype(bf16), rep_lanes_ref[...])
    for a in range(3):
        for c in range(3):
            band = jnp.zeros((rows, 256), f32)
            for b in range(3):
                at_row = (a * 9 + b * 3 + c) * ch
                full = dot(rep_rows_ref[...], spread[at_row : at_row + ch].astype(bf16))
                band = jnp.where(shift == b - 1, full, band)
            wband[a, rows * c : rows * (c + 1), :] = band.astype(bf16)
    head = dot(dot_nt(rep_rows_ref[...], headt_ref[...]).astype(bf16), rep_emb_ref[...])
    hband[...] = jnp.where(shift[:, :LANES] == 0, head, 0.0).astype(bf16)
    bias_row = jnp.concatenate([bias_ref[...], jnp.zeros((1, LANES - ch), f32)], axis=1)
    row_l = iota((rows, LANES), 0)
    lane_l = iota((rows, LANES), 1)
    bias = jnp.sum(jnp.where(lane_l == row_l // 8, jnp.broadcast_to(bias_row, (rows, LANES)), 0.0), axis=1, keepdims=True)

    conv_v[...] = dot(wband[1], feat_v[:, LANES : LANES + cells])
    wait_halo(fh_send, fh_recv, fh_ssem, fh_rsem)
    feat_v[0:rows, 0:LANES] = fh_recv[0]
    feat_v[0:rows, LANES + cells : 2 * LANES + cells] = fh_recv[1]
    conv_v[...] += dot(wband[0], feat_v[:, 0:cells]) + dot(wband[2], feat_v[:, 2 * LANES : 2 * LANES + cells])

    def right(v):
        return jnp.where(lane_l == 0, 0.0, pltpu.roll(v, 1, 1))

    def left(v):
        return jnp.where(lane_l == LANES - 1, 0.0, pltpu.roll(v, LANES - 1, 1))

    def spread_dpre(dpre, p):
        at_lane = slice(LANES * p, LANES * (p + 1))
        dpre_v[0:rows, at_lane] = left(dpre).astype(bf16)
        dpre_v[rows : 2 * rows, at_lane] = dpre.astype(bf16)
        dpre_v[2 * rows : 3 * rows, at_lane] = right(dpre).astype(bf16)

    for p in (0, planes - 1) + tuple(range(1, planes - 1)):
        at_lane = slice(LANES * p, LANES * (p + 1))
        pre = (
            conv_v[rows : 2 * rows, at_lane]
            + right(conv_v[0:rows, at_lane])
            + left(conv_v[2 * rows : 3 * rows, at_lane])
            + bias
        )
        sigma = jax.nn.sigmoid(pre)
        act_v[0:rows, at_lane] = (pre * sigma).astype(bf16)
        dact = dot(hband[...], cot_v[:, at_lane])
        dpre = (dact * sigma * (1.0 + pre * (1.0 - sigma))).astype(bf16)
        if p == 0:
            dh_send[0] = dpre
        if p == planes - 1:
            dh_send[1] = dpre
        spread_dpre(dpre.astype(f32), p + 1)
        if p == planes - 1:
            start_halo(dh_send, dh_recv, dh_ssem, dh_rsem)
    act_v[rows : rows + 16, :] = jnp.ones((16, cells), bf16)

    def p2(d):
        other = (y + d) % ys
        return remote(
            p2_send.at[pl.ds(pl.multiple_of(other * shard_rows, 16), shard_rows)],
            p2_recv.at[d - 1], p2_ssem.at[d - 1], p2_rsem.at[d - 1], at(z, other, s),
        )

    def p3(d, back):
        part = p3_all.at[(z + zs - d) % zs if back else z]
        return remote(part, part, p3_ssem.at[d - 1], p3_rsem.at[d - 1], at((z + d) % zs, y, s))

    def share(d):
        return remote(grad_shard, grad_shard, share_ssem.at[d - 1], share_rsem, at(z, y, (s + d) % ss))

    def b2(d, back):
        owner = (y + ys - d) % ys if back else y
        part = weights_v.at[pl.ds(pl.multiple_of(s * block_rows + owner * shard_rows, 16), shard_rows)]
        return remote(part, part, b2_ssem.at[d - 1], b2_rsem.at[d - 1], at(z, (y + d) % ys, s))

    def b3(d, back):
        owner = (s + ss - d) % ss if back else s
        part = weights_v.at[pl.ds(pl.multiple_of(owner * block_rows, 16), block_rows)]
        return remote(part, part, b3_ssem.at[d - 1], b3_rsem.at[d - 1], at(z, y, (s + d) % ss))

    def w1(d):
        part = win_send.at[pl.ds(pl.multiple_of((s + d) % ss * win_part, 16), win_part)]
        return remote(part, win_recv.at[d - 1], w1_ssem.at[d - 1], w1_rsem.at[d - 1], at(z, y, (s + d) % ss))

    def wy(d, back):
        part = wy_all.at[(y + ys - d) % ys if back else y]
        return remote(part, part, wy_ssem.at[d - 1], wy_rsem.at[d - 1], at(z, (y + d) % ys, s))

    def wz(d, back):
        part = wz_all.at[(z + zs - d) % zs if back else z]
        return remote(part, part, wz_ssem.at[d - 1], wz_rsem.at[d - 1], at((z + d) % zs, y, s))

    def wb(d, back):
        owner = (s + ss - d) % ss if back else s
        part = win_weights.at[pl.ds(pl.multiple_of(owner * win_part, 16), win_part)]
        return remote(part, part, wb_ssem.at[d - 1], wb_rsem.at[d - 1], at(z, y, (s + d) % ss))

    per_shard = shard_rows // win_part

    def wshare(d):
        part = win_grad.at[s % per_shard]
        return remote(part, part, wshare_ssem.at[d - 1], wshare_rsem.at[s % per_shard], at(z, y, (s + d) % ss))

    def updated(grad, state):
        count = grad.shape[0]
        return adam_update(grad, state[0:count, :], state[count : 2 * count, :], state[2 * count : 3 * count, :])

    def start_ys():
        for d in range(1, ss):
            p1(d).wait_recv()
        total = flat_b[pl.ds(pl.multiple_of(s * block_rows, 16), block_rows), :].astype(f32)
        for d in range(1, ss):
            total = total + p1_recv[d - 1].astype(f32)
        sum_v[...] = total
        p2_send[...] = total.astype(bf16)
        for d in range(1, ys):
            p2(d).start()

    def start_zs():
        for d in range(1, ys):
            p2(d).wait_recv()
        total = sum_v[pl.ds(pl.multiple_of(y * shard_rows, 16), shard_rows), :]
        for d in range(1, ys):
            total = total + p2_recv[d - 1].astype(f32)
        p3_all[z] = total.astype(bf16)
        for d in range(1, zs):
            p3(d, False).start()

    def start_gather_ys():
        @pl.when(jnp.logical_not(reducer))
        def _():
            col(1).wait_recv()

        for d in range(1, zs):
            p3(d, True).wait_recv()
        grad = p3_all[0].astype(f32)
        for i in range(1, zs):
            grad = grad + p3_all[i].astype(f32)
        grad = grad / LOSS_SCALE
        weights = updated(grad, col_state)[2].astype(bf16)
        weights_v[pl.ds(pl.multiple_of(s * block_rows + y * shard_rows, 16), shard_rows), :] = weights
        for d in range(1, ys):
            b2(d, False).start()

        @pl.when(reducer)
        def _():
            grad_shard[...] = grad
            for d in range(1, ss):
                share(d).start()

    def start_gather_slabs():
        for d in range(1, ys):
            b2(d, True).wait_recv()
        for d in range(1, ss):
            b3(d, False).start()

    def start_window_ys():
        for d in range(1, ss):
            w1(d).wait_recv()
        total = win_send[pl.ds(pl.multiple_of(s * win_part, 16), win_part), :].astype(f32)
        for d in range(1, ss):
            total = total + win_recv[d - 1].astype(f32)
        wy_all[y] = total.astype(bf16)
        for d in range(1, ys):
            wy(d, False).start()

    def start_window_zs():
        for d in range(1, ys):
            wy(d, True).wait_recv()
        total = wy_all[0].astype(f32)
        for i in range(1, ys):
            total = total + wy_all[i].astype(f32)
        wz_all[z] = total.astype(bf16)
        for d in range(1, zs):
            wz(d, False).start()

    in_window = (z == 0) & (y < WIN // shard_rows)
    win_owner = (z == 0) & (y == win_y)

    def start_window_gather():
        for d in range(1, zs):
            wz(d, True).wait_recv()
        grad = wz_all[0].astype(f32)
        for i in range(1, zs):
            grad = grad + wz_all[i].astype(f32)
        grad = grad / LOSS_SCALE
        weights = updated(grad, win_state)[2].astype(bf16)
        win_weights[pl.ds(pl.multiple_of(s * win_part, 16), win_part), :] = weights
        for d in range(1, ss):
            wb(d, False).start()

        @pl.when(win_owner)
        def _():
            win_grad[s % per_shard] = grad
            for d in range(1, ss):
                wshare(d).start()

    def finish_window():
        for d in range(1, ss):
            wb(d, True).wait_recv()

    def own_update():
        @pl.when(jnp.logical_not(reducer))
        def _():
            share(1).wait_recv()

        own_grad[...] = grad_shard[...]

        @pl.when(in_window)
        def _():
            for i in range(per_shard):
                @pl.when(s != y * per_shard + i)
                def _():
                    part = win_grad.at[i]
                    remote(part, part, wshare_ssem.at[0], wshare_rsem.at[i], at(z, y, (s + 1) % ss)).wait_recv()

                own_grad[i * win_part : (i + 1) * win_part, :] = win_grad[i]

        for i, value in enumerate(updated(own_grad[...], own_state)):
            shards_v[i] = value

    outs = [pltpu.make_async_copy(igrad_v, igrad_out, out_sem.at[0])]
    outs += [
        pltpu.make_async_copy(shards_v.at[i], ref, out_sem.at[1 + i]) for i, ref in enumerate((nmom_out, nsec_out, nmas_out))
    ]
    outs += [pltpu.make_async_copy(weights_v, weights_out, out_sem.at[4])]

    mask = ((lane < rows) & (shift >= -1) & (shift <= 1)) | ((lane >= rows) & (lane < rows + 8) & (shift == 0))
    mask = [mask[:, :LANES], mask[:, LANES:]]
    for a in range(3):
        grad_v[a] = dot_nt(dpre_v[:, LANES : LANES + cells], feat_v[:, LANES * a : LANES * a + cells])
    start_ys()
    for i in range(9, 13):
        copies[i].wait()

    def rolled(v, by):
        return jnp.concatenate(
            [pltpu.roll(v[8 * o : 8 * o + 8], by, 1, stride=1, stride_axis=0) for o in range(v.shape[0] // 8)], axis=0
        )

    for pair in range(5):
        for t in range(2):
            total = None
            for slot in range(2):
                if pair * 2 + slot < 9:
                    a, c = divmod(pair * 2 + slot, 3)
                    part = grad_v[a, rows * c : rows * (c + 1), LANES * t : LANES * (t + 1)]
                    part = rolled(jnp.where(mask[t], part, 0.0), 3 * slot)
                    total = part if total is None else total + part
            at_lane = pair * 256 + t * LANES
            packed_v[:, at_lane : at_lane + LANES] = total.astype(bf16)
    sums = dot(add_ref[0:ch, 0:rows], packed_v[...])
    ordered = dot(sums.astype(bf16), order_ref[...])
    lane8 = iota((8, LANES), 1)
    row8 = iota((8, LANES), 0)
    zero8 = jnp.zeros((8, LANES), f32)
    for t in range(ch // 8):
        whole, base = divmod(64 * t, LANES)
        by = base + 8 * row8
        tiles = []
        for k in range(6):
            piece = ordered[8 * t : 8 * t + 8, LANES * k : LANES * (k + 1)]
            if k == 5:
                piece = jnp.where(lane8 < 8, piece, 0.0)
            tiles.append(pltpu.roll(piece, base, 1, stride=8, stride_axis=0))
        for m in range(7):
            k = m - whole
            high = tiles[k] if 0 <= k < 6 else zero8
            low = tiles[k - 1] if 0 <= k - 1 < 6 else zero8
            stack_v[m * ch + 8 * t : m * ch + 8 * t + 8, :] = jnp.where(lane8 >= by, high, low)
        bgrad = jnp.broadcast_to(ordered[8 * t : 8 * t + 8, 27 * ch : 27 * ch + 1], (8, LANES))
        stack_v[7 * ch + 8 * t : 7 * ch + 8 * t + 8, :] = jnp.where(lane8 == 64 + 8 * t + row8, bgrad, 0.0)

    hgrad = dot_nt(act_v[...], cot_v[...])
    row_h = iota((rows + 16, LANES), 0)
    lane_h = iota((rows + 16, LANES), 1)
    hgrad = rolled(jnp.where(lane_h % 8 == 7 - row_h % 8, hgrad, 0.0), 0).astype(bf16)
    hgrad = dot(dot(add_ref[...], hgrad).astype(bf16), emb_order_ref[...])
    for t in range(4):
        piece = pltpu.roll(hgrad[8 * t : 8 * t + 8], 0, 1, stride=16, stride_axis=0)
        stack_v[192 + 8 * t : 200 + 8 * t, :] = jnp.where(lane8 >= 88, piece, 0.0)
        stack_v[224 + 8 * t : 232 + 8 * t, :] = jnp.where(lane8 < 88, piece, 0.0)
    window = dot(place_ref[...], stack_v[...].astype(bf16)) + flat_b[0:WIN, :].astype(f32)
    win_send[...] = window.astype(bf16)
    for d in range(1, ss):
        w1(d).start()

    @pl.when((z == 0) & (y != win_y))
    def _():
        ws_y(1).wait_recv()
        for d in range(1, zs):
            ws_z(d).start()

    start_zs()

    wait_halo(dh_send, dh_recv, dh_ssem, dh_rsem)
    spread_dpre(dh_recv[0].astype(f32), 0)
    spread_dpre(dh_recv[1].astype(f32), planes + 1)

    total = None
    for a in range(3):
        part = dot_tn(wband[a, :, 0:rows], dpre_v[:, LANES * (2 - a) : LANES * (2 - a) + cells])
        total = part if total is None else total + part
    for p in range(planes):
        igrad_v[:, p] = total[:, LANES * p : LANES * (p + 1)].reshape(ch, 8, LANES).astype(bf16)
    outs[0].start()

    start_window_ys()
    start_gather_ys()
    start_window_zs()
    start_gather_slabs()
    @pl.when(z != 0)
    def _():
        ws_z(1).wait_recv()

    start_window_gather()
    own_update()
    for out in outs[1:4]:
        out.start()
    finish_window()
    for d in range(1, ss):
        b3(d, True).wait_recv()
    for d in range(1, ss):
        b3(d, False).wait_send()
    for d in range(1, ys):
        b2(d, False).wait_send()
    weights_v[0:WIN, :] = win_weights[...]
    outs[4].start()

    for d in range(1, ss):
        p1(d).wait_send()
        w1(d).wait_send()
        wb(d, False).wait_send()
    for d in range(1, ys):
        p2(d).wait_send()
        wy(d, False).wait_send()
    for d in range(1, zs):
        p3(d, False).wait_send()
        wz(d, False).wait_send()

    @pl.when(reducer)
    def _():
        for d in range(1, zs):
            col(d).wait_send()
        for d in range(1, ss):
            share(d).wait_send()

    @pl.when(win_source)
    def _():
        for d in range(1, ys):
            ws_y(d).wait_send()

    @pl.when(z == 0)
    def _():
        for d in range(1, zs):
            ws_z(d).wait_send()

    @pl.when(win_owner)
    def _():
        for d in range(1, ss):
            wshare(d).wait_send()

    for out in outs:
        out.wait()


def copy_kernel(*refs):
    count = (len(refs) - 2) // 3
    in_sem, out_sem = refs[3 * count :]
    loads = [pltpu.make_async_copy(refs[i], refs[2 * count + i], in_sem.at[i]) for i in range(count)]
    stores = [pltpu.make_async_copy(refs[2 * count + i], refs[count + i], out_sem.at[i]) for i in range(count)]
    for load in loads:
        load.start()
    for load, store in zip(loads, stores):
        load.wait()
        store.start()
    for store in stores:
        store.wait()


def on_device(
    features, cotangent, conv_weight, conv_bias, head_weight, grad_rest, master, moment, second
):
    ss = lax.axis_size("slab")
    zs = ss
    ys = lax.axis_size("rep") // zs
    ch, planes = features.shape[1], features.shape[2]
    emb = cotangent.shape[1]
    rows = 8 * ch
    cells = planes * LANES
    shard_rows = master.shape[0] // LANES
    block_rows = ys * shard_rows
    all_rows = ss * block_rows
    win_part = WIN // ss
    rest = grad_rest.shape[2]
    sizes = (zs, ys, ss, shard_rows, planes, ch, emb)
    tables = selection_tables(ch, emb)
    hbm = pl.BlockSpec(memory_space=pltpu.HBM)
    dma = pltpu.SemaphoreType.DMA
    shard = jax.ShapeDtypeStruct((shard_rows, LANES), f32)
    outs = pl.pallas_call(
        functools.partial(kernel, sizes),
        out_shape=(
            jax.ShapeDtypeStruct(features.shape[1:], bf16),
            shard,
            shard,
            shard,
            jax.ShapeDtypeStruct((all_rows, LANES), bf16),
        ),
        in_specs=[hbm] * 16,
        out_specs=(hbm,) * 5,
        scratch_shapes=[
            pltpu.VMEM(features.shape[1:], bf16),
            pltpu.VMEM(cotangent.shape[1:], bf16),
            pltpu.VMEM((27, ch, ch), bf16),
            pltpu.VMEM((1, ch), f32),
            pltpu.VMEM((emb, ch), bf16),
            pltpu.VMEM((1, rest), f32),
            pltpu.VMEM((3 * shard_rows, LANES), f32),
            *[pltpu.VMEM(t.shape, bf16) for t in tables],
            pltpu.VMEM(features.shape[1:], bf16),
            pltpu.VMEM((3, shard_rows, LANES), f32),
            pltpu.VMEM((all_rows, LANES), bf16),
            pltpu.VMEM((all_rows, LANES), bf16),
            pltpu.VMEM((256, cells + 2 * LANES), bf16),
            pltpu.VMEM((8 * emb, cells), bf16),
            pltpu.VMEM((3, 3 * rows, 256), bf16),
            pltpu.VMEM((rows, LANES), bf16),
            pltpu.VMEM((3 * rows, cells), f32),
            pltpu.VMEM((rows + 16, cells), bf16),
            pltpu.VMEM((3 * rows, cells + 2 * LANES), bf16),
            pltpu.VMEM((3, 3 * rows, 256), f32),
            pltpu.VMEM((rows, 5 * 256), bf16),
            pltpu.VMEM((256, LANES), f32),
            pltpu.VMEM((2, rows, LANES), bf16),
            pltpu.VMEM((2, rows, LANES), bf16),
            pltpu.VMEM((2, rows, LANES), bf16),
            pltpu.VMEM((2, rows, LANES), bf16),
            pltpu.VMEM((ss - 1, block_rows, LANES), bf16),
            pltpu.VMEM((block_rows, LANES), f32),
            pltpu.VMEM((block_rows, LANES), bf16),
            pltpu.VMEM((ys - 1, shard_rows, LANES), bf16),
            pltpu.VMEM((zs, shard_rows, LANES), bf16),
            pltpu.VMEM((3 * shard_rows, LANES), f32),
            pltpu.VMEM((shard_rows, LANES), f32),
            pltpu.VMEM((shard_rows, LANES), f32),
            pltpu.VMEM((WIN, LANES), bf16),
            pltpu.VMEM((ss - 1, win_part, LANES), bf16),
            pltpu.VMEM((ys, win_part, LANES), bf16),
            pltpu.VMEM((zs, win_part, LANES), bf16),
            pltpu.VMEM((3 * win_part, LANES), f32),
            pltpu.VMEM((shard_rows // win_part, win_part, LANES), f32),
            pltpu.VMEM((WIN, LANES), bf16),
            dma((16,)), dma((5,)),
            dma((2,)), dma((2,)), dma((2,)), dma((2,)),
            dma((ss - 1,)), dma((ss - 1,)),
            dma((ys - 1,)), dma((ys - 1,)),
            dma((zs - 1,)), dma((zs - 1,)),
            dma((zs - 1,)), dma,
            dma((ss - 1,)), dma,
            dma((ys - 1,)), dma((ys - 1,)),
            dma((ss - 1,)), dma((ss - 1,)),
            dma((ss - 1,)), dma((ss - 1,)),
            dma((ys - 1,)), dma((ys - 1,)),
            dma((zs - 1,)), dma((zs - 1,)),
            dma((ss - 1,)), dma((ss - 1,)),
            dma((ys - 1,)), dma((zs - 1,)), dma,
            dma((ss - 1,)), dma((shard_rows // win_part,)),
        ],
        compiler_params=pltpu.CompilerParams(
            collective_id=0, has_side_effects=True, vmem_limit_bytes=60 << 20
        ),
    )(
        features[0],
        cotangent[0],
        conv_weight.transpose(2, 3, 4, 0, 1).reshape(27, ch, ch),
        conv_bias.reshape(1, ch),
        head_weight.T,
        grad_rest,
        master.reshape(shard_rows, LANES),
        moment.reshape(shard_rows, LANES),
        second.reshape(shard_rows, LANES),
        *tables,
    )
    igrad, new_moment, new_second, new_master, weights = pl.pallas_call(
        copy_kernel,
        out_shape=tuple(jax.ShapeDtypeStruct(out.shape, out.dtype) for out in outs),
        in_specs=[pl.BlockSpec(memory_space=pl.ANY)] * 5,
        out_specs=(pl.BlockSpec(memory_space=pl.ANY),) * 5,
        scratch_shapes=[pltpu.VMEM(out.shape, out.dtype) for out in outs] + [dma((5,)), dma((5,))],
        compiler_params=pltpu.CompilerParams(vmem_limit_bytes=60 << 20),
    )(*outs)
    return (
        igrad[None],
        new_moment.reshape(-1),
        new_second.reshape(-1),
        new_master.reshape(-1),
        weights.reshape(-1),
    )


def solution(mesh):
    return jax.shard_map(
        on_device,
        mesh=mesh,
        in_specs=(
            P("rep", None, "slab", None, None),
            P("rep", None, "slab", None, None),
            P(),
            P(),
            P(),
            P("rep", "slab", None),
            P("rep"),
            P("rep"),
            P("rep"),
        ),
        out_specs=(P("rep", None, "slab", None, None), P("rep"), P("rep"), P("rep"), P()),
        check_vma=False,
    )
```

```python
import functools

import jax
import jax.numpy as jnp
import numpy as np
from jax import lax
from jax.experimental import pallas as pl
from jax.experimental.pallas import tpu as pltpu
from jax.sharding import PartitionSpec as P

LOSS_SCALE = 2048

beta_one = 0.9
beta_two = 0.99
learn_rate = 0.01
adam_eps = 1e-08
step_count = 10.0

f32 = jnp.float32
bf16 = jnp.bfloat16
MESH = pl.DeviceIdType.MESH
LANES = 128
CONV_ROWS = 124
CONV_LANES = 104
WIN = 128


def adam_update(grad, moment, second, master):
    new_moment = beta_one * moment + (1.0 - beta_one) * grad
    new_second = beta_two * second + (1.0 - beta_two) * grad * grad
    update = (
        new_moment
        / (1.0 - beta_one**step_count)
        / (jnp.sqrt(new_second / (1.0 - beta_two**step_count)) + adam_eps)
    )
    return (new_moment, new_second, master - learn_rate * update)


def selection_tables(ch, emb):
    rows = 8 * ch
    repeat_rows = np.zeros((rows, ch), np.float32)
    repeat_rows[np.arange(rows), np.arange(rows) // 8] = 1
    repeat_lanes = np.zeros((ch, 256), np.float32)
    repeat_lanes[np.arange(rows) // 8, np.arange(rows)] = 1
    repeat_emb = np.zeros((emb, 128), np.float32)
    repeat_emb[np.arange(128) // 8, np.arange(128)] = 1
    add_rows = np.zeros((32, rows + 16), np.float32)
    for i in range(ch + 1):
        add_rows[i, 8 * i : 8 * i + 8] = 1
    order = np.zeros((5 * 256, 768), np.float32)
    for a in range(3):
        for c in range(3):
            pair, slot = divmod(a * 3 + c, 2)
            for i in range(ch):
                tile, local = divmod(i, 16)
                for b in range(3):
                    lane = (8 * local + 6 + b + 3 * slot) % 128
                    order[pair * 256 + tile * 128 + lane, i * 27 + a * 9 + b * 3 + c] = 1
    order[2 * 256 + 128 + 8 * 8 + 7, ch * 27] = 1
    emb_order = np.zeros((128, 128), np.float32)
    for e in range(emb):
        emb_order[8 * e + 7, 88 + e] = 1
    place = np.zeros((WIN, 256), np.float32)
    for o in range(ch):
        for k in range(7):
            place[5 * o + k, k * ch + o] = 1
        place[121, 7 * ch + o] = 1
    for i in range(ch + 1):
        place[121 + i // 8, 192 + i] = 1
        place[122 + i // 8, 224 + i] = 1
    tables = (repeat_rows, repeat_lanes, repeat_emb, add_rows, order, emb_order, place)
    return tuple(jnp.asarray(t, bf16) for t in tables)


def dot(lhs, rhs):
    return jnp.dot(lhs, rhs, preferred_element_type=f32)


def dot_nt(lhs, rhs):
    return lax.dot_general(lhs, rhs, (((1,), (1,)), ((), ())), preferred_element_type=f32)


def dot_tn(lhs, rhs):
    return lax.dot_general(lhs, rhs, (((0,), (0,)), ((), ())), preferred_element_type=f32)


def iota(shape, dim):
    return lax.broadcasted_iota(jnp.int32, shape, dim)


def kernel(
    sizes,
    feat_in, cot_in, w_in, bias_in, headt_in, rest_in, master_in, moment_in, second_in,
    rep_rows_in, rep_lanes_in, rep_emb_in, add_in, order_in, emb_order_in, place_in,
    igrad_out, nmom_out, nsec_out, nmas_out, weights_out,
    feat_ref, cot_ref, w_ref, bias_ref, headt_ref, rest_1d, own_state,
    rep_rows_ref, rep_lanes_ref, rep_emb_ref, add_ref, order_ref, emb_order_ref, place_ref,
    igrad_v, shards_v, weights_v,
    flat_b, feat_v, cot_v, wband, hband, conv_v, act_v, dpre_v, grad_v, packed_v, stack_v,
    fh_send, fh_recv, dh_send, dh_recv,
    p1a_recv, pair_sum, p1b_recv, sum_v, p2_send, p2_recv, p3_all, col_state, grad_shard, own_grad,
    win_send, win_recv, wy_all, wz_all, win_state, win_grad, win_weights,
    local_sem, out_sem, fh_ssem, fh_rsem, dh_ssem, dh_rsem,
    p1a_ssem, p1a_rsem, p1b_ssem, p1b_rsem, p2_ssem, p2_rsem, p3_ssem, p3_rsem,
    col_ssem, col_rsem, share_ssem, share_rsem, b2_ssem, b2_rsem, b3x_ssem, b3x_rsem, b3c_ssem, b3c_rsem,
    w1_ssem, w1_rsem, wy_ssem, wy_rsem, wz_ssem, wz_rsem, wb_ssem, wb_rsem,
    ws_y_ssem, ws_z_ssem, ws_rsem, wshare_ssem, wshare_rsem,
):
    zs, ys, ss, shard_rows, planes, ch, emb = sizes
    rows = 8 * ch
    cells = planes * LANES
    block_rows = ys * shard_rows
    rep = lax.axis_index("rep")
    s = lax.axis_index("slab")
    z = rep // ys
    y = rep % ys

    def at(zz, yy, sl):
        return (zz * ys + yy, sl)

    def remote(src, dst, ssem, rsem, device):
        return pltpu.make_async_remote_copy(
            src_ref=src, dst_ref=dst, send_sem=ssem, recv_sem=rsem, device_id=device, device_id_type=MESH
        )

    barrier = pltpu.get_barrier_semaphore()
    for d in range(1, ss):
        pl.semaphore_signal(barrier, inc=1, device_id=at(z, y, (s + d) % ss), device_id_type=MESH)
    for d in range(1, ys):
        pl.semaphore_signal(barrier, inc=1, device_id=at(z, (y + d) % ys, s), device_id_type=MESH)
    for d in range(1, zs):
        pl.semaphore_signal(barrier, inc=1, device_id=at((z + d) % zs, y, s), device_id_type=MESH)

    ins = (
        (feat_in, feat_ref), (w_in, w_ref), (rep_lanes_in, rep_lanes_ref), (rep_rows_in, rep_rows_ref),
        (rest_in.at[0], rest_1d), (headt_in, headt_ref), (rep_emb_in, rep_emb_ref), (bias_in, bias_ref),
        (cot_in, cot_ref), (order_in, order_ref), (add_in, add_ref), (emb_order_in, emb_order_ref),
        (place_in, place_ref),
        *[(ref, own_state.at[pl.ds(i * shard_rows, shard_rows)]) for i, ref in enumerate((moment_in, second_in, master_in))],
    )
    copies = [pltpu.make_async_copy(src, dst, local_sem.at[i]) for i, (src, dst) in enumerate(ins)]
    for copy in copies:
        copy.start()

    copies[4].wait()
    first, last = CONV_ROWS // 16, flat_b.shape[0] // 16 - 1
    flat_b[0 : 16 * first, :] = jnp.zeros((16 * first, LANES), bf16)
    lane16 = iota((16, LANES), 1)

    def moved(here, later):
        return pltpu.roll(jnp.where(lane16 >= LANES - CONV_LANES, here, later), CONV_LANES, 1).astype(bf16)

    def rest_rows(start, count):
        return rest_1d[0:1, pl.ds(start, count * LANES)].reshape(count, LANES)

    lane8 = iota((8, LANES), 1)

    def moved8(here, later):
        return pltpu.roll(jnp.where(lane8 >= LANES - CONV_LANES, here, later), CONV_LANES, 1)

    per_step = 8
    skipped = (16 * (first + 1) - CONV_ROWS - 1) * LANES

    def align_at(at_row):
        halves = []
        for h in range(2):
            start = (at_row + 8 * h) * LANES + skipped
            halves.append(moved8(rest_rows(start, 8), rest_rows(start + LANES, 8)))
        part = jnp.concatenate(halves, axis=0).astype(bf16)
        flat_b[pl.ds(at_row + 16 * (first + 1), 16), :] = part

    def align(j, carry):
        for i in range(per_step):
            align_at(pl.multiple_of(j * (16 * per_step), 16 * per_step) + 16 * i)
        return carry

    steps = (last - first - 1) // per_step
    lax.fori_loop(0, steps, align, 0)
    for j in range(steps * per_step, last - first - 1):
        align_at(16 * j)
    lead = CONV_ROWS - 16 * first
    start_rows = rest_rows(0, 8)
    flat_b[16 * first : 16 * first + 16, :] = moved(
        jnp.concatenate([jnp.zeros((lead + 1, LANES), f32), start_rows[0 : 15 - lead]], axis=0),
        jnp.concatenate([jnp.zeros((lead, LANES), f32), start_rows[0 : 16 - lead]], axis=0),
    )
    end_row = 16 * last - CONV_ROWS - 1
    end = rest_1d[0:1, (end_row + 16) * LANES :]
    end = jnp.concatenate([end, jnp.zeros((1, LANES - end.shape[1]), f32)], axis=1)
    end_rows = rest_rows(end_row * LANES, 16)
    flat_b[16 * last : 16 * last + 16, :] = moved(end_rows, jnp.concatenate([end_rows[1:16], end], axis=0))

    copies[0].wait()
    for p in range(planes):
        plane = feat_ref[:, p].astype(f32).reshape(rows, LANES).astype(bf16)
        feat_v[0:rows, LANES * (p + 1) : LANES * (p + 2)] = plane
        if p == 0:
            fh_send[0] = plane
        if p == planes - 1:
            fh_send[1] = plane
    feat_v[rows : rows + 16, :] = jnp.ones((16, cells + 2 * LANES), bf16)
    feat_v[rows + 16 : 256, :] = jnp.zeros((256 - rows - 16, cells + 2 * LANES), bf16)

    pl.semaphore_wait(barrier, (ss - 1) + (ys - 1) + (zs - 1))

    xs = ss // 2
    x = s // 2
    core = s % 2

    def block(ref, xx, cc):
        return ref.at[pl.ds(pl.multiple_of((xx * 2 + cc) * block_rows, 16), block_rows)]

    def p1a(i):
        return remote(
            block(flat_b, i, 1 - core), p1a_recv.at[i], p1a_ssem.at[i], p1a_rsem.at[i], at(z, y, x * 2 + 1 - core)
        )

    def p1b(d):
        to = (x + d) % xs
        return remote(
            pair_sum.at[to], p1b_recv.at[d - 1], p1b_ssem.at[d - 1], p1b_rsem.at[d - 1], at(z, y, to * 2 + core)
        )

    for i in range(xs):
        p1a(i).start()

    def halo(send, recv, ssem, rsem, up):
        source, slot = (1, 0) if up else (0, 1)
        other = (s + 1) % ss if up else (s + ss - 1) % ss
        return remote(send.at[source], recv.at[slot], ssem.at[source], rsem.at[slot], at(z, y, other))

    def start_halo(send, recv, ssem, rsem):
        @pl.when(s < ss - 1)
        def _():
            halo(send, recv, ssem, rsem, True).start()

        @pl.when(s > 0)
        def _():
            halo(send, recv, ssem, rsem, False).start()

        @pl.when(s == 0)
        def _():
            recv[0] = jnp.zeros((rows, LANES), bf16)

        @pl.when(s == ss - 1)
        def _():
            recv[1] = jnp.zeros((rows, LANES), bf16)

    def wait_halo(send, recv, ssem, rsem):
        @pl.when(s < ss - 1)
        def _():
            halo(send, recv, ssem, rsem, True).wait_send()
            halo(send, recv, ssem, rsem, False).wait_recv()

        @pl.when(s > 0)
        def _():
            halo(send, recv, ssem, rsem, False).wait_send()
            halo(send, recv, ssem, rsem, True).wait_recv()

    start_halo(fh_send, fh_recv, fh_ssem, fh_rsem)

    for i in range(xs):
        p1a(i).wait_recv()

        def add_pair(j, carry):
            at_row = pl.multiple_of(j * 32, 32)
            own = flat_b[pl.ds(pl.multiple_of((i * 2 + core) * block_rows + at_row, 32), 32), :].astype(f32)
            total = own + p1a_recv[i, pl.ds(at_row, 32), :].astype(f32)
            pair_sum[i, pl.ds(at_row, 32), :] = total.astype(bf16)
            return carry

        lax.fori_loop(0, block_rows // 32, add_pair, 0)
    for d in range(1, xs):
        p1b(d).start()

    for i in (13, 14, 15):
        copies[i].wait()
    reducer = z == s
    win_part = WIN // ss
    win_y = (s * win_part) // shard_rows
    win_row = (s * win_part) % shard_rows
    win_source = (z == 0) & (y == win_y)

    def col(d):
        return remote(own_state, col_state, col_ssem.at[d - 1], col_rsem, at((z + d) % zs, y, s))

    def ws_y(d):
        return remote(win_state, win_state, ws_y_ssem.at[d - 1], ws_rsem, at(z, (y + d) % ys, s))

    def ws_z(d):
        return remote(win_state, win_state, ws_z_ssem.at[d - 1], ws_rsem, at((z + d) % zs, y, s))

    @pl.when(reducer)
    def _():
        for d in range(1, zs):
            col(d).start()
        col_state[...] = own_state[...]

    @pl.when(win_source)
    def _():
        for i in range(3):
            win_state[i * win_part : (i + 1) * win_part, :] = own_state[
                pl.ds(pl.multiple_of(i * shard_rows + win_row, 16), win_part), :
            ]
        for d in range(1, ys):
            ws_y(d).start()
        for d in range(1, zs):
            ws_z(d).start()

    row = iota((rows, 256), 0)
    lane = iota((rows, 256), 1)
    shift = (lane % 8) - (7 - row % 8)
    for i in (1, 2, 3, 5, 6, 7, 8):
        copies[i].wait()
    for p in range(planes):
        cot_v[:, LANES * p : LANES * (p + 1)] = cot_ref[:, p].astype(f32).reshape(8 * emb, LANES).astype(bf16)
    spread = dot(w_ref[...].astype(f32).reshape(27 * ch, ch).astype(bf16), rep_lanes_ref[...])
    for a in range(3):
        for c in range(3):
            band = jnp.zeros((rows, 256), f32)
            for b in range(3):
                at_row = (a * 9 + b * 3 + c) * ch
                full = dot(rep_rows_ref[...], spread[at_row : at_row + ch].astype(bf16))
                band = jnp.where(shift == b - 1, full, band)
            wband[a, rows * c : rows * (c + 1), :] = band.astype(bf16)
    head = dot(dot_nt(rep_rows_ref[...], headt_ref[...]).astype(bf16), rep_emb_ref[...])
    hband[...] = jnp.where(shift[:, :LANES] == 0, head, 0.0).astype(bf16)
    bias_row = jnp.concatenate([bias_ref[...], jnp.zeros((1, LANES - ch), f32)], axis=1)
    row_l = iota((rows, LANES), 0)
    lane_l = iota((rows, LANES), 1)
    bias = jnp.sum(jnp.where(lane_l == row_l // 8, jnp.broadcast_to(bias_row, (rows, LANES)), 0.0), axis=1, keepdims=True)

    conv_v[...] = dot(wband[1], feat_v[:, LANES : LANES + cells])
    wait_halo(fh_send, fh_recv, fh_ssem, fh_rsem)
    feat_v[0:rows, 0:LANES] = fh_recv[0]
    feat_v[0:rows, LANES + cells : 2 * LANES + cells] = fh_recv[1]
    conv_v[...] += dot(wband[0], feat_v[:, 0:cells]) + dot(wband[2], feat_v[:, 2 * LANES : 2 * LANES + cells])

    def right(v):
        return jnp.where(lane_l == 0, 0.0, pltpu.roll(v, 1, 1))

    def left(v):
        return jnp.where(lane_l == LANES - 1, 0.0, pltpu.roll(v, LANES - 1, 1))

    def spread_dpre(dpre, p):
        at_lane = slice(LANES * p, LANES * (p + 1))
        dpre_v[0:rows, at_lane] = left(dpre).astype(bf16)
        dpre_v[rows : 2 * rows, at_lane] = dpre.astype(bf16)
        dpre_v[2 * rows : 3 * rows, at_lane] = right(dpre).astype(bf16)

    for p in (0, planes - 1) + tuple(range(1, planes - 1)):
        at_lane = slice(LANES * p, LANES * (p + 1))
        pre = (
            conv_v[rows : 2 * rows, at_lane]
            + right(conv_v[0:rows, at_lane])
            + left(conv_v[2 * rows : 3 * rows, at_lane])
            + bias
        )
        sigma = jax.nn.sigmoid(pre)
        act_v[0:rows, at_lane] = (pre * sigma).astype(bf16)
        dact = dot(hband[...], cot_v[:, at_lane])
        dpre = (dact * sigma * (1.0 + pre * (1.0 - sigma))).astype(bf16)
        if p == 0:
            dh_send[0] = dpre
        if p == planes - 1:
            dh_send[1] = dpre
        spread_dpre(dpre.astype(f32), p + 1)
        if p == planes - 1:
            start_halo(dh_send, dh_recv, dh_ssem, dh_rsem)
    act_v[rows : rows + 16, :] = jnp.ones((16, cells), bf16)

    def p2(d):
        other = (y + d) % ys
        return remote(
            p2_send.at[pl.ds(pl.multiple_of(other * shard_rows, 16), shard_rows)],
            p2_recv.at[d - 1], p2_ssem.at[d - 1], p2_rsem.at[d - 1], at(z, other, s),
        )

    def p3(d, back):
        part = p3_all.at[(z + zs - d) % zs if back else z]
        return remote(part, part, p3_ssem.at[d - 1], p3_rsem.at[d - 1], at((z + d) % zs, y, s))

    def share(d):
        return remote(grad_shard, grad_shard, share_ssem.at[d - 1], share_rsem, at(z, y, (s + d) % ss))

    def b2(d, back):
        owner = (y + ys - d) % ys if back else y
        part = weights_v.at[pl.ds(pl.multiple_of(s * block_rows + owner * shard_rows, 16), shard_rows)]
        return remote(part, part, b2_ssem.at[d - 1], b2_rsem.at[d - 1], at(z, (y + d) % ys, s))

    def b3x(d, back):
        part = block(weights_v, (x + xs - d) % xs if back else x, core)
        return remote(part, part, b3x_ssem.at[d - 1], b3x_rsem.at[d - 1], at(z, y, (x + d) % xs * 2 + core))

    def b3c(d, back):
        part = block(weights_v, (x + xs - d) % xs, 1 - core if back else core)
        return remote(part, part, b3c_ssem.at[d], b3c_rsem.at[d], at(z, y, x * 2 + 1 - core))

    def w1(d):
        part = win_send.at[pl.ds(pl.multiple_of((s + d) % ss * win_part, 16), win_part)]
        return remote(part, win_recv.at[d - 1], w1_ssem.at[d - 1], w1_rsem.at[d - 1], at(z, y, (s + d) % ss))

    def wy(d, back):
        part = wy_all.at[(y + ys - d) % ys if back else y]
        return remote(part, part, wy_ssem.at[d - 1], wy_rsem.at[d - 1], at(z, (y + d) % ys, s))

    def wz(d, back):
        part = wz_all.at[(z + zs - d) % zs if back else z]
        return remote(part, part, wz_ssem.at[d - 1], wz_rsem.at[d - 1], at((z + d) % zs, y, s))

    def wb(d, back):
        owner = (s + ss - d) % ss if back else s
        part = win_weights.at[pl.ds(pl.multiple_of(owner * win_part, 16), win_part)]
        return remote(part, part, wb_ssem.at[d - 1], wb_rsem.at[d - 1], at(z, y, (s + d) % ss))

    per_shard = shard_rows // win_part

    def wshare(d):
        part = win_grad.at[s % per_shard]
        return remote(part, part, wshare_ssem.at[d - 1], wshare_rsem.at[s % per_shard], at(z, y, (s + d) % ss))

    def wshare_in(i):
        part = win_grad.at[i]
        return remote(part, part, wshare_ssem.at[0], wshare_rsem.at[i], at(z, y, (s + 1) % ss))

    def updated(grad, state):
        count = grad.shape[0]
        return adam_update(grad, state[0:count, :], state[count : 2 * count, :], state[2 * count : 3 * count, :])

    def start_ys():
        for d in range(1, xs):
            p1b(d).wait_recv()
        total = pair_sum[x].astype(f32)
        for d in range(1, xs):
            total = total + p1b_recv[d - 1].astype(f32)
        sum_v[...] = total
        p2_send[...] = total.astype(bf16)
        for d in range(1, ys):
            p2(d).start()

    def start_zs():
        for d in range(1, ys):
            p2(d).wait_recv()
        total = sum_v[pl.ds(pl.multiple_of(y * shard_rows, 16), shard_rows), :]
        for d in range(1, ys):
            total = total + p2_recv[d - 1].astype(f32)
        p3_all[z] = total.astype(bf16)
        for d in range(1, zs):
            p3(d, False).start()

    def start_gather_ys():
        @pl.when(jnp.logical_not(reducer))
        def _():
            col(1).wait_recv()

        for d in range(1, zs):
            p3(d, True).wait_recv()
        grad = p3_all[0].astype(f32)
        for i in range(1, zs):
            grad = grad + p3_all[i].astype(f32)
        grad = grad / LOSS_SCALE
        weights = updated(grad, col_state)[2].astype(bf16)
        weights_v[pl.ds(pl.multiple_of(s * block_rows + y * shard_rows, 16), shard_rows), :] = weights
        for d in range(1, ys):
            b2(d, False).start()

        @pl.when(reducer)
        def _():
            grad_shard[...] = grad
            for d in range(1, ss):
                share(d).start()

    def start_gather_slabs():
        for d in range(1, ys):
            b2(d, True).wait_recv()
        for d in range(1, xs):
            b3x(d, False).start()
        b3c(0, False).start()

    def start_window_ys():
        for d in range(1, ss):
            w1(d).wait_recv()
        total = win_send[pl.ds(pl.multiple_of(s * win_part, 16), win_part), :].astype(f32)
        for d in range(1, ss):
            total = total + win_recv[d - 1].astype(f32)
        wy_all[y] = total.astype(bf16)
        for d in range(1, ys):
            wy(d, False).start()

    def start_window_zs():
        for d in range(1, ys):
            wy(d, True).wait_recv()
        total = wy_all[0].astype(f32)
        for i in range(1, ys):
            total = total + wy_all[i].astype(f32)
        wz_all[z] = total.astype(bf16)
        for d in range(1, zs):
            wz(d, False).start()

    in_window = (z == 0) & (y < WIN // shard_rows)
    win_owner = (z == 0) & (y == win_y)

    def start_window_gather():
        for d in range(1, zs):
            wz(d, True).wait_recv()
        grad = wz_all[0].astype(f32)
        for i in range(1, zs):
            grad = grad + wz_all[i].astype(f32)
        grad = grad / LOSS_SCALE
        weights = updated(grad, win_state)[2].astype(bf16)
        win_weights[pl.ds(pl.multiple_of(s * win_part, 16), win_part), :] = weights
        for d in range(1, ss):
            wb(d, False).start()

        @pl.when(win_owner)
        def _():
            win_grad[s % per_shard] = grad
            for d in range(1, ss):
                wshare(d).start()

    def finish_window():
        for d in range(1, ss):
            wb(d, True).wait_recv()

    def own_update():
        @pl.when(jnp.logical_not(reducer))
        def _():
            share(1).wait_recv()

        own_grad[...] = grad_shard[...]

        @pl.when(in_window)
        def _():
            for i in range(per_shard):
                @pl.when(s != y * per_shard + i)
                def _():
                    wshare_in(i).wait_recv()

                own_grad[i * win_part : (i + 1) * win_part, :] = win_grad[i]

        for i, value in enumerate(updated(own_grad[...], own_state)):
            shards_v[i] = value

    outs = [pltpu.make_async_copy(igrad_v, igrad_out, out_sem.at[0])]
    outs += [
        pltpu.make_async_copy(shards_v.at[i], ref, out_sem.at[1 + i]) for i, ref in enumerate((nmom_out, nsec_out, nmas_out))
    ]
    outs += [pltpu.make_async_copy(weights_v, weights_out, out_sem.at[4])]

    mask = ((lane < rows) & (shift >= -1) & (shift <= 1)) | ((lane >= rows) & (lane < rows + 8) & (shift == 0))
    mask = [mask[:, :LANES], mask[:, LANES:]]
    for a in range(3):
        grad_v[a] = dot_nt(dpre_v[:, LANES : LANES + cells], feat_v[:, LANES * a : LANES * a + cells])
    for i in range(9, 13):
        copies[i].wait()

    def rolled(v, by):
        return jnp.concatenate(
            [pltpu.roll(v[8 * o : 8 * o + 8], by, 1, stride=1, stride_axis=0) for o in range(v.shape[0] // 8)], axis=0
        )

    for pair in range(5):
        for t in range(2):
            total = None
            for slot in range(2):
                if pair * 2 + slot < 9:
                    a, c = divmod(pair * 2 + slot, 3)
                    part = grad_v[a, rows * c : rows * (c + 1), LANES * t : LANES * (t + 1)]
                    part = rolled(jnp.where(mask[t], part, 0.0), 3 * slot)
                    total = part if total is None else total + part
            at_lane = pair * 256 + t * LANES
            packed_v[:, at_lane : at_lane + LANES] = total.astype(bf16)
    sums = dot(add_ref[0:ch, 0:rows], packed_v[...])
    ordered = dot(sums.astype(bf16), order_ref[...])
    lane8 = iota((8, LANES), 1)
    row8 = iota((8, LANES), 0)
    zero8 = jnp.zeros((8, LANES), f32)
    for t in range(ch // 8):
        whole, base = divmod(64 * t, LANES)
        by = base + 8 * row8
        tiles = []
        for k in range(6):
            piece = ordered[8 * t : 8 * t + 8, LANES * k : LANES * (k + 1)]
            if k == 5:
                piece = jnp.where(lane8 < 8, piece, 0.0)
            tiles.append(pltpu.roll(piece, base, 1, stride=8, stride_axis=0))
        for m in range(7):
            k = m - whole
            high = tiles[k] if 0 <= k < 6 else zero8
            low = tiles[k - 1] if 0 <= k - 1 < 6 else zero8
            stack_v[m * ch + 8 * t : m * ch + 8 * t + 8, :] = jnp.where(lane8 >= by, high, low)
        bgrad = jnp.broadcast_to(ordered[8 * t : 8 * t + 8, 27 * ch : 27 * ch + 1], (8, LANES))
        stack_v[7 * ch + 8 * t : 7 * ch + 8 * t + 8, :] = jnp.where(lane8 == 64 + 8 * t + row8, bgrad, 0.0)

    hgrad = dot_nt(act_v[...], cot_v[...])
    row_h = iota((rows + 16, LANES), 0)
    lane_h = iota((rows + 16, LANES), 1)
    hgrad = rolled(jnp.where(lane_h % 8 == 7 - row_h % 8, hgrad, 0.0), 0).astype(bf16)
    hgrad = dot(dot(add_ref[...], hgrad).astype(bf16), emb_order_ref[...])
    for t in range(4):
        piece = pltpu.roll(hgrad[8 * t : 8 * t + 8], 0, 1, stride=16, stride_axis=0)
        stack_v[192 + 8 * t : 200 + 8 * t, :] = jnp.where(lane8 >= 88, piece, 0.0)
        stack_v[224 + 8 * t : 232 + 8 * t, :] = jnp.where(lane8 < 88, piece, 0.0)
    window = dot(place_ref[...], stack_v[...].astype(bf16)) + flat_b[0:WIN, :].astype(f32)
    win_send[...] = window.astype(bf16)
    for d in range(1, ss):
        w1(d).start()

    start_ys()
    @pl.when((z == 0) & (y != win_y))
    def _():
        ws_y(1).wait_recv()
        for d in range(1, zs):
            ws_z(d).start()

    wait_halo(dh_send, dh_recv, dh_ssem, dh_rsem)
    spread_dpre(dh_recv[0].astype(f32), 0)
    spread_dpre(dh_recv[1].astype(f32), planes + 1)

    total = None
    for a in range(3):
        part = dot_tn(wband[a, :, 0:rows], dpre_v[:, LANES * (2 - a) : LANES * (2 - a) + cells])
        total = part if total is None else total + part
    for p in range(planes):
        igrad_v[:, p] = total[:, LANES * p : LANES * (p + 1)].reshape(ch, 8, LANES).astype(bf16)
    outs[0].start()

    start_window_ys()
    start_zs()

    start_window_zs()
    start_gather_ys()
    @pl.when(z != 0)
    def _():
        ws_z(1).wait_recv()

    start_window_gather()
    start_gather_slabs()
    own_update()
    for out in outs[1:4]:
        out.start()
    finish_window()
    nearest = sorted(range(1, xs), key=lambda d: min(d, xs - d))
    for d in nearest:
        b3x(d, True).wait_recv()
        b3c(d, False).start()
    for d in [0] + nearest:
        b3c(d, True).wait_recv()
    for d in range(xs):
        b3c(d, False).wait_send()
    for d in range(1, xs):
        b3x(d, False).wait_send()
    for d in range(1, ys):
        b2(d, False).wait_send()
    weights_v[0:WIN, :] = win_weights[...]
    outs[4].start()

    for d in range(1, ss):
        w1(d).wait_send()
        wb(d, False).wait_send()
    for i in range(xs):
        p1a(i).wait_send()
    for d in range(1, xs):
        p1b(d).wait_send()
    for d in range(1, ys):
        p2(d).wait_send()
        wy(d, False).wait_send()
    for d in range(1, zs):
        p3(d, False).wait_send()
        wz(d, False).wait_send()

    @pl.when(reducer)
    def _():
        for d in range(1, zs):
            col(d).wait_send()
        for d in range(1, ss):
            share(d).wait_send()

    @pl.when(win_source)
    def _():
        for d in range(1, ys):
            ws_y(d).wait_send()

    @pl.when(z == 0)
    def _():
        for d in range(1, zs):
            ws_z(d).wait_send()

    @pl.when(win_owner)
    def _():
        for d in range(1, ss):
            wshare(d).wait_send()

    for out in outs:
        out.wait()


def copy_kernel(*refs):
    count = (len(refs) - 2) // 3
    in_sem, out_sem = refs[3 * count :]
    loads = [pltpu.make_async_copy(refs[i], refs[2 * count + i], in_sem.at[i]) for i in range(count)]
    stores = [pltpu.make_async_copy(refs[2 * count + i], refs[count + i], out_sem.at[i]) for i in range(count)]
    for load in loads:
        load.start()
    for load, store in zip(loads, stores):
        load.wait()
        store.start()
    for store in stores:
        store.wait()


def on_device(
    features, cotangent, conv_weight, conv_bias, head_weight, grad_rest, master, moment, second
):
    ss = lax.axis_size("slab")
    zs = ss
    ys = lax.axis_size("rep") // zs
    ch, planes = features.shape[1], features.shape[2]
    emb = cotangent.shape[1]
    rows = 8 * ch
    cells = planes * LANES
    shard_rows = master.shape[0] // LANES
    block_rows = ys * shard_rows
    all_rows = ss * block_rows
    win_part = WIN // ss
    rest = grad_rest.shape[2]
    sizes = (zs, ys, ss, shard_rows, planes, ch, emb)
    tables = selection_tables(ch, emb)
    hbm = pl.BlockSpec(memory_space=pltpu.HBM)
    dma = pltpu.SemaphoreType.DMA
    shard = jax.ShapeDtypeStruct((shard_rows, LANES), f32)
    outs = pl.pallas_call(
        functools.partial(kernel, sizes),
        out_shape=(
            jax.ShapeDtypeStruct(features.shape[1:], bf16),
            shard,
            shard,
            shard,
            jax.ShapeDtypeStruct((all_rows, LANES), bf16),
        ),
        in_specs=[hbm] * 16,
        out_specs=(hbm,) * 5,
        scratch_shapes=[
            pltpu.VMEM(features.shape[1:], bf16),
            pltpu.VMEM(cotangent.shape[1:], bf16),
            pltpu.VMEM((27, ch, ch), bf16),
            pltpu.VMEM((1, ch), f32),
            pltpu.VMEM((emb, ch), bf16),
            pltpu.VMEM((1, rest), f32),
            pltpu.VMEM((3 * shard_rows, LANES), f32),
            *[pltpu.VMEM(t.shape, bf16) for t in tables],
            pltpu.VMEM(features.shape[1:], bf16),
            pltpu.VMEM((3, shard_rows, LANES), f32),
            pltpu.VMEM((all_rows, LANES), bf16),
            pltpu.VMEM((all_rows, LANES), bf16),
            pltpu.VMEM((256, cells + 2 * LANES), bf16),
            pltpu.VMEM((8 * emb, cells), bf16),
            pltpu.VMEM((3, 3 * rows, 256), bf16),
            pltpu.VMEM((rows, LANES), bf16),
            pltpu.VMEM((3 * rows, cells), f32),
            pltpu.VMEM((rows + 16, cells), bf16),
            pltpu.VMEM((3 * rows, cells + 2 * LANES), bf16),
            pltpu.VMEM((3, 3 * rows, 256), f32),
            pltpu.VMEM((rows, 5 * 256), bf16),
            pltpu.VMEM((256, LANES), f32),
            pltpu.VMEM((2, rows, LANES), bf16),
            pltpu.VMEM((2, rows, LANES), bf16),
            pltpu.VMEM((2, rows, LANES), bf16),
            pltpu.VMEM((2, rows, LANES), bf16),
            pltpu.VMEM((ss // 2, block_rows, LANES), bf16),
            pltpu.VMEM((ss // 2, block_rows, LANES), bf16),
            pltpu.VMEM((max(ss // 2 - 1, 1), block_rows, LANES), bf16),
            pltpu.VMEM((block_rows, LANES), f32),
            pltpu.VMEM((block_rows, LANES), bf16),
            pltpu.VMEM((ys - 1, shard_rows, LANES), bf16),
            pltpu.VMEM((zs, shard_rows, LANES), bf16),
            pltpu.VMEM((3 * shard_rows, LANES), f32),
            pltpu.VMEM((shard_rows, LANES), f32),
            pltpu.VMEM((shard_rows, LANES), f32),
            pltpu.VMEM((WIN, LANES), bf16),
            pltpu.VMEM((ss - 1, win_part, LANES), bf16),
            pltpu.VMEM((ys, win_part, LANES), bf16),
            pltpu.VMEM((zs, win_part, LANES), bf16),
            pltpu.VMEM((3 * win_part, LANES), f32),
            pltpu.VMEM((shard_rows // win_part, win_part, LANES), f32),
            pltpu.VMEM((WIN, LANES), bf16),
            dma((16,)), dma((5,)),
            dma((2,)), dma((2,)), dma((2,)), dma((2,)),
            dma((ss // 2,)), dma((ss // 2,)),
            dma((max(ss // 2 - 1, 1),)), dma((max(ss // 2 - 1, 1),)),
            dma((ys - 1,)), dma((ys - 1,)),
            dma((zs - 1,)), dma((zs - 1,)),
            dma((zs - 1,)), dma,
            dma((ss - 1,)), dma,
            dma((ys - 1,)), dma((ys - 1,)),
            dma((max(ss // 2 - 1, 1),)), dma((max(ss // 2 - 1, 1),)),
            dma((ss // 2,)), dma((ss // 2,)),
            dma((ss - 1,)), dma((ss - 1,)),
            dma((ys - 1,)), dma((ys - 1,)),
            dma((zs - 1,)), dma((zs - 1,)),
            dma((ss - 1,)), dma((ss - 1,)),
            dma((ys - 1,)), dma((zs - 1,)), dma,
            dma((ss - 1,)), dma((shard_rows // win_part,)),
        ],
        compiler_params=pltpu.CompilerParams(
            collective_id=0, has_side_effects=True, vmem_limit_bytes=60 << 20
        ),
    )(
        features[0],
        cotangent[0],
        conv_weight.transpose(2, 3, 4, 0, 1).reshape(27, ch, ch),
        conv_bias.reshape(1, ch),
        head_weight.T,
        grad_rest,
        master.reshape(shard_rows, LANES),
        moment.reshape(shard_rows, LANES),
        second.reshape(shard_rows, LANES),
        *tables,
    )
    igrad, new_moment, new_second, new_master, weights = pl.pallas_call(
        copy_kernel,
        out_shape=tuple(jax.ShapeDtypeStruct(out.shape, out.dtype) for out in outs),
        in_specs=[pl.BlockSpec(memory_space=pl.ANY)] * 5,
        out_specs=(pl.BlockSpec(memory_space=pl.ANY),) * 5,
        scratch_shapes=[pltpu.VMEM(out.shape, out.dtype) for out in outs] + [dma((5,)), dma((5,))],
        compiler_params=pltpu.CompilerParams(vmem_limit_bytes=60 << 20),
    )(*outs)
    return (
        igrad[None],
        new_moment.reshape(-1),
        new_second.reshape(-1),
        new_master.reshape(-1),
        weights.reshape(-1),
    )


def solution(mesh):
    return jax.shard_map(
        on_device,
        mesh=mesh,
        in_specs=(
            P("rep", None, "slab", None, None),
            P("rep", None, "slab", None, None),
            P(),
            P(),
            P(),
            P("rep", "slab", None),
            P("rep"),
            P("rep"),
            P("rep"),
        ),
        out_specs=(P("rep", None, "slab", None, None), P("rep"), P("rep"), P("rep"), P()),
        check_vma=False,
    )
```

```python
import functools

import jax
import jax.numpy as jnp
import numpy as np
from jax import lax
from jax.experimental import pallas as pl
from jax.experimental.pallas import tpu as pltpu
from jax.sharding import PartitionSpec as P

LOSS_SCALE = 2048

beta_one = 0.9
beta_two = 0.99
learn_rate = 0.01
adam_eps = 1e-08
step_count = 10.0

f32 = jnp.float32
bf16 = jnp.bfloat16
MESH = pl.DeviceIdType.MESH
LANES = 128
CONV_ROWS = 124
CONV_LANES = 104
WIN = 128


def adam_update(grad, moment, second, master):
    new_moment = beta_one * moment + (1.0 - beta_one) * grad
    new_second = beta_two * second + (1.0 - beta_two) * grad * grad
    update = (
        new_moment
        / (1.0 - beta_one**step_count)
        / (jnp.sqrt(new_second / (1.0 - beta_two**step_count)) + adam_eps)
    )
    return (new_moment, new_second, master - learn_rate * update)


def selection_tables(ch, emb):
    rows = 8 * ch
    repeat_rows = np.zeros((rows, ch), np.float32)
    repeat_rows[np.arange(rows), np.arange(rows) // 8] = 1
    repeat_lanes = np.zeros((ch, 256), np.float32)
    repeat_lanes[np.arange(rows) // 8, np.arange(rows)] = 1
    repeat_emb = np.zeros((emb, 128), np.float32)
    repeat_emb[np.arange(128) // 8, np.arange(128)] = 1
    add_rows = np.zeros((32, rows + 16), np.float32)
    for i in range(ch + 1):
        add_rows[i, 8 * i : 8 * i + 8] = 1
    order = np.zeros((5 * 256, 768), np.float32)
    for a in range(3):
        for c in range(3):
            pair, slot = divmod(a * 3 + c, 2)
            for i in range(ch):
                tile, local = divmod(i, 16)
                for b in range(3):
                    lane = (8 * local + 6 + b + 3 * slot) % 128
                    order[pair * 256 + tile * 128 + lane, i * 27 + a * 9 + b * 3 + c] = 1
    order[2 * 256 + 128 + 8 * 8 + 7, ch * 27] = 1
    emb_order = np.zeros((128, 128), np.float32)
    for e in range(emb):
        emb_order[8 * e + 7, 88 + e] = 1
    place = np.zeros((WIN, 256), np.float32)
    for o in range(ch):
        for k in range(7):
            place[5 * o + k, k * ch + o] = 1
        place[121, 7 * ch + o] = 1
    for i in range(ch + 1):
        place[121 + i // 8, 192 + i] = 1
        place[122 + i // 8, 224 + i] = 1
    tables = (repeat_rows, repeat_lanes, repeat_emb, add_rows, order, emb_order, place)
    return tuple(jnp.asarray(t, bf16) for t in tables)


def far_first(count):
    return sorted(range(1, count), key=lambda d: -min(d, count - d))


def dot(lhs, rhs):
    return jnp.dot(lhs, rhs, preferred_element_type=f32)


def dot_nt(lhs, rhs):
    return lax.dot_general(lhs, rhs, (((1,), (1,)), ((), ())), preferred_element_type=f32)


def dot_tn(lhs, rhs):
    return lax.dot_general(lhs, rhs, (((0,), (0,)), ((), ())), preferred_element_type=f32)


def iota(shape, dim):
    return lax.broadcasted_iota(jnp.int32, shape, dim)


def kernel(
    sizes,
    feat_in, cot_in, w_in, bias_in, headt_in, rest_in, master_in, moment_in, second_in,
    rep_rows_in, rep_lanes_in, rep_emb_in, add_in, order_in, emb_order_in, place_in,
    igrad_out, nmom_out, nsec_out, nmas_out, weights_out,
    feat_ref, cot_ref, w_ref, bias_ref, headt_ref, rest_1d, own_state,
    rep_rows_ref, rep_lanes_ref, rep_emb_ref, add_ref, order_ref, emb_order_ref, place_ref,
    igrad_v, shards_v, weights_v,
    flat_b, feat_v, cot_v, wband, hband, conv_v, act_v, dpre_v, grad_v, packed_v, stack_v,
    fh_send, fh_recv, dh_send, dh_recv,
    p1a_recv, pair_sum, p1b_recv, sum_v, p2_send, p2_recv, p3_all, col_state, grad_shard, own_grad,
    win_send, win_recv, wy_all, wz_all, win_state, win_grad, win_weights,
    local_sem, out_sem, fh_ssem, fh_rsem, dh_ssem, dh_rsem,
    p1a_ssem, p1a_rsem, p1b_ssem, p1b_rsem, p2_ssem, p2_rsem, p3_ssem, p3_rsem,
    col_ssem, col_rsem, share_ssem, share_rsem, b2_ssem, b2_rsem, b3x_ssem, b3x_rsem, b3c_ssem, b3c_rsem,
    w1_ssem, w1_rsem, wy_ssem, wy_rsem, wz_ssem, wz_rsem, wb_ssem, wb_rsem,
    ws_y_ssem, ws_z_ssem, ws_rsem, wshare_ssem, wshare_rsem,
):
    zs, ys, ss, shard_rows, planes, ch, emb = sizes
    rows = 8 * ch
    cells = planes * LANES
    block_rows = ys * shard_rows
    rep = lax.axis_index("rep")
    s = lax.axis_index("slab")
    z = rep // ys
    y = rep % ys

    def at(zz, yy, sl):
        return (zz * ys + yy, sl)

    def remote(src, dst, ssem, rsem, device):
        return pltpu.make_async_remote_copy(
            src_ref=src, dst_ref=dst, send_sem=ssem, recv_sem=rsem, device_id=device, device_id_type=MESH
        )

    barrier = pltpu.get_barrier_semaphore()
    for d in far_first(max(ys, zs, ss)):
        if d < zs:
            pl.semaphore_signal(barrier, inc=1, device_id=at((z + d) % zs, y, s), device_id_type=MESH)
        if d < ys:
            pl.semaphore_signal(barrier, inc=1, device_id=at(z, (y + d) % ys, s), device_id_type=MESH)
        if d < ss:
            pl.semaphore_signal(barrier, inc=1, device_id=at(z, y, (s + d) % ss), device_id_type=MESH)

    ins = (
        (feat_in, feat_ref), (w_in, w_ref), (rep_lanes_in, rep_lanes_ref), (rep_rows_in, rep_rows_ref),
        (rest_in.at[0], rest_1d), (headt_in, headt_ref), (rep_emb_in, rep_emb_ref), (bias_in, bias_ref),
        (cot_in, cot_ref), (order_in, order_ref), (add_in, add_ref), (emb_order_in, emb_order_ref),
        (place_in, place_ref),
        *[(ref, own_state.at[pl.ds(i * shard_rows, shard_rows)]) for i, ref in enumerate((moment_in, second_in, master_in))],
    )
    copies = [pltpu.make_async_copy(src, dst, local_sem.at[i]) for i, (src, dst) in enumerate(ins)]
    for copy in copies:
        copy.start()

    copies[4].wait()
    first, last = CONV_ROWS // 16, flat_b.shape[0] // 16 - 1
    flat_b[0 : 16 * first, :] = jnp.zeros((16 * first, LANES), bf16)
    lane16 = iota((16, LANES), 1)

    def moved(here, later):
        return pltpu.roll(jnp.where(lane16 >= LANES - CONV_LANES, here, later), CONV_LANES, 1).astype(bf16)

    def rest_rows(start, count):
        return rest_1d[0:1, pl.ds(start, count * LANES)].reshape(count, LANES)

    lane8 = iota((8, LANES), 1)

    def moved8(here, later):
        return pltpu.roll(jnp.where(lane8 >= LANES - CONV_LANES, here, later), CONV_LANES, 1)

    per_step = 8
    skipped = (16 * (first + 1) - CONV_ROWS - 1) * LANES

    def align_at(at_row):
        halves = []
        for h in range(2):
            start = (at_row + 8 * h) * LANES + skipped
            halves.append(moved8(rest_rows(start, 8), rest_rows(start + LANES, 8)))
        part = jnp.concatenate(halves, axis=0).astype(bf16)
        flat_b[pl.ds(at_row + 16 * (first + 1), 16), :] = part

    def align(j, carry):
        for i in range(per_step):
            align_at(pl.multiple_of(j * (16 * per_step), 16 * per_step) + 16 * i)
        return carry

    steps = (last - first - 1) // per_step
    lax.fori_loop(0, steps, align, 0)
    for j in range(steps * per_step, last - first - 1):
        align_at(16 * j)
    lead = CONV_ROWS - 16 * first
    start_rows = rest_rows(0, 8)
    flat_b[16 * first : 16 * first + 16, :] = moved(
        jnp.concatenate([jnp.zeros((lead + 1, LANES), f32), start_rows[0 : 15 - lead]], axis=0),
        jnp.concatenate([jnp.zeros((lead, LANES), f32), start_rows[0 : 16 - lead]], axis=0),
    )
    end_row = 16 * last - CONV_ROWS - 1
    end = rest_1d[0:1, (end_row + 16) * LANES :]
    end = jnp.concatenate([end, jnp.zeros((1, LANES - end.shape[1]), f32)], axis=1)
    end_rows = rest_rows(end_row * LANES, 16)
    flat_b[16 * last : 16 * last + 16, :] = moved(end_rows, jnp.concatenate([end_rows[1:16], end], axis=0))

    pl.semaphore_wait(barrier, (ss - 1) + (ys - 1) + (zs - 1))

    xs = ss // 2
    x = s // 2
    core = s % 2

    def block(ref, xx, cc):
        return ref.at[pl.ds(pl.multiple_of((xx * 2 + cc) * block_rows, 16), block_rows)]

    def p1a(i):
        return remote(
            block(flat_b, i, 1 - core), p1a_recv.at[i], p1a_ssem.at[i], p1a_rsem.at[i], at(z, y, x * 2 + 1 - core)
        )

    def p1b(d):
        to = (x + d) % xs
        return remote(
            pair_sum.at[to], p1b_recv.at[d - 1], p1b_ssem.at[d - 1], p1b_rsem.at[d - 1], at(z, y, to * 2 + core)
        )

    order = [(x + d) % xs for d in far_first(xs) + [0]]
    for i in order:
        p1a(i).start()

    copies[0].wait()
    for p in range(planes):
        plane = feat_ref[:, p].astype(f32).reshape(rows, LANES).astype(bf16)
        feat_v[0:rows, LANES * (p + 1) : LANES * (p + 2)] = plane
        if p == 0:
            fh_send[0] = plane
        if p == planes - 1:
            fh_send[1] = plane
    feat_v[rows : rows + 16, :] = jnp.ones((16, cells + 2 * LANES), bf16)
    feat_v[rows + 16 : 256, :] = jnp.zeros((256 - rows - 16, cells + 2 * LANES), bf16)

    def halo(send, recv, ssem, rsem, up):
        source, slot = (1, 0) if up else (0, 1)
        other = (s + 1) % ss if up else (s + ss - 1) % ss
        return remote(send.at[source], recv.at[slot], ssem.at[source], rsem.at[slot], at(z, y, other))

    def start_halo(send, recv, ssem, rsem):
        @pl.when(s < ss - 1)
        def _():
            halo(send, recv, ssem, rsem, True).start()

        @pl.when(s > 0)
        def _():
            halo(send, recv, ssem, rsem, False).start()

        @pl.when(s == 0)
        def _():
            recv[0] = jnp.zeros((rows, LANES), bf16)

        @pl.when(s == ss - 1)
        def _():
            recv[1] = jnp.zeros((rows, LANES), bf16)

    def wait_halo(send, recv, ssem, rsem):
        @pl.when(s < ss - 1)
        def _():
            halo(send, recv, ssem, rsem, True).wait_send()
            halo(send, recv, ssem, rsem, False).wait_recv()

        @pl.when(s > 0)
        def _():
            halo(send, recv, ssem, rsem, False).wait_send()
            halo(send, recv, ssem, rsem, True).wait_recv()

    start_halo(fh_send, fh_recv, fh_ssem, fh_rsem)

    for d in far_first(xs) + [0]:
        to = (x + d) % xs
        p1a(to).wait_recv()
        own = flat_b[pl.ds(pl.multiple_of((to * 2 + core) * block_rows, 16), block_rows), :].astype(f32)
        pair_sum[to] = (own + p1a_recv[to].astype(f32)).astype(bf16)
        if d:
            p1b(d).start()

    for i in (13, 14, 15):
        copies[i].wait()
    reducer = z == s
    win_part = WIN // ss
    win_y = (s * win_part) // shard_rows
    win_row = (s * win_part) % shard_rows
    win_source = (z == 0) & (y == win_y)

    def col(d):
        return remote(own_state, col_state, col_ssem.at[d - 1], col_rsem, at((z + d) % zs, y, s))

    def ws_y(d):
        return remote(win_state, win_state, ws_y_ssem.at[d - 1], ws_rsem, at(z, (y + d) % ys, s))

    def ws_z(d):
        return remote(win_state, win_state, ws_z_ssem.at[d - 1], ws_rsem, at((z + d) % zs, y, s))

    @pl.when(reducer)
    def _():
        for d in far_first(zs):
            col(d).start()
        col_state[...] = own_state[...]

    @pl.when(win_source)
    def _():
        for i in range(3):
            win_state[i * win_part : (i + 1) * win_part, :] = own_state[
                pl.ds(pl.multiple_of(i * shard_rows + win_row, 16), win_part), :
            ]
        for d in far_first(ys):
            ws_y(d).start()
        for d in far_first(zs):
            ws_z(d).start()

    row = iota((rows, 256), 0)
    lane = iota((rows, 256), 1)
    shift = (lane % 8) - (7 - row % 8)
    for i in (1, 2, 3, 5, 6, 7, 8):
        copies[i].wait()
    for p in range(planes):
        cot_v[:, LANES * p : LANES * (p + 1)] = cot_ref[:, p].astype(f32).reshape(8 * emb, LANES).astype(bf16)
    spread = dot(w_ref[...].astype(f32).reshape(27 * ch, ch).astype(bf16), rep_lanes_ref[...])
    for a in range(3):
        for c in range(3):
            band = jnp.zeros((rows, 256), f32)
            for b in range(3):
                at_row = (a * 9 + b * 3 + c) * ch
                full = dot(rep_rows_ref[...], spread[at_row : at_row + ch].astype(bf16))
                band = jnp.where(shift == b - 1, full, band)
            wband[a, rows * c : rows * (c + 1), :] = band.astype(bf16)
    head = dot(dot_nt(rep_rows_ref[...], headt_ref[...]).astype(bf16), rep_emb_ref[...])
    hband[...] = jnp.where(shift[:, :LANES] == 0, head, 0.0).astype(bf16)
    bias_row = jnp.concatenate([bias_ref[...], jnp.zeros((1, LANES - ch), f32)], axis=1)
    row_l = iota((rows, LANES), 0)
    lane_l = iota((rows, LANES), 1)
    bias = jnp.sum(jnp.where(lane_l == row_l // 8, jnp.broadcast_to(bias_row, (rows, LANES)), 0.0), axis=1, keepdims=True)

    conv_v[...] = dot(wband[1], feat_v[:, LANES : LANES + cells])
    wait_halo(fh_send, fh_recv, fh_ssem, fh_rsem)
    feat_v[0:rows, 0:LANES] = fh_recv[0]
    feat_v[0:rows, LANES + cells : 2 * LANES + cells] = fh_recv[1]
    conv_v[...] += dot(wband[0], feat_v[:, 0:cells]) + dot(wband[2], feat_v[:, 2 * LANES : 2 * LANES + cells])

    def right(v):
        return jnp.where(lane_l == 0, 0.0, pltpu.roll(v, 1, 1))

    def left(v):
        return jnp.where(lane_l == LANES - 1, 0.0, pltpu.roll(v, LANES - 1, 1))

    def spread_dpre(dpre, p):
        at_lane = slice(LANES * p, LANES * (p + 1))
        dpre_v[0:rows, at_lane] = left(dpre).astype(bf16)
        dpre_v[rows : 2 * rows, at_lane] = dpre.astype(bf16)
        dpre_v[2 * rows : 3 * rows, at_lane] = right(dpre).astype(bf16)

    for p in (0, planes - 1) + tuple(range(1, planes - 1)):
        at_lane = slice(LANES * p, LANES * (p + 1))
        pre = (
            conv_v[rows : 2 * rows, at_lane]
            + right(conv_v[0:rows, at_lane])
            + left(conv_v[2 * rows : 3 * rows, at_lane])
            + bias
        )
        sigma = jax.nn.sigmoid(pre)
        act_v[0:rows, at_lane] = (pre * sigma).astype(bf16)
        dact = dot(hband[...], cot_v[:, at_lane])
        dpre = (dact * sigma * (1.0 + pre * (1.0 - sigma))).astype(bf16)
        if p == 0:
            dh_send[0] = dpre
        if p == planes - 1:
            dh_send[1] = dpre
        spread_dpre(dpre.astype(f32), p + 1)
        if p == planes - 1:
            start_halo(dh_send, dh_recv, dh_ssem, dh_rsem)
    act_v[rows : rows + 16, :] = jnp.ones((16, cells), bf16)

    def p2(d):
        other = (y + d) % ys
        return remote(
            p2_send.at[pl.ds(pl.multiple_of(other * shard_rows, 16), shard_rows)],
            p2_recv.at[d - 1], p2_ssem.at[d - 1], p2_rsem.at[d - 1], at(z, other, s),
        )

    def p3(d, back):
        part = p3_all.at[(z + zs - d) % zs if back else z]
        return remote(part, part, p3_ssem.at[d - 1], p3_rsem.at[d - 1], at((z + d) % zs, y, s))

    def share(d):
        return remote(grad_shard, grad_shard, share_ssem.at[d - 1], share_rsem, at(z, y, (s + d) % ss))

    def b2(d, back):
        owner = (y + ys - d) % ys if back else y
        part = weights_v.at[pl.ds(pl.multiple_of(s * block_rows + owner * shard_rows, 16), shard_rows)]
        return remote(part, part, b2_ssem.at[d - 1], b2_rsem.at[d - 1], at(z, (y + d) % ys, s))

    def b3x(d, back):
        part = block(weights_v, (x + xs - d) % xs if back else x, core)
        return remote(part, part, b3x_ssem.at[d - 1], b3x_rsem.at[d - 1], at(z, y, (x + d) % xs * 2 + core))

    def b3c(d, back):
        part = block(weights_v, (x + xs - d) % xs, 1 - core if back else core)
        return remote(part, part, b3c_ssem.at[d], b3c_rsem.at[d], at(z, y, x * 2 + 1 - core))

    def w1(d):
        part = win_send.at[pl.ds(pl.multiple_of((s + d) % ss * win_part, 16), win_part)]
        return remote(part, win_recv.at[d - 1], w1_ssem.at[d - 1], w1_rsem.at[d - 1], at(z, y, (s + d) % ss))

    def wy(d, back):
        part = wy_all.at[(y + ys - d) % ys if back else y]
        return remote(part, part, wy_ssem.at[d - 1], wy_rsem.at[d - 1], at(z, (y + d) % ys, s))

    def wz(d, back):
        part = wz_all.at[(z + zs - d) % zs if back else z]
        return remote(part, part, wz_ssem.at[d - 1], wz_rsem.at[d - 1], at((z + d) % zs, y, s))

    def wb(d, back):
        owner = (s + ss - d) % ss if back else s
        part = win_weights.at[pl.ds(pl.multiple_of(owner * win_part, 16), win_part)]
        return remote(part, part, wb_ssem.at[d - 1], wb_rsem.at[d - 1], at(z, y, (s + d) % ss))

    per_shard = shard_rows // win_part

    def wshare(d):
        part = win_grad.at[s % per_shard]
        return remote(part, part, wshare_ssem.at[d - 1], wshare_rsem.at[s % per_shard], at(z, y, (s + d) % ss))

    def wshare_in(i):
        part = win_grad.at[i]
        return remote(part, part, wshare_ssem.at[0], wshare_rsem.at[i], at(z, y, (s + 1) % ss))

    def updated(grad, state):
        count = grad.shape[0]
        return adam_update(grad, state[0:count, :], state[count : 2 * count, :], state[2 * count : 3 * count, :])

    def start_ys():
        for d in range(1, xs):
            p1b(d).wait_recv()
        total = pair_sum[x].astype(f32)
        for d in range(1, xs):
            total = total + p1b_recv[d - 1].astype(f32)
        sum_v[...] = total
        p2_send[...] = total.astype(bf16)
        for d in far_first(ys):
            p2(d).start()

    def start_zs():
        for d in range(1, ys):
            p2(d).wait_recv()
        total = sum_v[pl.ds(pl.multiple_of(y * shard_rows, 16), shard_rows), :]
        for d in range(1, ys):
            total = total + p2_recv[d - 1].astype(f32)
        p3_all[z] = total.astype(bf16)
        for d in far_first(zs):
            p3(d, False).start()

    def start_gather_ys():
        @pl.when(jnp.logical_not(reducer))
        def _():
            col(1).wait_recv()

        for d in range(1, zs):
            p3(d, True).wait_recv()
        grad = p3_all[0].astype(f32)
        for i in range(1, zs):
            grad = grad + p3_all[i].astype(f32)
        grad = grad / LOSS_SCALE
        weights = updated(grad, col_state)[2].astype(bf16)
        weights_v[pl.ds(pl.multiple_of(s * block_rows + y * shard_rows, 16), shard_rows), :] = weights
        for d in far_first(ys):
            b2(d, False).start()

        @pl.when(reducer)
        def _():
            grad_shard[...] = grad
            for d in range(1, ss):
                share(d).start()

    def start_gather_slabs():
        for d in range(1, ys):
            b2(d, True).wait_recv()
        for d in far_first(xs):
            b3x(d, False).start()
        b3c(0, False).start()

    def start_window_ys():
        for d in range(1, ss):
            w1(d).wait_recv()
        total = win_send[pl.ds(pl.multiple_of(s * win_part, 16), win_part), :].astype(f32)
        for d in range(1, ss):
            total = total + win_recv[d - 1].astype(f32)
        wy_all[y] = total.astype(bf16)
        for d in far_first(ys):
            wy(d, False).start()

    def start_window_zs():
        for d in range(1, ys):
            wy(d, True).wait_recv()
        total = wy_all[0].astype(f32)
        for i in range(1, ys):
            total = total + wy_all[i].astype(f32)
        wz_all[z] = total.astype(bf16)
        for d in far_first(zs):
            wz(d, False).start()

    in_window = (z == 0) & (y < WIN // shard_rows)
    win_owner = (z == 0) & (y == win_y)

    def start_window_gather():
        for d in range(1, zs):
            wz(d, True).wait_recv()
        grad = wz_all[0].astype(f32)
        for i in range(1, zs):
            grad = grad + wz_all[i].astype(f32)
        grad = grad / LOSS_SCALE
        weights = updated(grad, win_state)[2].astype(bf16)
        win_weights[pl.ds(pl.multiple_of(s * win_part, 16), win_part), :] = weights
        for d in range(1, ss):
            wb(d, False).start()

        @pl.when(win_owner)
        def _():
            win_grad[s % per_shard] = grad
            for d in range(1, ss):
                wshare(d).start()

    def finish_window():
        for d in range(1, ss):
            wb(d, True).wait_recv()

    def own_update():
        @pl.when(jnp.logical_not(reducer))
        def _():
            share(1).wait_recv()

        own_grad[...] = grad_shard[...]

        @pl.when(in_window)
        def _():
            for i in range(per_shard):
                @pl.when(s != y * per_shard + i)
                def _():
                    wshare_in(i).wait_recv()

                own_grad[i * win_part : (i + 1) * win_part, :] = win_grad[i]

        for i, value in enumerate(updated(own_grad[...], own_state)):
            shards_v[i] = value

    outs = [pltpu.make_async_copy(igrad_v, igrad_out, out_sem.at[0])]
    outs += [
        pltpu.make_async_copy(shards_v.at[i], ref, out_sem.at[1 + i]) for i, ref in enumerate((nmom_out, nsec_out, nmas_out))
    ]

    mask = ((lane < rows) & (shift >= -1) & (shift <= 1)) | ((lane >= rows) & (lane < rows + 8) & (shift == 0))
    mask = [mask[:, :LANES], mask[:, LANES:]]
    for a in range(3):
        grad_v[a] = dot_nt(dpre_v[:, LANES : LANES + cells], feat_v[:, LANES * a : LANES * a + cells])
    for i in range(9, 13):
        copies[i].wait()

    def rolled(v, by):
        return jnp.concatenate(
            [pltpu.roll(v[8 * o : 8 * o + 8], by, 1, stride=1, stride_axis=0) for o in range(v.shape[0] // 8)], axis=0
        )

    for pair in range(5):
        for t in range(2):
            total = None
            for slot in range(2):
                if pair * 2 + slot < 9:
                    a, c = divmod(pair * 2 + slot, 3)
                    part = grad_v[a, rows * c : rows * (c + 1), LANES * t : LANES * (t + 1)]
                    part = rolled(jnp.where(mask[t], part, 0.0), 3 * slot)
                    total = part if total is None else total + part
            at_lane = pair * 256 + t * LANES
            packed_v[:, at_lane : at_lane + LANES] = total.astype(bf16)
    sums = dot(add_ref[0:ch, 0:rows], packed_v[...])
    ordered = dot(sums.astype(bf16), order_ref[...])
    lane8 = iota((8, LANES), 1)
    row8 = iota((8, LANES), 0)
    zero8 = jnp.zeros((8, LANES), f32)
    for t in range(ch // 8):
        whole, base = divmod(64 * t, LANES)
        by = base + 8 * row8
        tiles = []
        for k in range(6):
            piece = ordered[8 * t : 8 * t + 8, LANES * k : LANES * (k + 1)]
            if k == 5:
                piece = jnp.where(lane8 < 8, piece, 0.0)
            tiles.append(pltpu.roll(piece, base, 1, stride=8, stride_axis=0))
        for m in range(7):
            k = m - whole
            high = tiles[k] if 0 <= k < 6 else zero8
            low = tiles[k - 1] if 0 <= k - 1 < 6 else zero8
            stack_v[m * ch + 8 * t : m * ch + 8 * t + 8, :] = jnp.where(lane8 >= by, high, low)
        bgrad = jnp.broadcast_to(ordered[8 * t : 8 * t + 8, 27 * ch : 27 * ch + 1], (8, LANES))
        stack_v[7 * ch + 8 * t : 7 * ch + 8 * t + 8, :] = jnp.where(lane8 == 64 + 8 * t + row8, bgrad, 0.0)

    hgrad = dot_nt(act_v[...], cot_v[...])
    row_h = iota((rows + 16, LANES), 0)
    lane_h = iota((rows + 16, LANES), 1)
    hgrad = rolled(jnp.where(lane_h % 8 == 7 - row_h % 8, hgrad, 0.0), 0).astype(bf16)
    hgrad = dot(dot(add_ref[...], hgrad).astype(bf16), emb_order_ref[...])
    for t in range(4):
        piece = pltpu.roll(hgrad[8 * t : 8 * t + 8], 0, 1, stride=16, stride_axis=0)
        stack_v[192 + 8 * t : 200 + 8 * t, :] = jnp.where(lane8 >= 88, piece, 0.0)
        stack_v[224 + 8 * t : 232 + 8 * t, :] = jnp.where(lane8 < 88, piece, 0.0)
    window = dot(place_ref[...], stack_v[...].astype(bf16)) + flat_b[0:WIN, :].astype(f32)
    win_send[...] = window.astype(bf16)
    for d in range(1, ss):
        w1(d).start()

    start_ys()
    @pl.when((z == 0) & (y != win_y))
    def _():
        ws_y(1).wait_recv()
        for d in far_first(zs):
            ws_z(d).start()

    wait_halo(dh_send, dh_recv, dh_ssem, dh_rsem)
    spread_dpre(dh_recv[0].astype(f32), 0)
    spread_dpre(dh_recv[1].astype(f32), planes + 1)

    total = None
    for a in range(3):
        part = dot_tn(wband[a, :, 0:rows], dpre_v[:, LANES * (2 - a) : LANES * (2 - a) + cells])
        total = part if total is None else total + part
    for p in range(planes):
        igrad_v[:, p] = total[:, LANES * p : LANES * (p + 1)].reshape(ch, 8, LANES).astype(bf16)
    outs[0].start()

    start_window_ys()
    start_zs()

    start_window_zs()
    start_gather_ys()
    @pl.when(z != 0)
    def _():
        ws_z(1).wait_recv()

    start_window_gather()
    start_gather_slabs()
    own_update()
    for out in outs[1:4]:
        out.start()
    finish_window()
    def out_block(xx, cc, sem):
        return pltpu.make_async_copy(block(weights_v, xx, cc), block(weights_out, xx, cc), out_sem.at[4 + sem])

    def write_block(xx, cc, sem):
        @pl.when((xx > 0) | (cc > 0))
        def _():
            out_block(xx, cc, sem).start()

    write_block(x, core, 0)
    nearest = sorted(range(1, xs), key=lambda d: min(d, xs - d))
    for d in nearest:
        b3x(d, True).wait_recv()
        b3c(d, False).start()
        write_block((x + xs - d) % xs, core, d)
    for d in [0] + nearest:
        b3c(d, True).wait_recv()
        write_block((x + xs - d) % xs, 1 - core, xs + d)
    for d in range(xs):
        b3c(d, False).wait_send()
    for d in range(1, xs):
        b3x(d, False).wait_send()
    for d in range(1, ys):
        b2(d, False).wait_send()
    weights_v[0:WIN, :] = win_weights[...]
    for d in range(xs):
        for cc in range(2):
            @pl.when(((x + xs - d) % xs == 0) & ((core if cc == 0 else 1 - core) == 0))
            def _():
                out_block(0, 0, cc * xs + d).start()

    for d in range(1, ss):
        w1(d).wait_send()
        wb(d, False).wait_send()
    for i in range(xs):
        p1a(i).wait_send()
    for d in range(1, xs):
        p1b(d).wait_send()
    for d in range(1, ys):
        p2(d).wait_send()
        wy(d, False).wait_send()
    for d in range(1, zs):
        p3(d, False).wait_send()
        wz(d, False).wait_send()

    @pl.when(reducer)
    def _():
        for d in range(1, zs):
            col(d).wait_send()
        for d in range(1, ss):
            share(d).wait_send()

    @pl.when(win_source)
    def _():
        for d in range(1, ys):
            ws_y(d).wait_send()

    @pl.when(z == 0)
    def _():
        for d in range(1, zs):
            ws_z(d).wait_send()

    @pl.when(win_owner)
    def _():
        for d in range(1, ss):
            wshare(d).wait_send()

    for out in outs:
        out.wait()
    for d in range(xs):
        for cc in range(2):
            out_block((x + xs - d) % xs, core if cc == 0 else 1 - core, cc * xs + d).wait()


def copy_kernel(*refs):
    count = (len(refs) - 2) // 3
    in_sem, out_sem = refs[3 * count :]
    ins, outs, held = refs[:count], refs[count : 2 * count], refs[2 * count : 3 * count]
    part = ins[-1].shape[0] // 4
    pieces = [(i, slice(None)) for i in range(count - 1)] + [(count - 1, pl.ds(part * j, part)) for j in range(4)]
    loads = [pltpu.make_async_copy(ins[i].at[p], held[i].at[p], in_sem.at[k]) for k, (i, p) in enumerate(pieces)]
    stores = [pltpu.make_async_copy(held[i].at[p], outs[i].at[p], out_sem.at[k]) for k, (i, p) in enumerate(pieces)]
    for load in loads:
        load.start()
    for load, store in zip(loads, stores):
        load.wait()
        store.start()
    for store in stores:
        store.wait()


def on_device(
    features, cotangent, conv_weight, conv_bias, head_weight, grad_rest, master, moment, second
):
    ss = lax.axis_size("slab")
    zs = ss
    ys = lax.axis_size("rep") // zs
    ch, planes = features.shape[1], features.shape[2]
    emb = cotangent.shape[1]
    rows = 8 * ch
    cells = planes * LANES
    shard_rows = master.shape[0] // LANES
    block_rows = ys * shard_rows
    all_rows = ss * block_rows
    win_part = WIN // ss
    rest = grad_rest.shape[2]
    sizes = (zs, ys, ss, shard_rows, planes, ch, emb)
    tables = selection_tables(ch, emb)
    hbm = pl.BlockSpec(memory_space=pltpu.HBM)
    dma = pltpu.SemaphoreType.DMA
    shard = jax.ShapeDtypeStruct((shard_rows, LANES), f32)
    outs = pl.pallas_call(
        functools.partial(kernel, sizes),
        out_shape=(
            jax.ShapeDtypeStruct(features.shape[1:], bf16),
            shard,
            shard,
            shard,
            jax.ShapeDtypeStruct((all_rows, LANES), bf16),
        ),
        in_specs=[hbm] * 16,
        out_specs=(hbm,) * 5,
        scratch_shapes=[
            pltpu.VMEM(features.shape[1:], bf16),
            pltpu.VMEM(cotangent.shape[1:], bf16),
            pltpu.VMEM((27, ch, ch), bf16),
            pltpu.VMEM((1, ch), f32),
            pltpu.VMEM((emb, ch), bf16),
            pltpu.VMEM((1, rest), f32),
            pltpu.VMEM((3 * shard_rows, LANES), f32),
            *[pltpu.VMEM(t.shape, bf16) for t in tables],
            pltpu.VMEM(features.shape[1:], bf16),
            pltpu.VMEM((3, shard_rows, LANES), f32),
            pltpu.VMEM((all_rows, LANES), bf16),
            pltpu.VMEM((all_rows, LANES), bf16),
            pltpu.VMEM((256, cells + 2 * LANES), bf16),
            pltpu.VMEM((8 * emb, cells), bf16),
            pltpu.VMEM((3, 3 * rows, 256), bf16),
            pltpu.VMEM((rows, LANES), bf16),
            pltpu.VMEM((3 * rows, cells), f32),
            pltpu.VMEM((rows + 16, cells), bf16),
            pltpu.VMEM((3 * rows, cells + 2 * LANES), bf16),
            pltpu.VMEM((3, 3 * rows, 256), f32),
            pltpu.VMEM((rows, 5 * 256), bf16),
            pltpu.VMEM((256, LANES), f32),
            pltpu.VMEM((2, rows, LANES), bf16),
            pltpu.VMEM((2, rows, LANES), bf16),
            pltpu.VMEM((2, rows, LANES), bf16),
            pltpu.VMEM((2, rows, LANES), bf16),
            pltpu.VMEM((ss // 2, block_rows, LANES), bf16),
            pltpu.VMEM((ss // 2, block_rows, LANES), bf16),
            pltpu.VMEM((max(ss // 2 - 1, 1), block_rows, LANES), bf16),
            pltpu.VMEM((block_rows, LANES), f32),
            pltpu.VMEM((block_rows, LANES), bf16),
            pltpu.VMEM((ys - 1, shard_rows, LANES), bf16),
            pltpu.VMEM((zs, shard_rows, LANES), bf16),
            pltpu.VMEM((3 * shard_rows, LANES), f32),
            pltpu.VMEM((shard_rows, LANES), f32),
            pltpu.VMEM((shard_rows, LANES), f32),
            pltpu.VMEM((WIN, LANES), bf16),
            pltpu.VMEM((ss - 1, win_part, LANES), bf16),
            pltpu.VMEM((ys, win_part, LANES), bf16),
            pltpu.VMEM((zs, win_part, LANES), bf16),
            pltpu.VMEM((3 * win_part, LANES), f32),
            pltpu.VMEM((shard_rows // win_part, win_part, LANES), f32),
            pltpu.VMEM((WIN, LANES), bf16),
            dma((16,)), dma((4 + ss,)),
            dma((2,)), dma((2,)), dma((2,)), dma((2,)),
            dma((ss // 2,)), dma((ss // 2,)),
            dma((max(ss // 2 - 1, 1),)), dma((max(ss // 2 - 1, 1),)),
            dma((ys - 1,)), dma((ys - 1,)),
            dma((zs - 1,)), dma((zs - 1,)),
            dma((zs - 1,)), dma,
            dma((ss - 1,)), dma,
            dma((ys - 1,)), dma((ys - 1,)),
            dma((max(ss // 2 - 1, 1),)), dma((max(ss // 2 - 1, 1),)),
            dma((ss // 2,)), dma((ss // 2,)),
            dma((ss - 1,)), dma((ss - 1,)),
            dma((ys - 1,)), dma((ys - 1,)),
            dma((zs - 1,)), dma((zs - 1,)),
            dma((ss - 1,)), dma((ss - 1,)),
            dma((ys - 1,)), dma((zs - 1,)), dma,
            dma((ss - 1,)), dma((shard_rows // win_part,)),
        ],
        compiler_params=pltpu.CompilerParams(
            collective_id=0, has_side_effects=True, vmem_limit_bytes=60 << 20
        ),
    )(
        features[0],
        cotangent[0],
        conv_weight.transpose(2, 3, 4, 0, 1).reshape(27, ch, ch),
        conv_bias.reshape(1, ch),
        head_weight.T,
        grad_rest,
        master.reshape(shard_rows, LANES),
        moment.reshape(shard_rows, LANES),
        second.reshape(shard_rows, LANES),
        *tables,
    )
    igrad, new_moment, new_second, new_master, weights = pl.pallas_call(
        copy_kernel,
        out_shape=tuple(jax.ShapeDtypeStruct(out.shape, out.dtype) for out in outs),
        in_specs=[pl.BlockSpec(memory_space=pl.ANY)] * 5,
        out_specs=(pl.BlockSpec(memory_space=pl.ANY),) * 5,
        scratch_shapes=[pltpu.VMEM(out.shape, out.dtype) for out in outs] + [dma((8,)), dma((8,))],
        compiler_params=pltpu.CompilerParams(vmem_limit_bytes=60 << 20),
    )(*outs)
    return (
        igrad[None],
        new_moment.reshape(-1),
        new_second.reshape(-1),
        new_master.reshape(-1),
        weights.reshape(-1),
    )


def solution(mesh):
    return jax.shard_map(
        on_device,
        mesh=mesh,
        in_specs=(
            P("rep", None, "slab", None, None),
            P("rep", None, "slab", None, None),
            P(),
            P(),
            P(),
            P("rep", "slab", None),
            P("rep"),
            P("rep"),
            P("rep"),
        ),
        out_specs=(P("rep", None, "slab", None, None), P("rep"), P("rep"), P("rep"), P()),
        check_vma=False,
    )
```

```python
import functools

import jax
import jax.numpy as jnp
import numpy as np
from jax import lax
from jax.experimental import pallas as pl
from jax.experimental.pallas import tpu as pltpu
from jax.sharding import PartitionSpec as P

LOSS_SCALE = 2048

beta_one = 0.9
beta_two = 0.99
learn_rate = 0.01
adam_eps = 1e-08
step_count = 10.0

f32 = jnp.float32
bf16 = jnp.bfloat16
MESH = pl.DeviceIdType.MESH
LANES = 128
CONV_ROWS = 124
CONV_LANES = 104
WIN = 128


def adam_update(grad, moment, second, master):
    new_moment = beta_one * moment + (1.0 - beta_one) * grad
    new_second = beta_two * second + (1.0 - beta_two) * grad * grad
    update = (
        new_moment
        / (1.0 - beta_one**step_count)
        / (jnp.sqrt(new_second / (1.0 - beta_two**step_count)) + adam_eps)
    )
    return (new_moment, new_second, master - learn_rate * update)


def selection_tables(ch, emb):
    rows = 8 * ch
    repeat_rows = np.zeros((rows, ch), np.float32)
    repeat_rows[np.arange(rows), np.arange(rows) // 8] = 1
    repeat_lanes = np.zeros((ch, 256), np.float32)
    repeat_lanes[np.arange(rows) // 8, np.arange(rows)] = 1
    repeat_emb = np.zeros((emb, 128), np.float32)
    repeat_emb[np.arange(128) // 8, np.arange(128)] = 1
    add_rows = np.zeros((32, rows + 16), np.float32)
    for i in range(ch + 1):
        add_rows[i, 8 * i : 8 * i + 8] = 1
    order = np.zeros((5 * 256, 768), np.float32)
    for a in range(3):
        for c in range(3):
            pair, slot = divmod(a * 3 + c, 2)
            for i in range(ch):
                tile, local = divmod(i, 16)
                for b in range(3):
                    lane = (8 * local + 6 + b + 3 * slot) % 128
                    order[pair * 256 + tile * 128 + lane, i * 27 + a * 9 + b * 3 + c] = 1
    order[2 * 256 + 128 + 8 * 8 + 7, ch * 27] = 1
    emb_order = np.zeros((128, 128), np.float32)
    for e in range(emb):
        emb_order[8 * e + 7, 88 + e] = 1
    place = np.zeros((WIN, 256), np.float32)
    for o in range(ch):
        for k in range(7):
            place[5 * o + k, k * ch + o] = 1
        place[121, 7 * ch + o] = 1
    for i in range(ch + 1):
        place[121 + i // 8, 192 + i] = 1
        place[122 + i // 8, 224 + i] = 1
    tables = (repeat_rows, repeat_lanes, repeat_emb, add_rows, order, emb_order, place)
    return tuple(jnp.asarray(t, bf16) for t in tables)


def far_first(count):
    return sorted(range(1, count), key=lambda d: -min(d, count - d))


def dot(lhs, rhs):
    return jnp.dot(lhs, rhs, preferred_element_type=f32)


def dot_nt(lhs, rhs):
    return lax.dot_general(lhs, rhs, (((1,), (1,)), ((), ())), preferred_element_type=f32)


def dot_tn(lhs, rhs):
    return lax.dot_general(lhs, rhs, (((0,), (0,)), ((), ())), preferred_element_type=f32)


def iota(shape, dim):
    return lax.broadcasted_iota(jnp.int32, shape, dim)


def kernel(
    sizes,
    feat_in, cot_in, w_in, bias_in, headt_in, rest_in, master_in, moment_in, second_in,
    rep_rows_in, rep_lanes_in, rep_emb_in, add_in, order_in, emb_order_in, place_in,
    igrad_out, nmom_out, nsec_out, nmas_out, weights_out,
    feat_ref, cot_ref, w_ref, bias_ref, headt_ref, rest_1d, own_state,
    rep_rows_ref, rep_lanes_ref, rep_emb_ref, add_ref, order_ref, emb_order_ref, place_ref,
    igrad_v, shards_v, weights_v, ordered_v,
    flat_b, feat_v, cot_v, wband, hband, conv_v, act_v, dpre_v, grad_v, packed_v, stack_v,
    fh_send, fh_recv, dh_send, dh_recv,
    p1a_recv, pair_sum, p1b_recv, sum_v, p2_send, p2_recv, p3_all, col_state, grad_shard, own_grad,
    win_send, win_recv, wy_all, wz_all, win_state, win_grad, win_weights,
    local_sem, out_sem, fh_ssem, fh_rsem, dh_ssem, dh_rsem,
    p1a_ssem, p1a_rsem, p1b_ssem, p1b_rsem, p2_ssem, p2_rsem, p3_ssem, p3_rsem,
    col_ssem, col_rsem, share_ssem, share_rsem, b2_ssem, b2_rsem, b3x_ssem, b3x_rsem, b3c_ssem, b3c_rsem,
    w1_ssem, w1_rsem, wy_ssem, wy_rsem, wz_ssem, wz_rsem, wb_ssem, wb_rsem,
    ws_y_ssem, ws_z_ssem, ws_rsem, wshare_ssem, wshare_rsem,
):
    zs, ys, ss, shard_rows, planes, ch, emb = sizes
    rows = 8 * ch
    cells = planes * LANES
    block_rows = ys * shard_rows
    rep = lax.axis_index("rep")
    s = lax.axis_index("slab")
    z = rep // ys
    y = rep % ys

    def at(zz, yy, sl):
        return (zz * ys + yy, sl)

    def remote(src, dst, ssem, rsem, device):
        return pltpu.make_async_remote_copy(
            src_ref=src, dst_ref=dst, send_sem=ssem, recv_sem=rsem, device_id=device, device_id_type=MESH
        )

    barrier = pltpu.get_barrier_semaphore()
    for d in far_first(max(ys, zs, ss)):
        if d < zs:
            pl.semaphore_signal(barrier, inc=1, device_id=at((z + d) % zs, y, s), device_id_type=MESH)
        if d < ys:
            pl.semaphore_signal(barrier, inc=1, device_id=at(z, (y + d) % ys, s), device_id_type=MESH)
        if d < ss:
            pl.semaphore_signal(barrier, inc=1, device_id=at(z, y, (s + d) % ss), device_id_type=MESH)

    ins = (
        (feat_in, feat_ref), (w_in, w_ref), (rep_lanes_in, rep_lanes_ref), (rep_rows_in, rep_rows_ref),
        (rest_in.at[0], rest_1d), (headt_in, headt_ref), (rep_emb_in, rep_emb_ref), (bias_in, bias_ref),
        (cot_in, cot_ref), (order_in, order_ref), (add_in, add_ref), (emb_order_in, emb_order_ref),
        (place_in, place_ref),
        *[(ref, own_state.at[pl.ds(i * shard_rows, shard_rows)]) for i, ref in enumerate((moment_in, second_in, master_in))],
    )
    copies = [pltpu.make_async_copy(src, dst, local_sem.at[i]) for i, (src, dst) in enumerate(ins)]
    for copy in copies:
        copy.start()

    copies[4].wait()
    first, last = CONV_ROWS // 16, flat_b.shape[0] // 16 - 1
    flat_b[0 : 16 * first, :] = jnp.zeros((16 * first, LANES), bf16)
    lane16 = iota((16, LANES), 1)

    def moved(here, later):
        return pltpu.roll(jnp.where(lane16 >= LANES - CONV_LANES, here, later), CONV_LANES, 1).astype(bf16)

    def rest_rows(start, count):
        return rest_1d[0:1, pl.ds(start, count * LANES)].reshape(count, LANES)

    lane8 = iota((8, LANES), 1)

    def moved8(here, later):
        return pltpu.roll(jnp.where(lane8 >= LANES - CONV_LANES, here, later), CONV_LANES, 1)

    per_step = 8
    skipped = (16 * (first + 1) - CONV_ROWS - 1) * LANES

    def align_at(at_row):
        halves = []
        for h in range(2):
            start = (at_row + 8 * h) * LANES + skipped
            halves.append(moved8(rest_rows(start, 8), rest_rows(start + LANES, 8)))
        part = jnp.concatenate(halves, axis=0).astype(bf16)
        flat_b[pl.ds(at_row + 16 * (first + 1), 16), :] = part

    def align(j, carry):
        for i in range(per_step):
            align_at(pl.multiple_of(j * (16 * per_step), 16 * per_step) + 16 * i)
        return carry

    steps = (last - first - 1) // per_step
    lax.fori_loop(0, steps, align, 0)
    for j in range(steps * per_step, last - first - 1):
        align_at(16 * j)
    lead = CONV_ROWS - 16 * first
    start_rows = rest_rows(0, 8)
    flat_b[16 * first : 16 * first + 16, :] = moved(
        jnp.concatenate([jnp.zeros((lead + 1, LANES), f32), start_rows[0 : 15 - lead]], axis=0),
        jnp.concatenate([jnp.zeros((lead, LANES), f32), start_rows[0 : 16 - lead]], axis=0),
    )
    end_row = 16 * last - CONV_ROWS - 1
    end = rest_1d[0:1, (end_row + 16) * LANES :]
    end = jnp.concatenate([end, jnp.zeros((1, LANES - end.shape[1]), f32)], axis=1)
    end_rows = rest_rows(end_row * LANES, 16)
    flat_b[16 * last : 16 * last + 16, :] = moved(end_rows, jnp.concatenate([end_rows[1:16], end], axis=0))

    pl.semaphore_wait(barrier, (ss - 1) + (ys - 1) + (zs - 1))

    xs = ss // 2
    x = s // 2
    core = s % 2

    def block(ref, xx, cc):
        return ref.at[pl.ds(pl.multiple_of((xx * 2 + cc) * block_rows, 16), block_rows)]

    def p1a(i):
        return remote(
            block(flat_b, i, 1 - core), p1a_recv.at[i], p1a_ssem.at[i], p1a_rsem.at[i], at(z, y, x * 2 + 1 - core)
        )

    def p1b(d):
        to = (x + d) % xs
        return remote(
            pair_sum.at[to], p1b_recv.at[d - 1], p1b_ssem.at[d - 1], p1b_rsem.at[d - 1], at(z, y, to * 2 + core)
        )

    order = [(x + d) % xs for d in far_first(xs) + [0]]
    for i in order:
        p1a(i).start()

    copies[0].wait()
    for p in range(planes):
        plane = feat_ref[:, p].astype(f32).reshape(rows, LANES).astype(bf16)
        feat_v[0:rows, LANES * (p + 1) : LANES * (p + 2)] = plane
        if p == 0:
            fh_send[0] = plane
        if p == planes - 1:
            fh_send[1] = plane
    feat_v[rows : rows + 16, :] = jnp.ones((16, cells + 2 * LANES), bf16)
    feat_v[rows + 16 : 256, :] = jnp.zeros((256 - rows - 16, cells + 2 * LANES), bf16)

    def halo(send, recv, ssem, rsem, up):
        source, slot = (1, 0) if up else (0, 1)
        other = (s + 1) % ss if up else (s + ss - 1) % ss
        return remote(send.at[source], recv.at[slot], ssem.at[source], rsem.at[slot], at(z, y, other))

    def start_halo(send, recv, ssem, rsem):
        @pl.when(s < ss - 1)
        def _():
            halo(send, recv, ssem, rsem, True).start()

        @pl.when(s > 0)
        def _():
            halo(send, recv, ssem, rsem, False).start()

        @pl.when(s == 0)
        def _():
            recv[0] = jnp.zeros((rows, LANES), bf16)

        @pl.when(s == ss - 1)
        def _():
            recv[1] = jnp.zeros((rows, LANES), bf16)

    def wait_halo(send, recv, ssem, rsem):
        @pl.when(s < ss - 1)
        def _():
            halo(send, recv, ssem, rsem, True).wait_send()
            halo(send, recv, ssem, rsem, False).wait_recv()

        @pl.when(s > 0)
        def _():
            halo(send, recv, ssem, rsem, False).wait_send()
            halo(send, recv, ssem, rsem, True).wait_recv()

    start_halo(fh_send, fh_recv, fh_ssem, fh_rsem)

    for d in far_first(xs) + [0]:
        to = (x + d) % xs
        p1a(to).wait_recv()
        own = flat_b[pl.ds(pl.multiple_of((to * 2 + core) * block_rows, 16), block_rows), :].astype(f32)
        pair_sum[to] = (own + p1a_recv[to].astype(f32)).astype(bf16)
        if d:
            p1b(d).start()

    for i in (13, 14, 15):
        copies[i].wait()
    reducer = z == s
    win_part = WIN // ss
    win_y = (s * win_part) // shard_rows
    win_row = (s * win_part) % shard_rows
    win_source = (z == 0) & (y == win_y)

    def col(d):
        return remote(own_state, col_state, col_ssem.at[d - 1], col_rsem, at((z + d) % zs, y, s))

    def ws_y(d):
        return remote(win_state, win_state, ws_y_ssem.at[d - 1], ws_rsem, at(z, (y + d) % ys, s))

    def ws_z(d):
        return remote(win_state, win_state, ws_z_ssem.at[d - 1], ws_rsem, at((z + d) % zs, y, s))

    @pl.when(reducer)
    def _():
        for d in far_first(zs):
            col(d).start()
        col_state[...] = own_state[...]

    @pl.when(win_source)
    def _():
        for i in range(3):
            win_state[i * win_part : (i + 1) * win_part, :] = own_state[
                pl.ds(pl.multiple_of(i * shard_rows + win_row, 16), win_part), :
            ]
        for d in far_first(ys):
            ws_y(d).start()
        for d in far_first(zs):
            ws_z(d).start()

    row = iota((rows, 256), 0)
    lane = iota((rows, 256), 1)
    shift = (lane % 8) - (7 - row % 8)
    for i in (1, 2, 3, 5, 6, 7, 8):
        copies[i].wait()
    for p in range(planes):
        cot_v[:, LANES * p : LANES * (p + 1)] = cot_ref[:, p].astype(f32).reshape(8 * emb, LANES).astype(bf16)
    spread = dot(w_ref[...].astype(f32).reshape(27 * ch, ch).astype(bf16), rep_lanes_ref[...])
    for a in range(3):
        for c in range(3):
            band = jnp.zeros((rows, 256), f32)
            for b in range(3):
                at_row = (a * 9 + b * 3 + c) * ch
                full = dot(rep_rows_ref[...], spread[at_row : at_row + ch].astype(bf16))
                band = jnp.where(shift == b - 1, full, band)
            wband[a, rows * c : rows * (c + 1), :] = band.astype(bf16)
    head = dot(dot_nt(rep_rows_ref[...], headt_ref[...]).astype(bf16), rep_emb_ref[...])
    hband[...] = jnp.where(shift[:, :LANES] == 0, head, 0.0).astype(bf16)
    bias_row = jnp.concatenate([bias_ref[...], jnp.zeros((1, LANES - ch), f32)], axis=1)
    row_l = iota((rows, LANES), 0)
    lane_l = iota((rows, LANES), 1)
    bias = jnp.sum(jnp.where(lane_l == row_l // 8, jnp.broadcast_to(bias_row, (rows, LANES)), 0.0), axis=1, keepdims=True)

    conv_v[...] = dot(wband[1], feat_v[:, LANES : LANES + cells])
    wait_halo(fh_send, fh_recv, fh_ssem, fh_rsem)
    feat_v[0:rows, 0:LANES] = fh_recv[0]
    feat_v[0:rows, LANES + cells : 2 * LANES + cells] = fh_recv[1]
    conv_v[...] += dot(wband[0], feat_v[:, 0:cells]) + dot(wband[2], feat_v[:, 2 * LANES : 2 * LANES + cells])

    def right(v):
        return jnp.where(lane_l == 0, 0.0, pltpu.roll(v, 1, 1))

    def left(v):
        return jnp.where(lane_l == LANES - 1, 0.0, pltpu.roll(v, LANES - 1, 1))

    def spread_dpre(dpre, p):
        at_lane = slice(LANES * p, LANES * (p + 1))
        dpre_v[0:rows, at_lane] = left(dpre).astype(bf16)
        dpre_v[rows : 2 * rows, at_lane] = dpre.astype(bf16)
        dpre_v[2 * rows : 3 * rows, at_lane] = right(dpre).astype(bf16)

    for p in (0, planes - 1) + tuple(range(1, planes - 1)):
        at_lane = slice(LANES * p, LANES * (p + 1))
        pre = (
            conv_v[rows : 2 * rows, at_lane]
            + right(conv_v[0:rows, at_lane])
            + left(conv_v[2 * rows : 3 * rows, at_lane])
            + bias
        )
        sigma = jax.nn.sigmoid(pre)
        act_v[0:rows, at_lane] = (pre * sigma).astype(bf16)
        dact = dot(hband[...], cot_v[:, at_lane])
        dpre = (dact * sigma * (1.0 + pre * (1.0 - sigma))).astype(bf16)
        if p == 0:
            dh_send[0] = dpre
        if p == planes - 1:
            dh_send[1] = dpre
        spread_dpre(dpre.astype(f32), p + 1)
        if p == planes - 1:
            start_halo(dh_send, dh_recv, dh_ssem, dh_rsem)
    act_v[rows : rows + 16, :] = jnp.ones((16, cells), bf16)

    def p2(d):
        other = (y + d) % ys
        return remote(
            p2_send.at[pl.ds(pl.multiple_of(other * shard_rows, 16), shard_rows)],
            p2_recv.at[d - 1], p2_ssem.at[d - 1], p2_rsem.at[d - 1], at(z, other, s),
        )

    def p3(d, back):
        part = p3_all.at[(z + zs - d) % zs if back else z]
        return remote(part, part, p3_ssem.at[d - 1], p3_rsem.at[d - 1], at((z + d) % zs, y, s))

    def share(d):
        return remote(grad_shard, grad_shard, share_ssem.at[d - 1], share_rsem, at(z, y, (s + d) % ss))

    near = ys // 4
    near_count = 2 * near + 1

    def shards_of(xx, slot, count):
        at_row = (xx * 2 + core) * block_rows + slot * shard_rows
        return weights_v.at[pl.ds(pl.multiple_of(at_row, 16), count * shard_rows)]

    def b2(d):
        return remote(
            shards_of(x, near, 1), shards_of(x, (near - d) % ys, 1),
            b2_ssem.at[d - 1], b2_rsem.at[d - 1], at(z, (y + d) % ys, s),
        )

    def b3x(d, far, back):
        slot, count = (near_count, ys - near_count) if far else (0, near_count)
        part = shards_of((x + xs - d) % xs if back else x, slot, count)
        return remote(part, part, b3x_ssem.at[d - 1, far], b3x_rsem.at[d - 1, far], at(z, y, (x + d) % xs * 2 + core))

    def b3c(d, back):
        xx = (x + xs - d) % xs
        return remote(
            block(ordered_v, xx, core), block(weights_out, xx, 1 - core if back else core),
            b3c_ssem.at[d], b3c_rsem.at[d], at(z, y, x * 2 + 1 - core),
        )

    def w1(d):
        part = win_send.at[pl.ds(pl.multiple_of((s + d) % ss * win_part, 16), win_part)]
        return remote(part, win_recv.at[d - 1], w1_ssem.at[d - 1], w1_rsem.at[d - 1], at(z, y, (s + d) % ss))

    def wy(d, back):
        part = wy_all.at[(y + ys - d) % ys if back else y]
        return remote(part, part, wy_ssem.at[d - 1], wy_rsem.at[d - 1], at(z, (y + d) % ys, s))

    def wz(d, back):
        part = wz_all.at[(z + zs - d) % zs if back else z]
        return remote(part, part, wz_ssem.at[d - 1], wz_rsem.at[d - 1], at((z + d) % zs, y, s))

    def wb(d, back):
        owner = (s + ss - d) % ss if back else s
        part = win_weights.at[pl.ds(pl.multiple_of(owner * win_part, 16), win_part)]
        return remote(part, part, wb_ssem.at[d - 1], wb_rsem.at[d - 1], at(z, y, (s + d) % ss))

    per_shard = shard_rows // win_part

    def wshare(d):
        part = win_grad.at[s % per_shard]
        return remote(part, part, wshare_ssem.at[d - 1], wshare_rsem.at[s % per_shard], at(z, y, (s + d) % ss))

    def wshare_in(i):
        part = win_grad.at[i]
        return remote(part, part, wshare_ssem.at[0], wshare_rsem.at[i], at(z, y, (s + 1) % ss))

    def updated(grad, state):
        count = grad.shape[0]
        return adam_update(grad, state[0:count, :], state[count : 2 * count, :], state[2 * count : 3 * count, :])

    def start_ys():
        for d in range(1, xs):
            p1b(d).wait_recv()
        total = pair_sum[x].astype(f32)
        for d in range(1, xs):
            total = total + p1b_recv[d - 1].astype(f32)
        sum_v[...] = total
        p2_send[...] = total.astype(bf16)
        for d in far_first(ys):
            p2(d).start()

    def start_zs():
        for d in range(1, ys):
            p2(d).wait_recv()
        total = sum_v[pl.ds(pl.multiple_of(y * shard_rows, 16), shard_rows), :]
        for d in range(1, ys):
            total = total + p2_recv[d - 1].astype(f32)
        p3_all[z] = total.astype(bf16)
        for d in far_first(zs):
            p3(d, False).start()

    def start_gather_ys():
        @pl.when(jnp.logical_not(reducer))
        def _():
            col(1).wait_recv()

        for d in range(1, zs):
            p3(d, True).wait_recv()
        grad = p3_all[0].astype(f32)
        for i in range(1, zs):
            grad = grad + p3_all[i].astype(f32)
        grad = grad / LOSS_SCALE
        weights = updated(grad, col_state)[2].astype(bf16)
        weights_v[pl.ds(pl.multiple_of(s * block_rows + near * shard_rows, 16), shard_rows), :] = weights
        for d in far_first(ys):
            b2(d).start()

        @pl.when(reducer)
        def _():
            grad_shard[...] = grad
            for d in range(1, ss):
                share(d).start()

    def start_gather_slabs():
        for far in range(2):
            for d in range(1, ys):
                if (min(d, ys - d) > near) == bool(far):
                    b2(d).wait_recv()
            for d in far_first(xs):
                b3x(d, far, False).start()

    def start_window_ys():
        for d in range(1, ss):
            w1(d).wait_recv()
        total = win_send[pl.ds(pl.multiple_of(s * win_part, 16), win_part), :].astype(f32)
        for d in range(1, ss):
            total = total + win_recv[d - 1].astype(f32)
        wy_all[y] = total.astype(bf16)
        for d in far_first(ys):
            wy(d, False).start()

    def start_window_zs():
        for d in range(1, ys):
            wy(d, True).wait_recv()
        total = wy_all[0].astype(f32)
        for i in range(1, ys):
            total = total + wy_all[i].astype(f32)
        wz_all[z] = total.astype(bf16)
        for d in far_first(zs):
            wz(d, False).start()

    in_window = (z == 0) & (y < WIN // shard_rows)
    win_owner = (z == 0) & (y == win_y)

    def start_window_gather():
        for d in range(1, zs):
            wz(d, True).wait_recv()
        grad = wz_all[0].astype(f32)
        for i in range(1, zs):
            grad = grad + wz_all[i].astype(f32)
        grad = grad / LOSS_SCALE
        weights = updated(grad, win_state)[2].astype(bf16)
        win_weights[pl.ds(pl.multiple_of(s * win_part, 16), win_part), :] = weights
        for d in range(1, ss):
            wb(d, False).start()

        @pl.when(win_owner)
        def _():
            win_grad[s % per_shard] = grad
            for d in range(1, ss):
                wshare(d).start()

    def finish_window():
        for d in range(1, ss):
            wb(d, True).wait_recv()

    def own_update():
        @pl.when(jnp.logical_not(reducer))
        def _():
            share(1).wait_recv()

        own_grad[...] = grad_shard[...]

        @pl.when(in_window)
        def _():
            for i in range(per_shard):
                @pl.when(s != y * per_shard + i)
                def _():
                    wshare_in(i).wait_recv()

                own_grad[i * win_part : (i + 1) * win_part, :] = win_grad[i]

        for i, value in enumerate(updated(own_grad[...], own_state)):
            shards_v[i] = value

    outs = [pltpu.make_async_copy(igrad_v, igrad_out, out_sem.at[0])]
    outs += [
        pltpu.make_async_copy(shards_v.at[i], ref, out_sem.at[1 + i]) for i, ref in enumerate((nmom_out, nsec_out, nmas_out))
    ]

    mask = ((lane < rows) & (shift >= -1) & (shift <= 1)) | ((lane >= rows) & (lane < rows + 8) & (shift == 0))
    mask = [mask[:, :LANES], mask[:, LANES:]]
    for a in range(3):
        grad_v[a] = dot_nt(dpre_v[:, LANES : LANES + cells], feat_v[:, LANES * a : LANES * a + cells])
    for i in range(9, 13):
        copies[i].wait()

    def rolled(v, by):
        return jnp.concatenate(
            [pltpu.roll(v[8 * o : 8 * o + 8], by, 1, stride=1, stride_axis=0) for o in range(v.shape[0] // 8)], axis=0
        )

    for pair in range(5):
        for t in range(2):
            total = None
            for slot in range(2):
                if pair * 2 + slot < 9:
                    a, c = divmod(pair * 2 + slot, 3)
                    part = grad_v[a, rows * c : rows * (c + 1), LANES * t : LANES * (t + 1)]
                    part = rolled(jnp.where(mask[t], part, 0.0), 3 * slot)
                    total = part if total is None else total + part
            at_lane = pair * 256 + t * LANES
            packed_v[:, at_lane : at_lane + LANES] = total.astype(bf16)
    sums = dot(add_ref[0:ch, 0:rows], packed_v[...])
    ordered = dot(sums.astype(bf16), order_ref[...])
    lane8 = iota((8, LANES), 1)
    row8 = iota((8, LANES), 0)
    zero8 = jnp.zeros((8, LANES), f32)
    for t in range(ch // 8):
        whole, base = divmod(64 * t, LANES)
        by = base + 8 * row8
        tiles = []
        for k in range(6):
            piece = ordered[8 * t : 8 * t + 8, LANES * k : LANES * (k + 1)]
            if k == 5:
                piece = jnp.where(lane8 < 8, piece, 0.0)
            tiles.append(pltpu.roll(piece, base, 1, stride=8, stride_axis=0))
        for m in range(7):
            k = m - whole
            high = tiles[k] if 0 <= k < 6 else zero8
            low = tiles[k - 1] if 0 <= k - 1 < 6 else zero8
            stack_v[m * ch + 8 * t : m * ch + 8 * t + 8, :] = jnp.where(lane8 >= by, high, low)
        bgrad = jnp.broadcast_to(ordered[8 * t : 8 * t + 8, 27 * ch : 27 * ch + 1], (8, LANES))
        stack_v[7 * ch + 8 * t : 7 * ch + 8 * t + 8, :] = jnp.where(lane8 == 64 + 8 * t + row8, bgrad, 0.0)

    hgrad = dot_nt(act_v[...], cot_v[...])
    row_h = iota((rows + 16, LANES), 0)
    lane_h = iota((rows + 16, LANES), 1)
    hgrad = rolled(jnp.where(lane_h % 8 == 7 - row_h % 8, hgrad, 0.0), 0).astype(bf16)
    hgrad = dot(dot(add_ref[...], hgrad).astype(bf16), emb_order_ref[...])
    for t in range(4):
        piece = pltpu.roll(hgrad[8 * t : 8 * t + 8], 0, 1, stride=16, stride_axis=0)
        stack_v[192 + 8 * t : 200 + 8 * t, :] = jnp.where(lane8 >= 88, piece, 0.0)
        stack_v[224 + 8 * t : 232 + 8 * t, :] = jnp.where(lane8 < 88, piece, 0.0)
    window = dot(place_ref[...], stack_v[...].astype(bf16)) + flat_b[0:WIN, :].astype(f32)
    win_send[...] = window.astype(bf16)
    for d in range(1, ss):
        w1(d).start()

    start_ys()
    @pl.when((z == 0) & (y != win_y))
    def _():
        ws_y(1).wait_recv()
        for d in far_first(zs):
            ws_z(d).start()

    wait_halo(dh_send, dh_recv, dh_ssem, dh_rsem)
    spread_dpre(dh_recv[0].astype(f32), 0)
    spread_dpre(dh_recv[1].astype(f32), planes + 1)

    total = None
    for a in range(3):
        part = dot_tn(wband[a, :, 0:rows], dpre_v[:, LANES * (2 - a) : LANES * (2 - a) + cells])
        total = part if total is None else total + part
    for p in range(planes):
        igrad_v[:, p] = total[:, LANES * p : LANES * (p + 1)].reshape(ch, 8, LANES).astype(bf16)
    outs[0].start()

    start_window_ys()
    start_zs()

    start_window_zs()
    start_gather_ys()
    @pl.when(z != 0)
    def _():
        ws_z(1).wait_recv()

    start_window_gather()
    start_gather_slabs()
    finish_window()

    def out_block(d):
        xx = (x + xs - d) % xs
        return pltpu.make_async_copy(block(ordered_v, xx, core), block(weights_out, xx, core), out_sem.at[4 + d])

    def finish_block(d):
        xx = (x + xs - d) % xs
        base = (xx * 2 + core) * block_rows
        for slot in range(ys):
            owner = (y + ys + slot - near) % ys
            ordered_v[pl.ds(pl.multiple_of(base + owner * shard_rows, 16), shard_rows), :] = weights_v[
                pl.ds(pl.multiple_of(base + slot * shard_rows, 16), shard_rows), :
            ]

        @pl.when((xx == 0) & (core == 0))
        def _():
            ordered_v[0:WIN, :] = win_weights[...]

        b3c(d, False).start()
        out_block(d).start()

    finish_block(0)
    own_update()
    for out in outs[1:4]:
        out.start()
    for d in sorted(range(1, xs), key=lambda d: min(d, xs - d)):
        for far in range(2):
            b3x(d, far, True).wait_recv()
        finish_block(d)
    for d in range(xs):
        b3c(d, True).wait_recv()

    for d in range(1, ss):
        w1(d).wait_send()
        wb(d, False).wait_send()
    for i in range(xs):
        p1a(i).wait_send()
    for d in range(1, xs):
        p1b(d).wait_send()
    for d in range(1, ys):
        p2(d).wait_send()
        wy(d, False).wait_send()
    for d in range(1, zs):
        p3(d, False).wait_send()
        wz(d, False).wait_send()

    @pl.when(reducer)
    def _():
        for d in range(1, zs):
            col(d).wait_send()
        for d in range(1, ss):
            share(d).wait_send()

    @pl.when(win_source)
    def _():
        for d in range(1, ys):
            ws_y(d).wait_send()

    @pl.when(z == 0)
    def _():
        for d in range(1, zs):
            ws_z(d).wait_send()

    @pl.when(win_owner)
    def _():
        for d in range(1, ss):
            wshare(d).wait_send()

    for d in range(xs):
        b3c(d, False).wait_send()
        out_block(d).wait()
    for d in range(1, xs):
        for far in range(2):
            b3x(d, far, False).wait_send()
    for d in range(1, ys):
        b2(d).wait_send()
    for out in outs:
        out.wait()


def copy_kernel(*refs):
    count = (len(refs) - 2) // 3
    in_sem, out_sem = refs[3 * count :]
    ins, outs, held = refs[:count], refs[count : 2 * count], refs[2 * count : 3 * count]
    part = ins[-1].shape[0] // 4
    pieces = [(i, slice(None)) for i in range(count - 1)] + [(count - 1, pl.ds(part * j, part)) for j in range(4)]
    loads = [pltpu.make_async_copy(ins[i].at[p], held[i].at[p], in_sem.at[k]) for k, (i, p) in enumerate(pieces)]
    stores = [pltpu.make_async_copy(held[i].at[p], outs[i].at[p], out_sem.at[k]) for k, (i, p) in enumerate(pieces)]
    for load in loads:
        load.start()
    for load, store in zip(loads, stores):
        load.wait()
        store.start()
    for store in stores:
        store.wait()


def on_device(
    features, cotangent, conv_weight, conv_bias, head_weight, grad_rest, master, moment, second
):
    ss = lax.axis_size("slab")
    zs = ss
    ys = lax.axis_size("rep") // zs
    ch, planes = features.shape[1], features.shape[2]
    emb = cotangent.shape[1]
    rows = 8 * ch
    cells = planes * LANES
    shard_rows = master.shape[0] // LANES
    block_rows = ys * shard_rows
    all_rows = ss * block_rows
    win_part = WIN // ss
    rest = grad_rest.shape[2]
    sizes = (zs, ys, ss, shard_rows, planes, ch, emb)
    tables = selection_tables(ch, emb)
    hbm = pl.BlockSpec(memory_space=pltpu.HBM)
    dma = pltpu.SemaphoreType.DMA
    shard = jax.ShapeDtypeStruct((shard_rows, LANES), f32)
    outs = pl.pallas_call(
        functools.partial(kernel, sizes),
        out_shape=(
            jax.ShapeDtypeStruct(features.shape[1:], bf16),
            shard,
            shard,
            shard,
            jax.ShapeDtypeStruct((all_rows, LANES), bf16),
        ),
        in_specs=[hbm] * 16,
        out_specs=(hbm,) * 5,
        scratch_shapes=[
            pltpu.VMEM(features.shape[1:], bf16),
            pltpu.VMEM(cotangent.shape[1:], bf16),
            pltpu.VMEM((27, ch, ch), bf16),
            pltpu.VMEM((1, ch), f32),
            pltpu.VMEM((emb, ch), bf16),
            pltpu.VMEM((1, rest), f32),
            pltpu.VMEM((3 * shard_rows, LANES), f32),
            *[pltpu.VMEM(t.shape, bf16) for t in tables],
            pltpu.VMEM(features.shape[1:], bf16),
            pltpu.VMEM((3, shard_rows, LANES), f32),
            pltpu.VMEM((all_rows, LANES), bf16),
            pltpu.VMEM((all_rows, LANES), bf16),
            pltpu.VMEM((all_rows, LANES), bf16),
            pltpu.VMEM((256, cells + 2 * LANES), bf16),
            pltpu.VMEM((8 * emb, cells), bf16),
            pltpu.VMEM((3, 3 * rows, 256), bf16),
            pltpu.VMEM((rows, LANES), bf16),
            pltpu.VMEM((3 * rows, cells), f32),
            pltpu.VMEM((rows + 16, cells), bf16),
            pltpu.VMEM((3 * rows, cells + 2 * LANES), bf16),
            pltpu.VMEM((3, 3 * rows, 256), f32),
            pltpu.VMEM((rows, 5 * 256), bf16),
            pltpu.VMEM((256, LANES), f32),
            pltpu.VMEM((2, rows, LANES), bf16),
            pltpu.VMEM((2, rows, LANES), bf16),
            pltpu.VMEM((2, rows, LANES), bf16),
            pltpu.VMEM((2, rows, LANES), bf16),
            pltpu.VMEM((ss // 2, block_rows, LANES), bf16),
            pltpu.VMEM((ss // 2, block_rows, LANES), bf16),
            pltpu.VMEM((max(ss // 2 - 1, 1), block_rows, LANES), bf16),
            pltpu.VMEM((block_rows, LANES), f32),
            pltpu.VMEM((block_rows, LANES), bf16),
            pltpu.VMEM((ys - 1, shard_rows, LANES), bf16),
            pltpu.VMEM((zs, shard_rows, LANES), bf16),
            pltpu.VMEM((3 * shard_rows, LANES), f32),
            pltpu.VMEM((shard_rows, LANES), f32),
            pltpu.VMEM((shard_rows, LANES), f32),
            pltpu.VMEM((WIN, LANES), bf16),
            pltpu.VMEM((ss - 1, win_part, LANES), bf16),
            pltpu.VMEM((ys, win_part, LANES), bf16),
            pltpu.VMEM((zs, win_part, LANES), bf16),
            pltpu.VMEM((3 * win_part, LANES), f32),
            pltpu.VMEM((shard_rows // win_part, win_part, LANES), f32),
            pltpu.VMEM((WIN, LANES), bf16),
            dma((16,)), dma((4 + ss,)),
            dma((2,)), dma((2,)), dma((2,)), dma((2,)),
            dma((ss // 2,)), dma((ss // 2,)),
            dma((max(ss // 2 - 1, 1),)), dma((max(ss // 2 - 1, 1),)),
            dma((ys - 1,)), dma((ys - 1,)),
            dma((zs - 1,)), dma((zs - 1,)),
            dma((zs - 1,)), dma,
            dma((ss - 1,)), dma,
            dma((ys - 1,)), dma((ys - 1,)),
            dma((max(ss // 2 - 1, 1), 2)), dma((max(ss // 2 - 1, 1), 2)),
            dma((ss // 2,)), dma((ss // 2,)),
            dma((ss - 1,)), dma((ss - 1,)),
            dma((ys - 1,)), dma((ys - 1,)),
            dma((zs - 1,)), dma((zs - 1,)),
            dma((ss - 1,)), dma((ss - 1,)),
            dma((ys - 1,)), dma((zs - 1,)), dma,
            dma((ss - 1,)), dma((shard_rows // win_part,)),
        ],
        compiler_params=pltpu.CompilerParams(
            collective_id=0, has_side_effects=True, vmem_limit_bytes=60 << 20
        ),
    )(
        features[0],
        cotangent[0],
        conv_weight.transpose(2, 3, 4, 0, 1).reshape(27, ch, ch),
        conv_bias.reshape(1, ch),
        head_weight.T,
        grad_rest,
        master.reshape(shard_rows, LANES),
        moment.reshape(shard_rows, LANES),
        second.reshape(shard_rows, LANES),
        *tables,
    )
    igrad, new_moment, new_second, new_master, weights = pl.pallas_call(
        copy_kernel,
        out_shape=tuple(jax.ShapeDtypeStruct(out.shape, out.dtype) for out in outs),
        in_specs=[pl.BlockSpec(memory_space=pl.ANY)] * 5,
        out_specs=(pl.BlockSpec(memory_space=pl.ANY),) * 5,
        scratch_shapes=[pltpu.VMEM(out.shape, out.dtype) for out in outs] + [dma((8,)), dma((8,))],
        compiler_params=pltpu.CompilerParams(vmem_limit_bytes=60 << 20),
    )(*outs)
    return (
        igrad[None],
        new_moment.reshape(-1),
        new_second.reshape(-1),
        new_master.reshape(-1),
        weights.reshape(-1),
    )


def solution(mesh):
    return jax.shard_map(
        on_device,
        mesh=mesh,
        in_specs=(
            P("rep", None, "slab", None, None),
            P("rep", None, "slab", None, None),
            P(),
            P(),
            P(),
            P("rep", "slab", None),
            P("rep"),
            P("rep"),
            P("rep"),
        ),
        out_specs=(P("rep", None, "slab", None, None), P("rep"), P("rep"), P("rep"), P()),
        check_vma=False,
    )
```

```python
import functools

import jax
import jax.numpy as jnp
import numpy as np
from jax import lax
from jax.experimental import pallas as pl
from jax.experimental.pallas import tpu as pltpu
from jax.sharding import PartitionSpec as P

LOSS_SCALE = 2048

beta_one = 0.9
beta_two = 0.99
learn_rate = 0.01
adam_eps = 1e-08
step_count = 10.0

f32 = jnp.float32
bf16 = jnp.bfloat16
MESH = pl.DeviceIdType.MESH
LANES = 128
CONV_ROWS = 124
CONV_LANES = 104
WIN = 128


def adam_update(grad, moment, second, master):
    new_moment = beta_one * moment + (1.0 - beta_one) * grad
    new_second = beta_two * second + (1.0 - beta_two) * grad * grad
    update = (
        new_moment
        / (1.0 - beta_one**step_count)
        / (jnp.sqrt(new_second / (1.0 - beta_two**step_count)) + adam_eps)
    )
    return (new_moment, new_second, master - learn_rate * update)


def selection_tables(ch, emb):
    rows = 8 * ch
    repeat_rows = np.zeros((rows, ch), np.float32)
    repeat_rows[np.arange(rows), np.arange(rows) // 8] = 1
    repeat_lanes = np.zeros((ch, 256), np.float32)
    repeat_lanes[np.arange(rows) // 8, np.arange(rows)] = 1
    repeat_emb = np.zeros((emb, 128), np.float32)
    repeat_emb[np.arange(128) // 8, np.arange(128)] = 1
    add_rows = np.zeros((32, rows + 16), np.float32)
    for i in range(ch + 1):
        add_rows[i, 8 * i : 8 * i + 8] = 1
    order = np.zeros((5 * 256, 768), np.float32)
    for a in range(3):
        for c in range(3):
            pair, slot = divmod(a * 3 + c, 2)
            for i in range(ch):
                tile, local = divmod(i, 16)
                for b in range(3):
                    lane = (8 * local + 6 + b + 3 * slot) % 128
                    order[pair * 256 + tile * 128 + lane, i * 27 + a * 9 + b * 3 + c] = 1
    order[2 * 256 + 128 + 8 * 8 + 7, ch * 27] = 1
    emb_order = np.zeros((128, 128), np.float32)
    for e in range(emb):
        emb_order[8 * e + 7, 88 + e] = 1
    place = np.zeros((WIN, 256), np.float32)
    for o in range(ch):
        for k in range(7):
            place[5 * o + k, k * ch + o] = 1
        place[121, 7 * ch + o] = 1
    for i in range(ch + 1):
        place[121 + i // 8, 192 + i] = 1
        place[122 + i // 8, 224 + i] = 1
    tables = (repeat_rows, repeat_lanes, repeat_emb, add_rows, order, emb_order, place)
    return tuple(jnp.asarray(t, bf16) for t in tables)


def far_first(count):
    return sorted(range(1, count), key=lambda d: -min(d, count - d))


def dot(lhs, rhs):
    return jnp.dot(lhs, rhs, preferred_element_type=f32)


def dot_nt(lhs, rhs):
    return lax.dot_general(lhs, rhs, (((1,), (1,)), ((), ())), preferred_element_type=f32)


def dot_tn(lhs, rhs):
    return lax.dot_general(lhs, rhs, (((0,), (0,)), ((), ())), preferred_element_type=f32)


def iota(shape, dim):
    return lax.broadcasted_iota(jnp.int32, shape, dim)


def kernel(
    sizes,
    feat_in, cot_in, w_in, bias_in, headt_in, rest_in, master_in, moment_in, second_in,
    rep_rows_in, rep_lanes_in, rep_emb_in, add_in, order_in, emb_order_in, place_in,
    igrad_out, nmom_out, nsec_out, nmas_out, weights_out,
    feat_ref, cot_ref, w_ref, bias_ref, headt_ref, rest_1d, own_state,
    rep_rows_ref, rep_lanes_ref, rep_emb_ref, add_ref, order_ref, emb_order_ref, place_ref,
    igrad_v, shards_v, weights_v, ordered_v,
    shared_rows, flat_b, feat_v, cot_v, wband, hband, conv_v, act_v, dpre_v, grad_v, packed_v, stack_v,
    fh_send, fh_recv, dh_send, dh_recv,
    p1a_recv, pair_sum, p1b_recv, sum_v, p2_send, p2_recv, p3_all, col_state, grad_shard, own_grad,
    win_send, win_recv, wy_all, wz_all, win_state, win_grad, win_weights,
    local_sem, out_sem, fh_ssem, fh_rsem, dh_ssem, dh_rsem,
    p1a_ssem, p1a_rsem, p1b_ssem, p1b_rsem, p2_ssem, p2_rsem, p3_ssem, p3_rsem,
    col_ssem, col_rsem, share_ssem, share_rsem, b2_ssem, b2_rsem, b3x_ssem, b3x_rsem, b3c_ssem, b3c_rsem,
    w1_ssem, w1_rsem, wy_ssem, wy_rsem, wz_ssem, wz_rsem, wb_ssem, wb_rsem,
    ws_y_ssem, ws_z_ssem, ws_rsem, wshare_ssem, wshare_rsem,
):
    zs, ys, ss, shard_rows, planes, ch, emb = sizes
    rows = 8 * ch
    cells = planes * LANES
    block_rows = ys * shard_rows
    rep = lax.axis_index("rep")
    s = lax.axis_index("slab")
    z = rep // ys
    y = rep % ys

    def at(zz, yy, sl):
        return (zz * ys + yy, sl)

    def remote(src, dst, ssem, rsem, device):
        return pltpu.make_async_remote_copy(
            src_ref=src, dst_ref=dst, send_sem=ssem, recv_sem=rsem, device_id=device, device_id_type=MESH
        )

    barrier = pltpu.get_barrier_semaphore()
    for d in far_first(max(ys, zs, ss)):
        if d < zs:
            pl.semaphore_signal(barrier, inc=1, device_id=at((z + d) % zs, y, s), device_id_type=MESH)
        if d < ys:
            pl.semaphore_signal(barrier, inc=1, device_id=at(z, (y + d) % ys, s), device_id_type=MESH)
        if d < ss:
            pl.semaphore_signal(barrier, inc=1, device_id=at(z, y, (s + d) % ss), device_id_type=MESH)

    ins = (
        (feat_in, feat_ref), (w_in, w_ref), (rep_lanes_in, rep_lanes_ref), (rep_rows_in, rep_rows_ref),
        (rest_in.at[0], rest_1d), (headt_in, headt_ref), (rep_emb_in, rep_emb_ref), (bias_in, bias_ref),
        (cot_in, cot_ref), (order_in, order_ref), (add_in, add_ref), (emb_order_in, emb_order_ref),
        (place_in, place_ref),
        *[(ref, own_state.at[pl.ds(i * shard_rows, shard_rows)]) for i, ref in enumerate((moment_in, second_in, master_in))],
    )
    copies = [pltpu.make_async_copy(src, dst, local_sem.at[i]) for i, (src, dst) in enumerate(ins)]
    for copy in copies:
        copy.start()

    near = ys // 4
    near_count = 2 * near + 1
    far_count = ys - near_count
    far_rows = far_count * shard_rows

    def placed(row):
        block_at = lax.div(row, block_rows)
        in_block = lax.rem(row, block_rows)
        slot = lax.rem(lax.div(in_block, shard_rows) + (2 * ys - near - 1) - y, ys)
        return pl.multiple_of(block_at * block_rows + slot * shard_rows + lax.rem(in_block, shard_rows), 16)

    def store_rows(row, value):
        flat_b[pl.ds(placed(jnp.int32(row)), 16), :] = value

    copies[4].wait()
    first, last = CONV_ROWS // 16, flat_b.shape[0] // 16 - 1
    for j in range(first):
        store_rows(16 * j, jnp.zeros((16, LANES), bf16))
    lane16 = iota((16, LANES), 1)

    def moved(here, later):
        return pltpu.roll(jnp.where(lane16 >= LANES - CONV_LANES, here, later), CONV_LANES, 1).astype(bf16)

    def rest_rows(start, count):
        return rest_1d[0:1, pl.ds(start, count * LANES)].reshape(count, LANES)

    lane8 = iota((8, LANES), 1)

    def moved8(here, later):
        return pltpu.roll(jnp.where(lane8 >= LANES - CONV_LANES, here, later), CONV_LANES, 1)

    per_step = 8
    skipped = (16 * (first + 1) - CONV_ROWS - 1) * LANES

    def align_at(at_row):
        halves = []
        for h in range(2):
            start = (at_row + 8 * h) * LANES + skipped
            halves.append(moved8(rest_rows(start, 8), rest_rows(start + LANES, 8)))
        part = jnp.concatenate(halves, axis=0).astype(bf16)
        store_rows(at_row + 16 * (first + 1), part)

    def align(j, carry):
        for i in range(per_step):
            align_at(pl.multiple_of(j * (16 * per_step), 16 * per_step) + 16 * i)
        return carry

    steps = (last - first - 1) // per_step
    lax.fori_loop(0, steps, align, 0)
    for j in range(steps * per_step, last - first - 1):
        align_at(16 * j)
    lead = CONV_ROWS - 16 * first
    start_rows = rest_rows(0, 8)
    shared_rows[...] = moved(
        jnp.concatenate([jnp.zeros((lead + 1, LANES), f32), start_rows[0 : 15 - lead]], axis=0),
        jnp.concatenate([jnp.zeros((lead, LANES), f32), start_rows[0 : 16 - lead]], axis=0),
    )
    store_rows(16 * first, shared_rows[...])
    end_row = 16 * last - CONV_ROWS - 1
    end = rest_1d[0:1, (end_row + 16) * LANES :]
    end = jnp.concatenate([end, jnp.zeros((1, LANES - end.shape[1]), f32)], axis=1)
    end_rows = rest_rows(end_row * LANES, 16)
    store_rows(16 * last, moved(end_rows, jnp.concatenate([end_rows[1:16], end], axis=0)))

    pl.semaphore_wait(barrier, (ss - 1) + (ys - 1) + (zs - 1))

    xs = ss // 2
    x = s // 2
    core = s % 2

    def block(ref, xx, cc):
        return ref.at[pl.ds(pl.multiple_of((xx * 2 + cc) * block_rows, 16), block_rows)]

    def p1a(i):
        return remote(
            block(flat_b, i, 1 - core), p1a_recv.at[i], p1a_ssem.at[i], p1a_rsem.at[i], at(z, y, x * 2 + 1 - core)
        )

    def p1b(d, part):
        to = (x + d) % xs
        some = pl.ds(far_rows, block_rows - far_rows) if part else pl.ds(0, far_rows)
        return remote(
            pair_sum.at[to, some], p1b_recv.at[d - 1, some],
            p1b_ssem.at[d - 1, part], p1b_rsem.at[d - 1, part], at(z, y, to * 2 + core),
        )

    order = [(x + d) % xs for d in far_first(xs) + [0]]
    for i in order:
        p1a(i).start()

    copies[0].wait()
    for p in range(planes):
        plane = feat_ref[:, p].astype(f32).reshape(rows, LANES).astype(bf16)
        feat_v[0:rows, LANES * (p + 1) : LANES * (p + 2)] = plane
        if p == 0:
            fh_send[0] = plane
        if p == planes - 1:
            fh_send[1] = plane
    feat_v[rows : rows + 16, :] = jnp.ones((16, cells + 2 * LANES), bf16)
    feat_v[rows + 16 : 256, :] = jnp.zeros((256 - rows - 16, cells + 2 * LANES), bf16)

    def halo(send, recv, ssem, rsem, up):
        source, slot = (1, 0) if up else (0, 1)
        other = (s + 1) % ss if up else (s + ss - 1) % ss
        return remote(send.at[source], recv.at[slot], ssem.at[source], rsem.at[slot], at(z, y, other))

    def start_halo(send, recv, ssem, rsem):
        @pl.when(s < ss - 1)
        def _():
            halo(send, recv, ssem, rsem, True).start()

        @pl.when(s > 0)
        def _():
            halo(send, recv, ssem, rsem, False).start()

        @pl.when(s == 0)
        def _():
            recv[0] = jnp.zeros((rows, LANES), bf16)

        @pl.when(s == ss - 1)
        def _():
            recv[1] = jnp.zeros((rows, LANES), bf16)

    def wait_halo(send, recv, ssem, rsem):
        @pl.when(s < ss - 1)
        def _():
            halo(send, recv, ssem, rsem, True).wait_send()
            halo(send, recv, ssem, rsem, False).wait_recv()

        @pl.when(s > 0)
        def _():
            halo(send, recv, ssem, rsem, False).wait_send()
            halo(send, recv, ssem, rsem, True).wait_recv()

    start_halo(fh_send, fh_recv, fh_ssem, fh_rsem)

    for d in far_first(xs) + [0]:
        to = (x + d) % xs
        p1a(to).wait_recv()
        own = flat_b[pl.ds(pl.multiple_of((to * 2 + core) * block_rows, 16), block_rows), :].astype(f32)
        pair_sum[to] = (own + p1a_recv[to].astype(f32)).astype(bf16)
        if d:
            p1b(d, 0).start()
    for d in far_first(xs):
        p1b(d, 1).start()

    for i in (13, 14, 15):
        copies[i].wait()
    reducer = z == s
    win_part = WIN // ss
    win_y = (s * win_part) // shard_rows
    win_row = (s * win_part) % shard_rows
    win_source = (z == 0) & (y == win_y)

    def col(d):
        return remote(own_state, col_state, col_ssem.at[d - 1], col_rsem, at((z + d) % zs, y, s))

    def ws_y(d):
        return remote(win_state, win_state, ws_y_ssem.at[d - 1], ws_rsem, at(z, (y + d) % ys, s))

    def ws_z(d):
        return remote(win_state, win_state, ws_z_ssem.at[d - 1], ws_rsem, at((z + d) % zs, y, s))

    @pl.when(reducer)
    def _():
        for d in far_first(zs):
            col(d).start()
        col_state[...] = own_state[...]

    @pl.when(win_source)
    def _():
        for i in range(3):
            win_state[i * win_part : (i + 1) * win_part, :] = own_state[
                pl.ds(pl.multiple_of(i * shard_rows + win_row, 16), win_part), :
            ]
        for d in far_first(ys):
            ws_y(d).start()
        for d in far_first(zs):
            ws_z(d).start()

    row = iota((rows, 256), 0)
    lane = iota((rows, 256), 1)
    shift = (lane % 8) - (7 - row % 8)
    for i in (1, 2, 3, 5, 6, 7, 8):
        copies[i].wait()
    for p in range(planes):
        cot_v[:, LANES * p : LANES * (p + 1)] = cot_ref[:, p].astype(f32).reshape(8 * emb, LANES).astype(bf16)
    spread = dot(w_ref[...].astype(f32).reshape(27 * ch, ch).astype(bf16), rep_lanes_ref[...])
    for a in range(3):
        for c in range(3):
            band = jnp.zeros((rows, 256), f32)
            for b in range(3):
                at_row = (a * 9 + b * 3 + c) * ch
                full = dot(rep_rows_ref[...], spread[at_row : at_row + ch].astype(bf16))
                band = jnp.where(shift == b - 1, full, band)
            wband[a, rows * c : rows * (c + 1), :] = band.astype(bf16)
    head = dot(dot_nt(rep_rows_ref[...], headt_ref[...]).astype(bf16), rep_emb_ref[...])
    hband[...] = jnp.where(shift[:, :LANES] == 0, head, 0.0).astype(bf16)
    bias_row = jnp.concatenate([bias_ref[...], jnp.zeros((1, LANES - ch), f32)], axis=1)
    row_l = iota((rows, LANES), 0)
    lane_l = iota((rows, LANES), 1)
    bias = jnp.sum(jnp.where(lane_l == row_l // 8, jnp.broadcast_to(bias_row, (rows, LANES)), 0.0), axis=1, keepdims=True)

    conv_v[...] = dot(wband[1], feat_v[:, LANES : LANES + cells])
    wait_halo(fh_send, fh_recv, fh_ssem, fh_rsem)
    feat_v[0:rows, 0:LANES] = fh_recv[0]
    feat_v[0:rows, LANES + cells : 2 * LANES + cells] = fh_recv[1]
    conv_v[...] += dot(wband[0], feat_v[:, 0:cells]) + dot(wband[2], feat_v[:, 2 * LANES : 2 * LANES + cells])

    def right(v):
        return jnp.where(lane_l == 0, 0.0, pltpu.roll(v, 1, 1))

    def left(v):
        return jnp.where(lane_l == LANES - 1, 0.0, pltpu.roll(v, LANES - 1, 1))

    def spread_dpre(dpre, p):
        at_lane = slice(LANES * p, LANES * (p + 1))
        dpre_v[0:rows, at_lane] = left(dpre).astype(bf16)
        dpre_v[rows : 2 * rows, at_lane] = dpre.astype(bf16)
        dpre_v[2 * rows : 3 * rows, at_lane] = right(dpre).astype(bf16)

    for p in (0, planes - 1) + tuple(range(1, planes - 1)):
        at_lane = slice(LANES * p, LANES * (p + 1))
        pre = (
            conv_v[rows : 2 * rows, at_lane]
            + right(conv_v[0:rows, at_lane])
            + left(conv_v[2 * rows : 3 * rows, at_lane])
            + bias
        )
        sigma = jax.nn.sigmoid(pre)
        act_v[0:rows, at_lane] = (pre * sigma).astype(bf16)
        dact = dot(hband[...], cot_v[:, at_lane])
        dpre = (dact * sigma * (1.0 + pre * (1.0 - sigma))).astype(bf16)
        if p == 0:
            dh_send[0] = dpre
        if p == planes - 1:
            dh_send[1] = dpre
        spread_dpre(dpre.astype(f32), p + 1)
        if p == planes - 1:
            start_halo(dh_send, dh_recv, dh_ssem, dh_rsem)
    act_v[rows : rows + 16, :] = jnp.ones((16, cells), bf16)

    def p2(d):
        slot = (d - near - 1) % ys
        return remote(
            p2_send.at[pl.ds(slot * shard_rows, shard_rows)], p2_recv.at[d - 1],
            p2_ssem.at[d - 1], p2_rsem.at[d - 1], at(z, (y + d) % ys, s),
        )

    def p3(d, back):
        part = p3_all.at[(z + zs - d) % zs if back else z]
        return remote(part, part, p3_ssem.at[d - 1], p3_rsem.at[d - 1], at((z + d) % zs, y, s))

    def share(d):
        return remote(grad_shard, grad_shard, share_ssem.at[d - 1], share_rsem, at(z, y, (s + d) % ss))

    def shards_of(xx, slot, count):
        at_row = (xx * 2 + core) * block_rows + slot * shard_rows
        return weights_v.at[pl.ds(pl.multiple_of(at_row, 16), count * shard_rows)]

    def b2(d):
        return remote(
            shards_of(x, near, 1), shards_of(x, (near - d) % ys, 1),
            b2_ssem.at[d - 1], b2_rsem.at[d - 1], at(z, (y + d) % ys, s),
        )

    def b3x(d, far, back):
        slot, count = (near_count, ys - near_count) if far else (0, near_count)
        part = shards_of((x + xs - d) % xs if back else x, slot, count)
        return remote(part, part, b3x_ssem.at[d - 1, far], b3x_rsem.at[d - 1, far], at(z, y, (x + d) % xs * 2 + core))

    def b3c(d, back):
        xx = (x + xs - d) % xs
        return remote(
            block(ordered_v, xx, core), block(weights_out, xx, 1 - core if back else core),
            b3c_ssem.at[d], b3c_rsem.at[d], at(z, y, x * 2 + 1 - core),
        )

    def w1(d):
        part = win_send.at[pl.ds(pl.multiple_of((s + d) % ss * win_part, 16), win_part)]
        return remote(part, win_recv.at[d - 1], w1_ssem.at[d - 1], w1_rsem.at[d - 1], at(z, y, (s + d) % ss))

    def wy(d, back):
        part = wy_all.at[(y + ys - d) % ys if back else y]
        return remote(part, part, wy_ssem.at[d - 1], wy_rsem.at[d - 1], at(z, (y + d) % ys, s))

    def wz(d, back):
        part = wz_all.at[(z + zs - d) % zs if back else z]
        return remote(part, part, wz_ssem.at[d - 1], wz_rsem.at[d - 1], at((z + d) % zs, y, s))

    def wb(d, back):
        owner = (s + ss - d) % ss if back else s
        part = win_weights.at[pl.ds(pl.multiple_of(owner * win_part, 16), win_part)]
        return remote(part, part, wb_ssem.at[d - 1], wb_rsem.at[d - 1], at(z, y, (s + d) % ss))

    per_shard = shard_rows // win_part

    def wshare(d):
        part = win_grad.at[s % per_shard]
        return remote(part, part, wshare_ssem.at[d - 1], wshare_rsem.at[s % per_shard], at(z, y, (s + d) % ss))

    def wshare_in(i):
        part = win_grad.at[i]
        return remote(part, part, wshare_ssem.at[0], wshare_rsem.at[i], at(z, y, (s + 1) % ss))

    def updated(grad, state):
        count = grad.shape[0]
        return adam_update(grad, state[0:count, :], state[count : 2 * count, :], state[2 * count : 3 * count, :])

    def start_ys():
        for part, some in enumerate((slice(0, far_rows), slice(far_rows, block_rows))):
            for d in range(1, xs):
                p1b(d, part).wait_recv()
            total = pair_sum[x, some].astype(f32)
            for d in range(1, xs):
                total = total + p1b_recv[d - 1, some].astype(f32)
            sum_v[some, :] = total
            p2_send[some, :] = total.astype(bf16)
            for d in far_first(ys):
                if (min(d, ys - d) <= near) == bool(part):
                    p2(d).start()

    def start_zs():
        for d in range(1, ys):
            p2(d).wait_recv()
        total = sum_v[(ys - 1 - near) * shard_rows : (ys - near) * shard_rows, :]
        for d in range(1, ys):
            total = total + p2_recv[d - 1].astype(f32)
        p3_all[z] = total.astype(bf16)
        for d in far_first(zs):
            p3(d, False).start()

    def start_gather_ys():
        @pl.when(jnp.logical_not(reducer))
        def _():
            col(1).wait_recv()

        for d in range(1, zs):
            p3(d, True).wait_recv()
        grad = p3_all[0].astype(f32)
        for i in range(1, zs):
            grad = grad + p3_all[i].astype(f32)
        grad = grad / LOSS_SCALE
        weights = updated(grad, col_state)[2].astype(bf16)
        weights_v[pl.ds(pl.multiple_of(s * block_rows + near * shard_rows, 16), shard_rows), :] = weights
        for d in far_first(ys):
            b2(d).start()

        @pl.when(reducer)
        def _():
            grad_shard[...] = grad
            for d in range(1, ss):
                share(d).start()

    def start_gather_slabs():
        for far in range(2):
            for d in range(1, ys):
                if (min(d, ys - d) > near) == bool(far):
                    b2(d).wait_recv()
            for d in far_first(xs):
                b3x(d, far, False).start()

    def start_window_ys():
        for d in range(1, ss):
            w1(d).wait_recv()
        total = win_send[pl.ds(pl.multiple_of(s * win_part, 16), win_part), :].astype(f32)
        for d in range(1, ss):
            total = total + win_recv[d - 1].astype(f32)
        wy_all[y] = total.astype(bf16)
        for d in far_first(ys):
            wy(d, False).start()

    def start_window_zs():
        for d in range(1, ys):
            wy(d, True).wait_recv()
        total = wy_all[0].astype(f32)
        for i in range(1, ys):
            total = total + wy_all[i].astype(f32)
        wz_all[z] = total.astype(bf16)
        for d in far_first(zs):
            wz(d, False).start()

    in_window = (z == 0) & (y < WIN // shard_rows)
    win_owner = (z == 0) & (y == win_y)

    def start_window_gather():
        for d in range(1, zs):
            wz(d, True).wait_recv()
        grad = wz_all[0].astype(f32)
        for i in range(1, zs):
            grad = grad + wz_all[i].astype(f32)
        grad = grad / LOSS_SCALE
        weights = updated(grad, win_state)[2].astype(bf16)
        win_weights[pl.ds(pl.multiple_of(s * win_part, 16), win_part), :] = weights
        for d in range(1, ss):
            wb(d, False).start()

        @pl.when(win_owner)
        def _():
            win_grad[s % per_shard] = grad
            for d in range(1, ss):
                wshare(d).start()

    def finish_window():
        for d in range(1, ss):
            wb(d, True).wait_recv()

    def own_update():
        @pl.when(jnp.logical_not(reducer))
        def _():
            share(1).wait_recv()

        own_grad[...] = grad_shard[...]

        @pl.when(in_window)
        def _():
            for i in range(per_shard):
                @pl.when(s != y * per_shard + i)
                def _():
                    wshare_in(i).wait_recv()

                own_grad[i * win_part : (i + 1) * win_part, :] = win_grad[i]

        for i, value in enumerate(updated(own_grad[...], own_state)):
            shards_v[i] = value

    outs = [pltpu.make_async_copy(igrad_v, igrad_out, out_sem.at[0])]
    outs += [
        pltpu.make_async_copy(shards_v.at[i], ref, out_sem.at[1 + i]) for i, ref in enumerate((nmom_out, nsec_out, nmas_out))
    ]

    mask = ((lane < rows) & (shift >= -1) & (shift <= 1)) | ((lane >= rows) & (lane < rows + 8) & (shift == 0))
    mask = [mask[:, :LANES], mask[:, LANES:]]
    for a in range(3):
        grad_v[a] = dot_nt(dpre_v[:, LANES : LANES + cells], feat_v[:, LANES * a : LANES * a + cells])
    for i in range(9, 13):
        copies[i].wait()

    def rolled(v, by):
        return jnp.concatenate(
            [pltpu.roll(v[8 * o : 8 * o + 8], by, 1, stride=1, stride_axis=0) for o in range(v.shape[0] // 8)], axis=0
        )

    for pair in range(5):
        for t in range(2):
            total = None
            for slot in range(2):
                if pair * 2 + slot < 9:
                    a, c = divmod(pair * 2 + slot, 3)
                    part = grad_v[a, rows * c : rows * (c + 1), LANES * t : LANES * (t + 1)]
                    part = rolled(jnp.where(mask[t], part, 0.0), 3 * slot)
                    total = part if total is None else total + part
            at_lane = pair * 256 + t * LANES
            packed_v[:, at_lane : at_lane + LANES] = total.astype(bf16)
    sums = dot(add_ref[0:ch, 0:rows], packed_v[...])
    ordered = dot(sums.astype(bf16), order_ref[...])
    lane8 = iota((8, LANES), 1)
    row8 = iota((8, LANES), 0)
    zero8 = jnp.zeros((8, LANES), f32)
    for t in range(ch // 8):
        whole, base = divmod(64 * t, LANES)
        by = base + 8 * row8
        tiles = []
        for k in range(6):
            piece = ordered[8 * t : 8 * t + 8, LANES * k : LANES * (k + 1)]
            if k == 5:
                piece = jnp.where(lane8 < 8, piece, 0.0)
            tiles.append(pltpu.roll(piece, base, 1, stride=8, stride_axis=0))
        for m in range(7):
            k = m - whole
            high = tiles[k] if 0 <= k < 6 else zero8
            low = tiles[k - 1] if 0 <= k - 1 < 6 else zero8
            stack_v[m * ch + 8 * t : m * ch + 8 * t + 8, :] = jnp.where(lane8 >= by, high, low)
        bgrad = jnp.broadcast_to(ordered[8 * t : 8 * t + 8, 27 * ch : 27 * ch + 1], (8, LANES))
        stack_v[7 * ch + 8 * t : 7 * ch + 8 * t + 8, :] = jnp.where(lane8 == 64 + 8 * t + row8, bgrad, 0.0)

    hgrad = dot_nt(act_v[...], cot_v[...])
    row_h = iota((rows + 16, LANES), 0)
    lane_h = iota((rows + 16, LANES), 1)
    hgrad = rolled(jnp.where(lane_h % 8 == 7 - row_h % 8, hgrad, 0.0), 0).astype(bf16)
    hgrad = dot(dot(add_ref[...], hgrad).astype(bf16), emb_order_ref[...])
    for t in range(4):
        piece = pltpu.roll(hgrad[8 * t : 8 * t + 8], 0, 1, stride=16, stride_axis=0)
        stack_v[192 + 8 * t : 200 + 8 * t, :] = jnp.where(lane8 >= 88, piece, 0.0)
        stack_v[224 + 8 * t : 232 + 8 * t, :] = jnp.where(lane8 < 88, piece, 0.0)
    window = dot(place_ref[...], stack_v[...].astype(bf16))
    win_send[0 : 16 * first, :] = window[0 : 16 * first].astype(bf16)
    win_send[16 * first : WIN, :] = (window[16 * first : WIN] + shared_rows[...].astype(f32)).astype(bf16)
    for d in range(1, ss):
        w1(d).start()

    start_ys()
    @pl.when((z == 0) & (y != win_y))
    def _():
        ws_y(1).wait_recv()
        for d in far_first(zs):
            ws_z(d).start()

    wait_halo(dh_send, dh_recv, dh_ssem, dh_rsem)
    spread_dpre(dh_recv[0].astype(f32), 0)
    spread_dpre(dh_recv[1].astype(f32), planes + 1)

    total = None
    for a in range(3):
        part = dot_tn(wband[a, :, 0:rows], dpre_v[:, LANES * (2 - a) : LANES * (2 - a) + cells])
        total = part if total is None else total + part
    for p in range(planes):
        igrad_v[:, p] = total[:, LANES * p : LANES * (p + 1)].reshape(ch, 8, LANES).astype(bf16)
    outs[0].start()

    start_window_ys()
    start_zs()

    start_window_zs()
    start_gather_ys()
    @pl.when(z != 0)
    def _():
        ws_z(1).wait_recv()

    start_window_gather()
    start_gather_slabs()
    def out_block(d):
        xx = (x + xs - d) % xs
        return pltpu.make_async_copy(block(ordered_v, xx, core), block(weights_out, xx, core), out_sem.at[4 + d])

    def finish_block(d):
        base = ((x + xs - d) % xs * 2 + core) * block_rows
        for slot in range(ys):
            owner = (y + ys + slot - near) % ys
            ordered_v[pl.ds(pl.multiple_of(base + owner * shard_rows, 16), shard_rows), :] = weights_v[
                pl.ds(pl.multiple_of(base + slot * shard_rows, 16), shard_rows), :
            ]

        @pl.when((x != d) | (core != 0))
        def _():
            b3c(d, False).start()
            out_block(d).start()

    nearest = sorted(range(1, xs), key=lambda d: min(d, xs - d))
    finish_block(0)
    for d in nearest:
        for far in range(2):
            b3x(d, far, True).wait_recv()
        finish_block(d)
    finish_window()

    @pl.when(core == 0)
    def _():
        ordered_v[0:WIN, :] = win_weights[...]
        for d in range(xs):
            @pl.when(x == d)
            def _():
                b3c(d, False).start()
                out_block(d).start()

    own_update()
    for out in outs[1:4]:
        out.start()
    for d in range(xs):
        b3c(d, True).wait_recv()

    for d in range(1, ss):
        w1(d).wait_send()
        wb(d, False).wait_send()
    for i in range(xs):
        p1a(i).wait_send()
    for d in range(1, xs):
        p1b(d, 0).wait_send()
        p1b(d, 1).wait_send()
    for d in range(1, ys):
        p2(d).wait_send()
        wy(d, False).wait_send()
    for d in range(1, zs):
        p3(d, False).wait_send()
        wz(d, False).wait_send()

    @pl.when(reducer)
    def _():
        for d in range(1, zs):
            col(d).wait_send()
        for d in range(1, ss):
            share(d).wait_send()

    @pl.when(win_source)
    def _():
        for d in range(1, ys):
            ws_y(d).wait_send()

    @pl.when(z == 0)
    def _():
        for d in range(1, zs):
            ws_z(d).wait_send()

    @pl.when(win_owner)
    def _():
        for d in range(1, ss):
            wshare(d).wait_send()

    for d in range(xs):
        b3c(d, False).wait_send()
        out_block(d).wait()
    for d in range(1, xs):
        for far in range(2):
            b3x(d, far, False).wait_send()
    for d in range(1, ys):
        b2(d).wait_send()
    for out in outs:
        out.wait()


def copy_kernel(*refs):
    count = (len(refs) - 2) // 3
    in_sem, out_sem = refs[3 * count :]
    ins, outs, held = refs[:count], refs[count : 2 * count], refs[2 * count : 3 * count]
    part = ins[-1].shape[0] // 4
    pieces = [(i, slice(None)) for i in range(count - 1)] + [(count - 1, pl.ds(part * j, part)) for j in range(4)]
    loads = [pltpu.make_async_copy(ins[i].at[p], held[i].at[p], in_sem.at[k]) for k, (i, p) in enumerate(pieces)]
    stores = [pltpu.make_async_copy(held[i].at[p], outs[i].at[p], out_sem.at[k]) for k, (i, p) in enumerate(pieces)]
    for load in loads:
        load.start()
    for load, store in zip(loads, stores):
        load.wait()
        store.start()
    for store in stores:
        store.wait()


def on_device(
    features, cotangent, conv_weight, conv_bias, head_weight, grad_rest, master, moment, second
):
    ss = lax.axis_size("slab")
    zs = ss
    ys = lax.axis_size("rep") // zs
    ch, planes = features.shape[1], features.shape[2]
    emb = cotangent.shape[1]
    rows = 8 * ch
    cells = planes * LANES
    shard_rows = master.shape[0] // LANES
    block_rows = ys * shard_rows
    all_rows = ss * block_rows
    win_part = WIN // ss
    rest = grad_rest.shape[2]
    sizes = (zs, ys, ss, shard_rows, planes, ch, emb)
    tables = selection_tables(ch, emb)
    hbm = pl.BlockSpec(memory_space=pltpu.HBM)
    dma = pltpu.SemaphoreType.DMA
    shard = jax.ShapeDtypeStruct((shard_rows, LANES), f32)
    outs = pl.pallas_call(
        functools.partial(kernel, sizes),
        out_shape=(
            jax.ShapeDtypeStruct(features.shape[1:], bf16),
            shard,
            shard,
            shard,
            jax.ShapeDtypeStruct((all_rows, LANES), bf16),
        ),
        in_specs=[hbm] * 16,
        out_specs=(hbm,) * 5,
        scratch_shapes=[
            pltpu.VMEM(features.shape[1:], bf16),
            pltpu.VMEM(cotangent.shape[1:], bf16),
            pltpu.VMEM((27, ch, ch), bf16),
            pltpu.VMEM((1, ch), f32),
            pltpu.VMEM((emb, ch), bf16),
            pltpu.VMEM((1, rest), f32),
            pltpu.VMEM((3 * shard_rows, LANES), f32),
            *[pltpu.VMEM(t.shape, bf16) for t in tables],
            pltpu.VMEM(features.shape[1:], bf16),
            pltpu.VMEM((3, shard_rows, LANES), f32),
            pltpu.VMEM((all_rows, LANES), bf16),
            pltpu.VMEM((all_rows, LANES), bf16),
            pltpu.VMEM((16, LANES), bf16),
            pltpu.VMEM((all_rows, LANES), bf16),
            pltpu.VMEM((256, cells + 2 * LANES), bf16),
            pltpu.VMEM((8 * emb, cells), bf16),
            pltpu.VMEM((3, 3 * rows, 256), bf16),
            pltpu.VMEM((rows, LANES), bf16),
            pltpu.VMEM((3 * rows, cells), f32),
            pltpu.VMEM((rows + 16, cells), bf16),
            pltpu.VMEM((3 * rows, cells + 2 * LANES), bf16),
            pltpu.VMEM((3, 3 * rows, 256), f32),
            pltpu.VMEM((rows, 5 * 256), bf16),
            pltpu.VMEM((256, LANES), f32),
            pltpu.VMEM((2, rows, LANES), bf16),
            pltpu.VMEM((2, rows, LANES), bf16),
            pltpu.VMEM((2, rows, LANES), bf16),
            pltpu.VMEM((2, rows, LANES), bf16),
            pltpu.VMEM((ss // 2, block_rows, LANES), bf16),
            pltpu.VMEM((ss // 2, block_rows, LANES), bf16),
            pltpu.VMEM((max(ss // 2 - 1, 1), block_rows, LANES), bf16),
            pltpu.VMEM((block_rows, LANES), f32),
            pltpu.VMEM((block_rows, LANES), bf16),
            pltpu.VMEM((ys - 1, shard_rows, LANES), bf16),
            pltpu.VMEM((zs, shard_rows, LANES), bf16),
            pltpu.VMEM((3 * shard_rows, LANES), f32),
            pltpu.VMEM((shard_rows, LANES), f32),
            pltpu.VMEM((shard_rows, LANES), f32),
            pltpu.VMEM((WIN, LANES), bf16),
            pltpu.VMEM((ss - 1, win_part, LANES), bf16),
            pltpu.VMEM((ys, win_part, LANES), bf16),
            pltpu.VMEM((zs, win_part, LANES), bf16),
            pltpu.VMEM((3 * win_part, LANES), f32),
            pltpu.VMEM((shard_rows // win_part, win_part, LANES), f32),
            pltpu.VMEM((WIN, LANES), bf16),
            dma((16,)), dma((4 + ss,)),
            dma((2,)), dma((2,)), dma((2,)), dma((2,)),
            dma((ss // 2,)), dma((ss // 2,)),
            dma((max(ss // 2 - 1, 1), 2)), dma((max(ss // 2 - 1, 1), 2)),
            dma((ys - 1,)), dma((ys - 1,)),
            dma((zs - 1,)), dma((zs - 1,)),
            dma((zs - 1,)), dma,
            dma((ss - 1,)), dma,
            dma((ys - 1,)), dma((ys - 1,)),
            dma((max(ss // 2 - 1, 1), 2)), dma((max(ss // 2 - 1, 1), 2)),
            dma((ss // 2,)), dma((ss // 2,)),
            dma((ss - 1,)), dma((ss - 1,)),
            dma((ys - 1,)), dma((ys - 1,)),
            dma((zs - 1,)), dma((zs - 1,)),
            dma((ss - 1,)), dma((ss - 1,)),
            dma((ys - 1,)), dma((zs - 1,)), dma,
            dma((ss - 1,)), dma((shard_rows // win_part,)),
        ],
        compiler_params=pltpu.CompilerParams(
            collective_id=0, has_side_effects=True, vmem_limit_bytes=60 << 20
        ),
    )(
        features[0],
        cotangent[0],
        conv_weight.transpose(2, 3, 4, 0, 1).reshape(27, ch, ch),
        conv_bias.reshape(1, ch),
        head_weight.T,
        grad_rest,
        master.reshape(shard_rows, LANES),
        moment.reshape(shard_rows, LANES),
        second.reshape(shard_rows, LANES),
        *tables,
    )
    igrad, new_moment, new_second, new_master, weights = pl.pallas_call(
        copy_kernel,
        out_shape=tuple(jax.ShapeDtypeStruct(out.shape, out.dtype) for out in outs),
        in_specs=[pl.BlockSpec(memory_space=pl.ANY)] * 5,
        out_specs=(pl.BlockSpec(memory_space=pl.ANY),) * 5,
        scratch_shapes=[pltpu.VMEM(out.shape, out.dtype) for out in outs] + [dma((8,)), dma((8,))],
        compiler_params=pltpu.CompilerParams(vmem_limit_bytes=60 << 20),
    )(*outs)
    return (
        igrad[None],
        new_moment.reshape(-1),
        new_second.reshape(-1),
        new_master.reshape(-1),
        weights.reshape(-1),
    )


def solution(mesh):
    return jax.shard_map(
        on_device,
        mesh=mesh,
        in_specs=(
            P("rep", None, "slab", None, None),
            P("rep", None, "slab", None, None),
            P(),
            P(),
            P(),
            P("rep", "slab", None),
            P("rep"),
            P("rep"),
            P("rep"),
        ),
        out_specs=(P("rep", None, "slab", None, None), P("rep"), P("rep"), P("rep"), P()),
        check_vma=False,
    )
```

```python
import functools

import jax
import jax.numpy as jnp
import numpy as np
from jax import lax
from jax.experimental import pallas as pl
from jax.experimental.pallas import tpu as pltpu
from jax.sharding import PartitionSpec as P

LOSS_SCALE = 2048

beta_one = 0.9
beta_two = 0.99
learn_rate = 0.01
adam_eps = 1e-08
step_count = 10.0

f32 = jnp.float32
bf16 = jnp.bfloat16
MESH = pl.DeviceIdType.MESH
LANES = 128
CONV_ROWS = 124
CONV_LANES = 104
WIN = 128


def adam_update(grad, moment, second, master):
    new_moment = beta_one * moment + (1.0 - beta_one) * grad
    new_second = beta_two * second + (1.0 - beta_two) * grad * grad
    update = (
        new_moment
        / (1.0 - beta_one**step_count)
        / (jnp.sqrt(new_second / (1.0 - beta_two**step_count)) + adam_eps)
    )
    return (new_moment, new_second, master - learn_rate * update)


def selection_tables(ch, emb):
    rows = 8 * ch
    repeat_rows = np.zeros((rows, ch), np.float32)
    repeat_rows[np.arange(rows), np.arange(rows) // 8] = 1
    repeat_lanes = np.zeros((ch, 256), np.float32)
    repeat_lanes[np.arange(rows) // 8, np.arange(rows)] = 1
    repeat_emb = np.zeros((emb, 128), np.float32)
    repeat_emb[np.arange(128) // 8, np.arange(128)] = 1
    add_rows = np.zeros((32, rows + 16), np.float32)
    for i in range(ch + 1):
        add_rows[i, 8 * i : 8 * i + 8] = 1
    order = np.zeros((5 * 256, 768), np.float32)
    for a in range(3):
        for c in range(3):
            pair, slot = divmod(a * 3 + c, 2)
            for i in range(ch):
                tile, local = divmod(i, 16)
                for b in range(3):
                    lane = (8 * local + 6 + b + 3 * slot) % 128
                    order[pair * 256 + tile * 128 + lane, i * 27 + a * 9 + b * 3 + c] = 1
    order[2 * 256 + 128 + 8 * 8 + 7, ch * 27] = 1
    emb_order = np.zeros((128, 128), np.float32)
    for e in range(emb):
        emb_order[8 * e + 7, 88 + e] = 1
    place = np.zeros((WIN, 256), np.float32)
    for o in range(ch):
        for k in range(7):
            place[5 * o + k, k * ch + o] = 1
        place[121, 7 * ch + o] = 1
    for i in range(ch + 1):
        place[121 + i // 8, 192 + i] = 1
        place[122 + i // 8, 224 + i] = 1
    tables = (repeat_rows, repeat_lanes, repeat_emb, add_rows, order, emb_order, place)
    return tuple(jnp.asarray(t, bf16) for t in tables)


def far_first(count):
    return sorted(range(1, count), key=lambda d: -min(d, count - d))


def dot(lhs, rhs):
    return jnp.dot(lhs, rhs, preferred_element_type=f32)


def dot_nt(lhs, rhs):
    return lax.dot_general(lhs, rhs, (((1,), (1,)), ((), ())), preferred_element_type=f32)


def dot_tn(lhs, rhs):
    return lax.dot_general(lhs, rhs, (((0,), (0,)), ((), ())), preferred_element_type=f32)


def iota(shape, dim):
    return lax.broadcasted_iota(jnp.int32, shape, dim)


def kernel(
    sizes,
    feat_in, cot_in, w_in, bias_in, headt_in, rest_in, master_in, moment_in, second_in,
    rep_rows_in, rep_lanes_in, rep_emb_in, add_in, order_in, emb_order_in, place_in,
    igrad_out, nmom_out, nsec_out, nmas_out, weights_out,
    feat_ref, cot_ref, w_ref, bias_ref, headt_ref, rest_1d, own_state,
    rep_rows_ref, rep_lanes_ref, rep_emb_ref, add_ref, order_ref, emb_order_ref, place_ref,
    igrad_v, shards_v, weights_v, ordered_v,
    shared_rows, flat_b, feat_v, cot_v, wband, hband, conv_v, act_v, dpre_v, grad_v, packed_v, stack_v,
    fh_send, fh_recv, dh_send, dh_recv,
    p1a_recv, pair_sum, p1b_recv, sum_v, p2_send, p2_recv, p3_all, col_state, grad_shard, own_grad,
    win_send, win_recv, wy_all, wz_all, win_state, win_grad, win_weights,
    local_sem, out_sem, fh_ssem, fh_rsem, dh_ssem, dh_rsem,
    p1a_ssem, p1a_rsem, p1b_ssem, p1b_rsem, p2_ssem, p2_rsem, p3_ssem, p3_rsem,
    col_ssem, col_rsem, share_ssem, share_rsem, b2_ssem, b2_rsem, b3x_ssem, b3x_rsem, b3c_ssem, b3c_rsem,
    w1_ssem, w1_rsem, wy_ssem, wy_rsem, wz_ssem, wz_rsem, wb_ssem, wb_rsem,
    ws_y_ssem, ws_z_ssem, ws_rsem, wshare_ssem, wshare_rsem,
):
    zs, ys, ss, shard_rows, planes, ch, emb = sizes
    rows = 8 * ch
    cells = planes * LANES
    block_rows = ys * shard_rows
    rep = lax.axis_index("rep")
    s = lax.axis_index("slab")
    z = rep // ys
    y = rep % ys

    def at(zz, yy, sl):
        return (zz * ys + yy, sl)

    def remote(src, dst, ssem, rsem, device):
        return pltpu.make_async_remote_copy(
            src_ref=src, dst_ref=dst, send_sem=ssem, recv_sem=rsem, device_id=device, device_id_type=MESH
        )

    barrier = pltpu.get_barrier_semaphore()
    for d in far_first(max(ys, zs, ss)):
        if d < zs:
            pl.semaphore_signal(barrier, inc=1, device_id=at((z + d) % zs, y, s), device_id_type=MESH)
        if d < ys:
            pl.semaphore_signal(barrier, inc=1, device_id=at(z, (y + d) % ys, s), device_id_type=MESH)
        if d < ss:
            pl.semaphore_signal(barrier, inc=1, device_id=at(z, y, (s + d) % ss), device_id_type=MESH)

    ins = (
        (feat_in, feat_ref), (w_in, w_ref), (rep_lanes_in, rep_lanes_ref), (rep_rows_in, rep_rows_ref),
        (rest_in.at[0], rest_1d), (headt_in, headt_ref), (rep_emb_in, rep_emb_ref), (bias_in, bias_ref),
        (cot_in, cot_ref), (order_in, order_ref), (add_in, add_ref), (emb_order_in, emb_order_ref),
        (place_in, place_ref),
        *[(ref, own_state.at[pl.ds(i * shard_rows, shard_rows)]) for i, ref in enumerate((moment_in, second_in, master_in))],
    )
    copies = [pltpu.make_async_copy(src, dst, local_sem.at[i]) for i, (src, dst) in enumerate(ins)]
    for copy in copies:
        copy.start()

    near = ys // 4
    near_count = 2 * near + 1
    far_count = ys - near_count
    far_rows = far_count * shard_rows

    def placed(row):
        block_at = lax.div(row, block_rows)
        in_block = lax.rem(row, block_rows)
        slot = lax.rem(lax.div(in_block, shard_rows) + (2 * ys - near - 1) - y, ys)
        return pl.multiple_of(block_at * block_rows + slot * shard_rows + lax.rem(in_block, shard_rows), 16)

    def store_rows(row, value):
        flat_b[pl.ds(placed(jnp.int32(row)), 16), :] = value

    copies[4].wait()
    first, last = CONV_ROWS // 16, flat_b.shape[0] // 16 - 1
    for j in range(first):
        store_rows(16 * j, jnp.zeros((16, LANES), bf16))
    lane16 = iota((16, LANES), 1)

    def moved(here, later):
        return pltpu.roll(jnp.where(lane16 >= LANES - CONV_LANES, here, later), CONV_LANES, 1).astype(bf16)

    def rest_rows(start, count):
        return rest_1d[0:1, pl.ds(start, count * LANES)].reshape(count, LANES)

    lane8 = iota((8, LANES), 1)

    def moved8(here, later):
        return pltpu.roll(jnp.where(lane8 >= LANES - CONV_LANES, here, later), CONV_LANES, 1)

    per_step = 8
    skipped = (16 * (first + 1) - CONV_ROWS - 1) * LANES

    def align_at(at_row):
        halves = []
        for h in range(2):
            start = (at_row + 8 * h) * LANES + skipped
            halves.append(moved8(rest_rows(start, 8), rest_rows(start + LANES, 8)))
        part = jnp.concatenate(halves, axis=0).astype(bf16)
        store_rows(at_row + 16 * (first + 1), part)

    def align(j, carry):
        for i in range(per_step):
            align_at(pl.multiple_of(j * (16 * per_step), 16 * per_step) + 16 * i)
        return carry

    steps = (last - first - 1) // per_step
    lax.fori_loop(0, steps, align, 0)
    for j in range(steps * per_step, last - first - 1):
        align_at(16 * j)
    lead = CONV_ROWS - 16 * first
    start_rows = rest_rows(0, 8)
    shared_rows[...] = moved(
        jnp.concatenate([jnp.zeros((lead + 1, LANES), f32), start_rows[0 : 15 - lead]], axis=0),
        jnp.concatenate([jnp.zeros((lead, LANES), f32), start_rows[0 : 16 - lead]], axis=0),
    )
    store_rows(16 * first, shared_rows[...])
    end_row = 16 * last - CONV_ROWS - 1
    end = rest_1d[0:1, (end_row + 16) * LANES :]
    end = jnp.concatenate([end, jnp.zeros((1, LANES - end.shape[1]), f32)], axis=1)
    end_rows = rest_rows(end_row * LANES, 16)
    store_rows(16 * last, moved(end_rows, jnp.concatenate([end_rows[1:16], end], axis=0)))

    pl.semaphore_wait(barrier, (ss - 1) + (ys - 1) + (zs - 1))

    xs = ss // 2
    x = s // 2
    core = s % 2

    def block(ref, xx, cc):
        return ref.at[pl.ds(pl.multiple_of((xx * 2 + cc) * block_rows, 16), block_rows)]

    def part_rows(part):
        return (far_rows, block_rows - far_rows) if part else (0, far_rows)

    def p1a(i, part):
        start, count = part_rows(part)
        at_row = (i * 2 + 1 - core) * block_rows + start
        return remote(
            flat_b.at[pl.ds(pl.multiple_of(at_row, 16), count)], p1a_recv.at[i, pl.ds(start, count)],
            p1a_ssem.at[i, part], p1a_rsem.at[i, part], at(z, y, x * 2 + 1 - core),
        )

    def p1b(d, part):
        to = (x + d) % xs
        some = pl.ds(far_rows, block_rows - far_rows) if part else pl.ds(0, far_rows)
        return remote(
            pair_sum.at[to, some], p1b_recv.at[d - 1, some],
            p1b_ssem.at[d - 1, part], p1b_rsem.at[d - 1, part], at(z, y, to * 2 + core),
        )

    order = [(x + d) % xs for d in far_first(xs) + [0]]
    for part in range(2):
        for i in order:
            p1a(i, part).start()

    copies[0].wait()
    for p in range(planes):
        plane = feat_ref[:, p].astype(f32).reshape(rows, LANES).astype(bf16)
        feat_v[0:rows, LANES * (p + 1) : LANES * (p + 2)] = plane
        if p == 0:
            fh_send[0] = plane
        if p == planes - 1:
            fh_send[1] = plane
    feat_v[rows : rows + 16, :] = jnp.ones((16, cells + 2 * LANES), bf16)
    feat_v[rows + 16 : 256, :] = jnp.zeros((256 - rows - 16, cells + 2 * LANES), bf16)

    def halo(send, recv, ssem, rsem, up):
        source, slot = (1, 0) if up else (0, 1)
        other = (s + 1) % ss if up else (s + ss - 1) % ss
        return remote(send.at[source], recv.at[slot], ssem.at[source], rsem.at[slot], at(z, y, other))

    def start_halo(send, recv, ssem, rsem):
        @pl.when(s < ss - 1)
        def _():
            halo(send, recv, ssem, rsem, True).start()

        @pl.when(s > 0)
        def _():
            halo(send, recv, ssem, rsem, False).start()

        @pl.when(s == 0)
        def _():
            recv[0] = jnp.zeros((rows, LANES), bf16)

        @pl.when(s == ss - 1)
        def _():
            recv[1] = jnp.zeros((rows, LANES), bf16)

    def wait_halo(send, recv, ssem, rsem):
        @pl.when(s < ss - 1)
        def _():
            halo(send, recv, ssem, rsem, True).wait_send()
            halo(send, recv, ssem, rsem, False).wait_recv()

        @pl.when(s > 0)
        def _():
            halo(send, recv, ssem, rsem, False).wait_send()
            halo(send, recv, ssem, rsem, True).wait_recv()

    start_halo(fh_send, fh_recv, fh_ssem, fh_rsem)

    for part in range(2):
        start, count = part_rows(part)
        for d in far_first(xs) + [0]:
            to = (x + d) % xs
            p1a(to, part).wait_recv()
            own_row = pl.multiple_of((to * 2 + core) * block_rows + start, 16)
            own = flat_b[pl.ds(own_row, count), :].astype(f32)
            total = own + p1a_recv[to, start : start + count].astype(f32)
            pair_sum[to, start : start + count] = total.astype(bf16)
            if d:
                p1b(d, part).start()

    for i in (13, 14, 15):
        copies[i].wait()
    reducer = z == s
    win_part = WIN // ss
    win_y = (s * win_part) // shard_rows
    win_row = (s * win_part) % shard_rows
    win_source = (z == 0) & (y == win_y)

    def col(d):
        return remote(own_state, col_state, col_ssem.at[d - 1], col_rsem, at((z + d) % zs, y, s))

    def ws_y(d):
        return remote(win_state, win_state, ws_y_ssem.at[d - 1], ws_rsem, at(z, (y + d) % ys, s))

    def ws_z(d):
        return remote(win_state, win_state, ws_z_ssem.at[d - 1], ws_rsem, at((z + d) % zs, y, s))

    @pl.when(reducer)
    def _():
        for d in far_first(zs):
            col(d).start()
        col_state[...] = own_state[...]

    @pl.when(win_source)
    def _():
        for i in range(3):
            win_state[i * win_part : (i + 1) * win_part, :] = own_state[
                pl.ds(pl.multiple_of(i * shard_rows + win_row, 16), win_part), :
            ]
        for d in far_first(ys):
            ws_y(d).start()
        for d in far_first(zs):
            ws_z(d).start()

    row = iota((rows, 256), 0)
    lane = iota((rows, 256), 1)
    shift = (lane % 8) - (7 - row % 8)
    for i in (1, 2, 3, 5, 6, 7, 8):
        copies[i].wait()
    for p in range(planes):
        cot_v[:, LANES * p : LANES * (p + 1)] = cot_ref[:, p].astype(f32).reshape(8 * emb, LANES).astype(bf16)
    spread = dot(w_ref[...].astype(f32).reshape(27 * ch, ch).astype(bf16), rep_lanes_ref[...])
    for a in range(3):
        for c in range(3):
            band = jnp.zeros((rows, 256), f32)
            for b in range(3):
                at_row = (a * 9 + b * 3 + c) * ch
                full = dot(rep_rows_ref[...], spread[at_row : at_row + ch].astype(bf16))
                band = jnp.where(shift == b - 1, full, band)
            wband[a, rows * c : rows * (c + 1), :] = band.astype(bf16)
    head = dot(dot_nt(rep_rows_ref[...], headt_ref[...]).astype(bf16), rep_emb_ref[...])
    hband[...] = jnp.where(shift[:, :LANES] == 0, head, 0.0).astype(bf16)
    bias_row = jnp.concatenate([bias_ref[...], jnp.zeros((1, LANES - ch), f32)], axis=1)
    row_l = iota((rows, LANES), 0)
    lane_l = iota((rows, LANES), 1)
    bias = jnp.sum(jnp.where(lane_l == row_l // 8, jnp.broadcast_to(bias_row, (rows, LANES)), 0.0), axis=1, keepdims=True)

    conv_v[...] = dot(wband[1], feat_v[:, LANES : LANES + cells])
    wait_halo(fh_send, fh_recv, fh_ssem, fh_rsem)
    feat_v[0:rows, 0:LANES] = fh_recv[0]
    feat_v[0:rows, LANES + cells : 2 * LANES + cells] = fh_recv[1]
    conv_v[...] += dot(wband[0], feat_v[:, 0:cells]) + dot(wband[2], feat_v[:, 2 * LANES : 2 * LANES + cells])

    def right(v):
        return jnp.where(lane_l == 0, 0.0, pltpu.roll(v, 1, 1))

    def left(v):
        return jnp.where(lane_l == LANES - 1, 0.0, pltpu.roll(v, LANES - 1, 1))

    def spread_dpre(dpre, p):
        at_lane = slice(LANES * p, LANES * (p + 1))
        dpre_v[0:rows, at_lane] = left(dpre).astype(bf16)
        dpre_v[rows : 2 * rows, at_lane] = dpre.astype(bf16)
        dpre_v[2 * rows : 3 * rows, at_lane] = right(dpre).astype(bf16)

    for p in (0, planes - 1) + tuple(range(1, planes - 1)):
        at_lane = slice(LANES * p, LANES * (p + 1))
        pre = (
            conv_v[rows : 2 * rows, at_lane]
            + right(conv_v[0:rows, at_lane])
            + left(conv_v[2 * rows : 3 * rows, at_lane])
            + bias
        )
        sigma = jax.nn.sigmoid(pre)
        act_v[0:rows, at_lane] = (pre * sigma).astype(bf16)
        dact = dot(hband[...], cot_v[:, at_lane])
        dpre = (dact * sigma * (1.0 + pre * (1.0 - sigma))).astype(bf16)
        if p == 0:
            dh_send[0] = dpre
        if p == planes - 1:
            dh_send[1] = dpre
        spread_dpre(dpre.astype(f32), p + 1)
        if p == planes - 1:
            start_halo(dh_send, dh_recv, dh_ssem, dh_rsem)
    act_v[rows : rows + 16, :] = jnp.ones((16, cells), bf16)

    def p2(d):
        slot = (d - near - 1) % ys
        return remote(
            p2_send.at[pl.ds(slot * shard_rows, shard_rows)], p2_recv.at[d - 1],
            p2_ssem.at[d - 1], p2_rsem.at[d - 1], at(z, (y + d) % ys, s),
        )

    def p3(d, back):
        part = p3_all.at[(z + zs - d) % zs if back else z]
        return remote(part, part, p3_ssem.at[d - 1], p3_rsem.at[d - 1], at((z + d) % zs, y, s))

    def share(d):
        return remote(grad_shard, grad_shard, share_ssem.at[d - 1], share_rsem, at(z, y, (s + d) % ss))

    def shards_of(xx, slot, count):
        at_row = (xx * 2 + core) * block_rows + slot * shard_rows
        return weights_v.at[pl.ds(pl.multiple_of(at_row, 16), count * shard_rows)]

    def b2(d):
        return remote(
            shards_of(x, near, 1), shards_of(x, (near - d) % ys, 1),
            b2_ssem.at[d - 1], b2_rsem.at[d - 1], at(z, (y + d) % ys, s),
        )

    def b3x(d, far, back):
        slot, count = (near_count, ys - near_count) if far else (0, near_count)
        part = shards_of((x + xs - d) % xs if back else x, slot, count)
        return remote(part, part, b3x_ssem.at[d - 1, far], b3x_rsem.at[d - 1, far], at(z, y, (x + d) % xs * 2 + core))

    def b3c(d, back):
        xx = (x + xs - d) % xs
        return remote(
            block(ordered_v, xx, core), block(weights_out, xx, 1 - core if back else core),
            b3c_ssem.at[d], b3c_rsem.at[d], at(z, y, x * 2 + 1 - core),
        )

    def w1(d):
        part = win_send.at[pl.ds(pl.multiple_of((s + d) % ss * win_part, 16), win_part)]
        return remote(part, win_recv.at[d - 1], w1_ssem.at[d - 1], w1_rsem.at[d - 1], at(z, y, (s + d) % ss))

    def wy(d, back):
        part = wy_all.at[(y + ys - d) % ys if back else y]
        return remote(part, part, wy_ssem.at[d - 1], wy_rsem.at[d - 1], at(z, (y + d) % ys, s))

    def wz(d, back):
        part = wz_all.at[(z + zs - d) % zs if back else z]
        return remote(part, part, wz_ssem.at[d - 1], wz_rsem.at[d - 1], at((z + d) % zs, y, s))

    def wb(d, back):
        owner = (s + ss - d) % ss if back else s
        part = win_weights.at[pl.ds(pl.multiple_of(owner * win_part, 16), win_part)]
        return remote(part, part, wb_ssem.at[d - 1], wb_rsem.at[d - 1], at(z, y, (s + d) % ss))

    per_shard = shard_rows // win_part

    def wshare(d):
        part = win_grad.at[s % per_shard]
        return remote(part, part, wshare_ssem.at[d - 1], wshare_rsem.at[s % per_shard], at(z, y, (s + d) % ss))

    def wshare_in(i):
        part = win_grad.at[i]
        return remote(part, part, wshare_ssem.at[0], wshare_rsem.at[i], at(z, y, (s + 1) % ss))

    def updated(grad, state):
        count = grad.shape[0]
        return adam_update(grad, state[0:count, :], state[count : 2 * count, :], state[2 * count : 3 * count, :])

    def start_ys():
        for part, some in enumerate((slice(0, far_rows), slice(far_rows, block_rows))):
            for d in range(1, xs):
                p1b(d, part).wait_recv()
            total = pair_sum[x, some].astype(f32)
            for d in range(1, xs):
                total = total + p1b_recv[d - 1, some].astype(f32)
            sum_v[some, :] = total
            p2_send[some, :] = total.astype(bf16)
            for d in far_first(ys):
                if (min(d, ys - d) <= near) == bool(part):
                    p2(d).start()

    def start_zs():
        for d in range(1, ys):
            p2(d).wait_recv()
        total = sum_v[(ys - 1 - near) * shard_rows : (ys - near) * shard_rows, :]
        for d in range(1, ys):
            total = total + p2_recv[d - 1].astype(f32)
        p3_all[z] = total.astype(bf16)
        for d in far_first(zs):
            p3(d, False).start()

    def start_gather_ys():
        @pl.when(jnp.logical_not(reducer))
        def _():
            col(1).wait_recv()

        for d in range(1, zs):
            p3(d, True).wait_recv()
        grad = p3_all[0].astype(f32)
        for i in range(1, zs):
            grad = grad + p3_all[i].astype(f32)
        grad = grad / LOSS_SCALE
        weights = updated(grad, col_state)[2].astype(bf16)
        weights_v[pl.ds(pl.multiple_of(s * block_rows + near * shard_rows, 16), shard_rows), :] = weights
        for d in far_first(ys):
            b2(d).start()

        @pl.when(reducer)
        def _():
            grad_shard[...] = grad
            for d in range(1, ss):
                share(d).start()

    def start_gather_slabs():
        for far in range(2):
            for d in range(1, ys):
                if (min(d, ys - d) > near) == bool(far):
                    b2(d).wait_recv()
            for d in far_first(xs):
                b3x(d, far, False).start()

    def start_window_ys():
        for d in range(1, ss):
            w1(d).wait_recv()
        total = win_send[pl.ds(pl.multiple_of(s * win_part, 16), win_part), :].astype(f32)
        for d in range(1, ss):
            total = total + win_recv[d - 1].astype(f32)
        wy_all[y] = total.astype(bf16)
        for d in far_first(ys):
            wy(d, False).start()

    def start_window_zs():
        for d in range(1, ys):
            wy(d, True).wait_recv()
        total = wy_all[0].astype(f32)
        for i in range(1, ys):
            total = total + wy_all[i].astype(f32)
        wz_all[z] = total.astype(bf16)
        for d in far_first(zs):
            wz(d, False).start()

    in_window = (z == 0) & (y < WIN // shard_rows)
    win_owner = (z == 0) & (y == win_y)

    def start_window_gather():
        for d in range(1, zs):
            wz(d, True).wait_recv()
        grad = wz_all[0].astype(f32)
        for i in range(1, zs):
            grad = grad + wz_all[i].astype(f32)
        grad = grad / LOSS_SCALE
        weights = updated(grad, win_state)[2].astype(bf16)
        win_weights[pl.ds(pl.multiple_of(s * win_part, 16), win_part), :] = weights
        for d in range(1, ss):
            wb(d, False).start()

        @pl.when(win_owner)
        def _():
            win_grad[s % per_shard] = grad
            for d in range(1, ss):
                wshare(d).start()

    def finish_window():
        for d in range(1, ss):
            wb(d, True).wait_recv()

    def own_update():
        @pl.when(jnp.logical_not(reducer))
        def _():
            share(1).wait_recv()

        own_grad[...] = grad_shard[...]

        @pl.when(in_window)
        def _():
            for i in range(per_shard):
                @pl.when(s != y * per_shard + i)
                def _():
                    wshare_in(i).wait_recv()

                own_grad[i * win_part : (i + 1) * win_part, :] = win_grad[i]

        for i, value in enumerate(updated(own_grad[...], own_state)):
            shards_v[i] = value

    outs = [pltpu.make_async_copy(igrad_v, igrad_out, out_sem.at[0])]
    outs += [
        pltpu.make_async_copy(shards_v.at[i], ref, out_sem.at[1 + i]) for i, ref in enumerate((nmom_out, nsec_out, nmas_out))
    ]

    mask = ((lane < rows) & (shift >= -1) & (shift <= 1)) | ((lane >= rows) & (lane < rows + 8) & (shift == 0))
    mask = [mask[:, :LANES], mask[:, LANES:]]
    for a in range(3):
        grad_v[a] = dot_nt(dpre_v[:, LANES : LANES + cells], feat_v[:, LANES * a : LANES * a + cells])
    for i in range(9, 13):
        copies[i].wait()

    def rolled(v, by):
        return jnp.concatenate(
            [pltpu.roll(v[8 * o : 8 * o + 8], by, 1, stride=1, stride_axis=0) for o in range(v.shape[0] // 8)], axis=0
        )

    for pair in range(5):
        for t in range(2):
            total = None
            for slot in range(2):
                if pair * 2 + slot < 9:
                    a, c = divmod(pair * 2 + slot, 3)
                    part = grad_v[a, rows * c : rows * (c + 1), LANES * t : LANES * (t + 1)]
                    part = rolled(jnp.where(mask[t], part, 0.0), 3 * slot)
                    total = part if total is None else total + part
            at_lane = pair * 256 + t * LANES
            packed_v[:, at_lane : at_lane + LANES] = total.astype(bf16)
    sums = dot(add_ref[0:ch, 0:rows], packed_v[...])
    ordered = dot(sums.astype(bf16), order_ref[...])
    lane8 = iota((8, LANES), 1)
    row8 = iota((8, LANES), 0)
    zero8 = jnp.zeros((8, LANES), f32)
    for t in range(ch // 8):
        whole, base = divmod(64 * t, LANES)
        by = base + 8 * row8
        tiles = []
        for k in range(6):
            piece = ordered[8 * t : 8 * t + 8, LANES * k : LANES * (k + 1)]
            if k == 5:
                piece = jnp.where(lane8 < 8, piece, 0.0)
            tiles.append(pltpu.roll(piece, base, 1, stride=8, stride_axis=0))
        for m in range(7):
            k = m - whole
            high = tiles[k] if 0 <= k < 6 else zero8
            low = tiles[k - 1] if 0 <= k - 1 < 6 else zero8
            stack_v[m * ch + 8 * t : m * ch + 8 * t + 8, :] = jnp.where(lane8 >= by, high, low)
        bgrad = jnp.broadcast_to(ordered[8 * t : 8 * t + 8, 27 * ch : 27 * ch + 1], (8, LANES))
        stack_v[7 * ch + 8 * t : 7 * ch + 8 * t + 8, :] = jnp.where(lane8 == 64 + 8 * t + row8, bgrad, 0.0)

    hgrad = dot_nt(act_v[...], cot_v[...])
    row_h = iota((rows + 16, LANES), 0)
    lane_h = iota((rows + 16, LANES), 1)
    hgrad = rolled(jnp.where(lane_h % 8 == 7 - row_h % 8, hgrad, 0.0), 0).astype(bf16)
    hgrad = dot(dot(add_ref[...], hgrad).astype(bf16), emb_order_ref[...])
    for t in range(4):
        piece = pltpu.roll(hgrad[8 * t : 8 * t + 8], 0, 1, stride=16, stride_axis=0)
        stack_v[192 + 8 * t : 200 + 8 * t, :] = jnp.where(lane8 >= 88, piece, 0.0)
        stack_v[224 + 8 * t : 232 + 8 * t, :] = jnp.where(lane8 < 88, piece, 0.0)
    window = dot(place_ref[...], stack_v[...].astype(bf16))
    win_send[0 : 16 * first, :] = window[0 : 16 * first].astype(bf16)
    win_send[16 * first : WIN, :] = (window[16 * first : WIN] + shared_rows[...].astype(f32)).astype(bf16)
    for d in range(1, ss):
        w1(d).start()

    start_ys()
    @pl.when((z == 0) & (y != win_y))
    def _():
        ws_y(1).wait_recv()
        for d in far_first(zs):
            ws_z(d).start()

    wait_halo(dh_send, dh_recv, dh_ssem, dh_rsem)
    spread_dpre(dh_recv[0].astype(f32), 0)
    spread_dpre(dh_recv[1].astype(f32), planes + 1)

    total = None
    for a in range(3):
        part = dot_tn(wband[a, :, 0:rows], dpre_v[:, LANES * (2 - a) : LANES * (2 - a) + cells])
        total = part if total is None else total + part
    for p in range(planes):
        igrad_v[:, p] = total[:, LANES * p : LANES * (p + 1)].reshape(ch, 8, LANES).astype(bf16)
    outs[0].start()

    start_window_ys()
    start_zs()

    start_window_zs()
    start_gather_ys()
    @pl.when(z != 0)
    def _():
        ws_z(1).wait_recv()

    start_window_gather()
    start_gather_slabs()
    def out_block(d):
        xx = (x + xs - d) % xs
        return pltpu.make_async_copy(block(ordered_v, xx, core), block(weights_out, xx, core), out_sem.at[4 + d])

    def finish_block(d):
        base = ((x + xs - d) % xs * 2 + core) * block_rows
        for slot in range(ys):
            owner = (y + ys + slot - near) % ys
            ordered_v[pl.ds(pl.multiple_of(base + owner * shard_rows, 16), shard_rows), :] = weights_v[
                pl.ds(pl.multiple_of(base + slot * shard_rows, 16), shard_rows), :
            ]

        @pl.when((x != d) | (core != 0))
        def _():
            b3c(d, False).start()
            out_block(d).start()

    nearest = sorted(range(1, xs), key=lambda d: min(d, xs - d))
    finish_block(0)
    for d in nearest:
        for far in range(2):
            b3x(d, far, True).wait_recv()
        finish_block(d)
    finish_window()

    @pl.when(core == 0)
    def _():
        ordered_v[0:WIN, :] = win_weights[...]
        for d in range(xs):
            @pl.when(x == d)
            def _():
                b3c(d, False).start()
                out_block(d).start()

    own_update()
    for out in outs[1:4]:
        out.start()
    for d in range(xs):
        b3c(d, True).wait_recv()

    for d in range(1, ss):
        w1(d).wait_send()
        wb(d, False).wait_send()
    for i in range(xs):
        p1a(i, 0).wait_send()
        p1a(i, 1).wait_send()
    for d in range(1, xs):
        p1b(d, 0).wait_send()
        p1b(d, 1).wait_send()
    for d in range(1, ys):
        p2(d).wait_send()
        wy(d, False).wait_send()
    for d in range(1, zs):
        p3(d, False).wait_send()
        wz(d, False).wait_send()

    @pl.when(reducer)
    def _():
        for d in range(1, zs):
            col(d).wait_send()
        for d in range(1, ss):
            share(d).wait_send()

    @pl.when(win_source)
    def _():
        for d in range(1, ys):
            ws_y(d).wait_send()

    @pl.when(z == 0)
    def _():
        for d in range(1, zs):
            ws_z(d).wait_send()

    @pl.when(win_owner)
    def _():
        for d in range(1, ss):
            wshare(d).wait_send()

    for d in range(xs):
        b3c(d, False).wait_send()
        out_block(d).wait()
    for d in range(1, xs):
        for far in range(2):
            b3x(d, far, False).wait_send()
    for d in range(1, ys):
        b2(d).wait_send()
    for out in outs:
        out.wait()


def copy_kernel(*refs):
    count = (len(refs) - 2) // 3
    in_sem, out_sem = refs[3 * count :]
    ins, outs, held = refs[:count], refs[count : 2 * count], refs[2 * count : 3 * count]
    part = ins[-1].shape[0] // 4
    pieces = [(i, slice(None)) for i in range(count - 1)] + [(count - 1, pl.ds(part * j, part)) for j in range(4)]
    loads = [pltpu.make_async_copy(ins[i].at[p], held[i].at[p], in_sem.at[k]) for k, (i, p) in enumerate(pieces)]
    stores = [pltpu.make_async_copy(held[i].at[p], outs[i].at[p], out_sem.at[k]) for k, (i, p) in enumerate(pieces)]
    for load in loads:
        load.start()
    for load, store in zip(loads, stores):
        load.wait()
        store.start()
    for store in stores:
        store.wait()


def on_device(
    features, cotangent, conv_weight, conv_bias, head_weight, grad_rest, master, moment, second
):
    ss = lax.axis_size("slab")
    zs = ss
    ys = lax.axis_size("rep") // zs
    ch, planes = features.shape[1], features.shape[2]
    emb = cotangent.shape[1]
    rows = 8 * ch
    cells = planes * LANES
    shard_rows = master.shape[0] // LANES
    block_rows = ys * shard_rows
    all_rows = ss * block_rows
    win_part = WIN // ss
    rest = grad_rest.shape[2]
    sizes = (zs, ys, ss, shard_rows, planes, ch, emb)
    tables = selection_tables(ch, emb)
    hbm = pl.BlockSpec(memory_space=pltpu.HBM)
    dma = pltpu.SemaphoreType.DMA
    shard = jax.ShapeDtypeStruct((shard_rows, LANES), f32)
    outs = pl.pallas_call(
        functools.partial(kernel, sizes),
        out_shape=(
            jax.ShapeDtypeStruct(features.shape[1:], bf16),
            shard,
            shard,
            shard,
            jax.ShapeDtypeStruct((all_rows, LANES), bf16),
        ),
        in_specs=[hbm] * 16,
        out_specs=(hbm,) * 5,
        scratch_shapes=[
            pltpu.VMEM(features.shape[1:], bf16),
            pltpu.VMEM(cotangent.shape[1:], bf16),
            pltpu.VMEM((27, ch, ch), bf16),
            pltpu.VMEM((1, ch), f32),
            pltpu.VMEM((emb, ch), bf16),
            pltpu.VMEM((1, rest), f32),
            pltpu.VMEM((3 * shard_rows, LANES), f32),
            *[pltpu.VMEM(t.shape, bf16) for t in tables],
            pltpu.VMEM(features.shape[1:], bf16),
            pltpu.VMEM((3, shard_rows, LANES), f32),
            pltpu.VMEM((all_rows, LANES), bf16),
            pltpu.VMEM((all_rows, LANES), bf16),
            pltpu.VMEM((16, LANES), bf16),
            pltpu.VMEM((all_rows, LANES), bf16),
            pltpu.VMEM((256, cells + 2 * LANES), bf16),
            pltpu.VMEM((8 * emb, cells), bf16),
            pltpu.VMEM((3, 3 * rows, 256), bf16),
            pltpu.VMEM((rows, LANES), bf16),
            pltpu.VMEM((3 * rows, cells), f32),
            pltpu.VMEM((rows + 16, cells), bf16),
            pltpu.VMEM((3 * rows, cells + 2 * LANES), bf16),
            pltpu.VMEM((3, 3 * rows, 256), f32),
            pltpu.VMEM((rows, 5 * 256), bf16),
            pltpu.VMEM((256, LANES), f32),
            pltpu.VMEM((2, rows, LANES), bf16),
            pltpu.VMEM((2, rows, LANES), bf16),
            pltpu.VMEM((2, rows, LANES), bf16),
            pltpu.VMEM((2, rows, LANES), bf16),
            pltpu.VMEM((ss // 2, block_rows, LANES), bf16),
            pltpu.VMEM((ss // 2, block_rows, LANES), bf16),
            pltpu.VMEM((max(ss // 2 - 1, 1), block_rows, LANES), bf16),
            pltpu.VMEM((block_rows, LANES), f32),
            pltpu.VMEM((block_rows, LANES), bf16),
            pltpu.VMEM((ys - 1, shard_rows, LANES), bf16),
            pltpu.VMEM((zs, shard_rows, LANES), bf16),
            pltpu.VMEM((3 * shard_rows, LANES), f32),
            pltpu.VMEM((shard_rows, LANES), f32),
            pltpu.VMEM((shard_rows, LANES), f32),
            pltpu.VMEM((WIN, LANES), bf16),
            pltpu.VMEM((ss - 1, win_part, LANES), bf16),
            pltpu.VMEM((ys, win_part, LANES), bf16),
            pltpu.VMEM((zs, win_part, LANES), bf16),
            pltpu.VMEM((3 * win_part, LANES), f32),
            pltpu.VMEM((shard_rows // win_part, win_part, LANES), f32),
            pltpu.VMEM((WIN, LANES), bf16),
            dma((16,)), dma((4 + ss,)),
            dma((2,)), dma((2,)), dma((2,)), dma((2,)),
            dma((ss // 2, 2)), dma((ss // 2, 2)),
            dma((max(ss // 2 - 1, 1), 2)), dma((max(ss // 2 - 1, 1), 2)),
            dma((ys - 1,)), dma((ys - 1,)),
            dma((zs - 1,)), dma((zs - 1,)),
            dma((zs - 1,)), dma,
            dma((ss - 1,)), dma,
            dma((ys - 1,)), dma((ys - 1,)),
            dma((max(ss // 2 - 1, 1), 2)), dma((max(ss // 2 - 1, 1), 2)),
            dma((ss // 2,)), dma((ss // 2,)),
            dma((ss - 1,)), dma((ss - 1,)),
            dma((ys - 1,)), dma((ys - 1,)),
            dma((zs - 1,)), dma((zs - 1,)),
            dma((ss - 1,)), dma((ss - 1,)),
            dma((ys - 1,)), dma((zs - 1,)), dma,
            dma((ss - 1,)), dma((shard_rows // win_part,)),
        ],
        compiler_params=pltpu.CompilerParams(
            collective_id=0, has_side_effects=True, vmem_limit_bytes=60 << 20
        ),
    )(
        features[0],
        cotangent[0],
        conv_weight.transpose(2, 3, 4, 0, 1).reshape(27, ch, ch),
        conv_bias.reshape(1, ch),
        head_weight.T,
        grad_rest,
        master.reshape(shard_rows, LANES),
        moment.reshape(shard_rows, LANES),
        second.reshape(shard_rows, LANES),
        *tables,
    )
    igrad, new_moment, new_second, new_master, weights = pl.pallas_call(
        copy_kernel,
        out_shape=tuple(jax.ShapeDtypeStruct(out.shape, out.dtype) for out in outs),
        in_specs=[pl.BlockSpec(memory_space=pl.ANY)] * 5,
        out_specs=(pl.BlockSpec(memory_space=pl.ANY),) * 5,
        scratch_shapes=[pltpu.VMEM(out.shape, out.dtype) for out in outs] + [dma((8,)), dma((8,))],
        compiler_params=pltpu.CompilerParams(vmem_limit_bytes=60 << 20),
    )(*outs)
    return (
        igrad[None],
        new_moment.reshape(-1),
        new_second.reshape(-1),
        new_master.reshape(-1),
        weights.reshape(-1),
    )


def solution(mesh):
    return jax.shard_map(
        on_device,
        mesh=mesh,
        in_specs=(
            P("rep", None, "slab", None, None),
            P("rep", None, "slab", None, None),
            P(),
            P(),
            P(),
            P("rep", "slab", None),
            P("rep"),
            P("rep"),
            P("rep"),
        ),
        out_specs=(P("rep", None, "slab", None, None), P("rep"), P("rep"), P("rep"), P()),
        check_vma=False,
    )
```
